512 devices in a mesh: gx: 16 (over z, core), gy: 8 (over y), gz: 4 (over x).
Axes of the slice: x: 4, y: 8, z: 8, core: 2. Of those that a mesh axis runs over, the one named last changes fastest.
Arguments:
- populations: float32 [19, 32, 256, 512], P(None, 'gx', 'gy', 'gz')
- orientation: float32 [6, 32, 256, 512], P(None, 'gx', 'gy', 'gz')
- slot_table: int32 [32, 256, 4], P('gx', 'gy', 'gz'), may hold values from -1 to 15, as said below
- w_in: bfloat16 [6, 512], replicated, may hold values from -12 to 12
- b_in: float32 [512], replicated, may hold values from -3 to 3
- w_mid: bfloat16 [512, 512], replicated, may hold values from -0.25 to 0.25
- b_mid: float32 [512], replicated, may hold values from -3 to 3
- w_out: bfloat16 [512, 15], replicated, may hold values from -0.25 to 0.25
- b_out: float32 [15], replicated, may hold values from -2 to 2
Outputs:
- flow_moments: bfloat16 [4, 32, 256, 512], P(None, 'gx', 'gy', 'gz')
- closure: bfloat16 [15, 32, 256, 512], P(None, 'gx', 'gy', 'gz')
The draws below stay inside these ranges and needn't reach their ends.
Inputs may be any that keep to these rules, and one draw needn't show every extreme that they name: `slot_table`: on one device the non-negative values are distinct: d + j marks the j-th block that the device sends to index d of gx for evaluation. A device with n occupied blocks sends n / 16 of them to every index of gx, using j from 0 upward; n is at most 16, which some device of every group along gx holds, and every device receives exactly 16 blocks in all.
All inputs are finite; a program needn't handle non-finite values.
Results may differ from the reference program's by a relative error of at most 0.0059.
Values may be sent and summed in bfloat16 or wider, within the bound.
No kernel may reach another device: no remote copies, remote signals or barrier semaphores. Data moves between devices by JAX's collectives and lax.ppermute only.
A program may use at most 128 MiB of HBM per device.

```python
import math
import jax
import jax.numpy as jnp
from jax import lax

CX = 2
CY = 32
CZ = 128
ITERS = 2
COMPONENTS = 6
CLOSURE_TERMS = 15
HIDDEN_UNITS = 512
NX = 32
NY = 256
NZ = 512
NZB = 4
SLOTS = 1
CAP = 16
N_GX = 16
N_GY = 8
N_GZ = 4


DRAW_VELOCITIES = [(0, 0, 0), (1, 0, 0), (-1, 0, 0), (0, 1, 0), (0, -1, 0), (0, 0, 1), (0, 0, -1), (1, 1, 0), (-1, -1, 0), (1, -1, 0), (-1, 1, 0), (1, 0, 1), (-1, 0, -1), (1, 0, -1), (-1, 0, 1), (0, 1, 1), (0, -1, -1), (0, 1, -1), (0, -1, 1)]


DRAW_WEIGHTS = [1.0 / 3.0] + [1.0 / 18.0] * 6 + [1.0 / 36.0] * 12


def draw_populations(key, part):
    key = jax.random.fold_in(key, 11)
    key_density, key_drift, key_scaling = jax.random.split(key, 3)
    cell_shape = (NX, NY, NZ)
    grid_shape = (19, NX, NY, NZ)
    height = (jnp.arange(NZ, dtype=jnp.float32) + 0.5) / NZ
    peak_speed = 0.1
    density = jnp.exp(jax.random.uniform(key_density, cell_shape, jnp.float32, math.log(0.4), math.log(2.5)))
    drift = jax.random.uniform(key_drift, (3,) + cell_shape, jnp.float32, -0.12, 0.12)
    scaling = jax.random.uniform(key_scaling, grid_shape, jnp.float32, 0.5, 1.5)
    shear_flow = peak_speed * 4.0 * height * (1.0 - height)
    speed_x = drift[0] + shear_flow[None, None, :]
    speed_y = drift[1]
    speed_z = drift[2]
    speed_square = speed_x * speed_x + speed_y * speed_y + speed_z * speed_z
    layers = []
    for number in range(19):
        step_x, step_y, step_z = DRAW_VELOCITIES[number]
        projection = step_x * speed_x + step_y * speed_y + step_z * speed_z
        balance = DRAW_WEIGHTS[number] * density * (1.0 + 3.0 * projection + 4.5 * projection * projection - 1.5 * speed_square)
        layers.append(balance)
    return jnp.stack(layers) * scaling


def draw_orientation(key, part):
    key = jax.random.fold_in(key, 13)
    key_direction, key_mixing = jax.random.split(key)
    grid_shape = (3, NX, NY, NZ)
    cell_shape = (NX, NY, NZ)
    direction = jax.random.normal(key_direction, grid_shape, jnp.float32)
    mixing = jax.random.uniform(key_mixing, cell_shape, jnp.float32, 0.1, 0.3)
    length_square = direction[0] * direction[0] + direction[1] * direction[1] + direction[2] * direction[2] + 0.01
    factor = (1.0 - mixing) / length_square
    isotropic = mixing / 3.0
    entry_11 = factor * direction[0] * direction[0] + isotropic
    entry_22 = factor * direction[1] * direction[1] + isotropic
    entry_33 = factor * direction[2] * direction[2] + isotropic
    entry_12 = factor * direction[0] * direction[1]
    entry_13 = factor * direction[0] * direction[2]
    entry_23 = factor * direction[1] * direction[2]
    return jnp.stack([entry_11, entry_22, entry_33, entry_12, entry_13, entry_23])


def draw_slot_table(key, part):
    key = jax.random.fold_in(key, 17)
    owner_count = NX // CX
    span_count = NY // CY
    group_count = span_count * NZB
    block_total = CX * CY
    key_pairs, key_loads, key_offsets, key_blocks = jax.random.split(key, 4)
    group_keys = jax.random.split(key_pairs, group_count)
    pairings = jax.vmap(lambda one_key: jax.random.permutation(one_key, owner_count))(group_keys)
    low_loads = jax.random.randint(key_loads, (group_count, owner_count // 2), 1, SLOTS + 1)
    low_loads = low_loads.at[:, 0].set(SLOTS)
    loads_by_position = jnp.concatenate([low_loads, SLOTS + 1 - low_loads], axis=1)
    inverse = jnp.argsort(pairings, axis=1)
    loads = jnp.take_along_axis(loads_by_position, inverse, axis=1)
    offsets = jax.random.randint(key_offsets, (group_count, owner_count), 0, owner_count)
    block_keys = jax.random.split(key_blocks, group_count * owner_count)
    orders = jax.vmap(lambda one_key: jax.random.permutation(one_key, block_total))(block_keys)
    ranks = jnp.argsort(orders, axis=1)
    counts = (loads * owner_count).reshape(-1)
    shifts = offsets.reshape(-1)
    destination = (shifts[:, None] + ranks) % owner_count
    slot_place = ranks // owner_count
    values = jnp.where(ranks < counts[:, None], destination * SLOTS + slot_place, -1).astype(jnp.int32)
    values = values.reshape(span_count, NZB, owner_count, CX, CY)
    values = jnp.transpose(values, (2, 3, 0, 4, 1))
    return values.reshape(NX, NY, NZB)


def scatter_about(own_key, shape, scale, limit, kind=jnp.bfloat16):
    return jnp.clip(scale * jax.random.normal(own_key, shape, jnp.float32), -limit, limit).astype(kind)


def setup_inputs(seed: int = 0) -> dict:
    seeds = jax.random.split(jax.random.key(seed), 10)
    populations = draw_populations(jax.random.fold_in(seeds[9], 71), 0)
    orientation = draw_orientation(jax.random.fold_in(seeds[9], 71), 0)
    slot_table = draw_slot_table(jax.random.fold_in(seeds[9], 71), 0)
    w_in = scatter_about(seeds[3], (COMPONENTS, HIDDEN_UNITS), 2.0, 12.0)
    b_in = scatter_about(seeds[4], (HIDDEN_UNITS,), 0.5, 3.0, jnp.float32)
    w_mid = scatter_about(seeds[5], (HIDDEN_UNITS, HIDDEN_UNITS), HIDDEN_UNITS ** -0.5, 0.25)
    b_mid = scatter_about(seeds[6], (HIDDEN_UNITS,), 0.5, 3.0, jnp.float32)
    w_out = scatter_about(seeds[7], (HIDDEN_UNITS, CLOSURE_TERMS), HIDDEN_UNITS ** -0.5, 0.25)
    b_out = scatter_about(seeds[8], (CLOSURE_TERMS,), 0.3, 2.0, jnp.float32)
    return {"populations": populations, "orientation": orientation, "slot_table": slot_table, "w_in": w_in, "b_in": b_in, "w_mid": w_mid, "b_mid": b_mid, "w_out": w_out, "b_out": b_out}


VELOCITIES = [(0, 0, 0), (1, 0, 0), (-1, 0, 0), (0, 1, 0), (0, -1, 0), (0, 0, 1), (0, 0, -1), (1, 1, 0), (-1, -1, 0), (1, -1, 0), (-1, 1, 0), (1, 0, 1), (-1, 0, -1), (1, 0, -1), (-1, 0, 1), (0, 1, 1), (0, -1, -1), (0, 1, -1), (0, -1, 1)]
LATTICE_WEIGHTS = [1.0 / 3.0] + [1.0 / 18.0] * 6 + [1.0 / 36.0] * 12
RELAX_TIME = 0.8
SHAPE_FACTOR = 0.95
ORIENT_STEP = 4.0
TENSOR_PAIRS = [(0, 0), (1, 1), (2, 2), (0, 1), (0, 2), (1, 2)]
REFERENCE_GROUP = 32


def opposite_of(number):
    if number == 0:
        return 0
    return number + 1 if number % 2 == 1 else number - 1


def fluid_moments(populations):
    density = populations[0]
    for number in range(1, 19):
        density = density + populations[number]
    velocity = []
    for axis_number in range(3):
        momentum = None
        for number in range(19):
            component = VELOCITIES[number][axis_number]
            if component != 0:
                summand = populations[number] if component > 0 else -populations[number]
                momentum = summand if momentum is None else momentum + summand
        velocity.append(momentum / density)
    return density, velocity


def collide(populations, density, velocity):
    speed_square = velocity[0] * velocity[0] + velocity[1] * velocity[1] + velocity[2] * velocity[2]
    relaxed = []
    for number in range(19):
        projection = jnp.zeros_like(density)
        for axis_number in range(3):
            component = VELOCITIES[number][axis_number]
            if component != 0:
                projection = projection + component * velocity[axis_number]
        equilibrium = LATTICE_WEIGHTS[number] * density * (1.0 + 3.0 * projection + 4.5 * projection * projection - 1.5 * speed_square)
        relaxed.append(populations[number] - (populations[number] - equilibrium) / RELAX_TIME)
    return jnp.stack(relaxed)


def full_tensor(entries):
    return [[entries[0], entries[3], entries[4]], [entries[3], entries[1], entries[5]], [entries[4], entries[5], entries[2]]]


def jeffery_rate(entries, gradient):
    tensor = full_tensor(entries)
    strain = [[0.5 * (gradient[row_index][col_index] + gradient[col_index][row_index]) for col_index in range(3)] for row_index in range(3)]
    rotation = [[0.5 * (gradient[row_index][col_index] - gradient[col_index][row_index]) for col_index in range(3)] for row_index in range(3)]
    contraction = None
    for row_index in range(3):
        for col_index in range(3):
            product = tensor[row_index][col_index] * strain[row_index][col_index]
            contraction = product if contraction is None else contraction + product
    rate_list = []
    for row_index, col_index in TENSOR_PAIRS:
        turned = None
        stretched = None
        for inner_index in range(3):
            spin_term = tensor[row_index][inner_index] * rotation[inner_index][col_index] - rotation[row_index][inner_index] * tensor[inner_index][col_index]
            strain_term = strain[row_index][inner_index] * tensor[inner_index][col_index] + tensor[row_index][inner_index] * strain[inner_index][col_index]
            turned = spin_term if turned is None else turned + spin_term
            stretched = strain_term if stretched is None else stretched + strain_term
        rate_list.append(turned + SHAPE_FACTOR * (stretched - 2.0 * contraction * tensor[row_index][col_index]))
    return rate_list


def plus_minus(grid_field, axis_number, outside_low, outside_high):
    if axis_number < 2:
        return jnp.roll(grid_field, -1, axis_number + 1), jnp.roll(grid_field, 1, axis_number + 1)
    forward = jnp.concatenate([grid_field[..., 1:], outside_high], axis=-1)
    backward = jnp.concatenate([outside_low, grid_field[..., :-1]], axis=-1)
    return forward, backward


def network_group(one_group, w_in, b_in, w_mid, b_mid, w_out, b_out):
    group_size = one_group.shape[0]
    depth_cells = one_group.shape[2]
    rows_flat = jnp.transpose(one_group, (0, 2, 1)).reshape(group_size * depth_cells, one_group.shape[1])
    first_layer = jnp.dot(rows_flat, w_in, preferred_element_type=jnp.float32) + b_in
    hidden_one = jax.nn.silu(first_layer).astype(jnp.bfloat16)
    second_layer = jnp.dot(hidden_one, w_mid, preferred_element_type=jnp.float32) + b_mid
    hidden_two = jax.nn.silu(second_layer).astype(jnp.bfloat16)
    third_layer = jnp.dot(hidden_two, w_out, preferred_element_type=jnp.float32) + b_out
    return jnp.transpose(third_layer.reshape(group_size, depth_cells, w_out.shape[1]), (0, 2, 1)).astype(jnp.bfloat16)


def reference(populations, orientation, slot_table, w_in, b_in, w_mid, b_mid, w_out, b_out):
    for step_number in range(ITERS):
        density, velocity = fluid_moments(populations)
        relaxed = collide(populations, density, velocity)
        read = []
        for number in range(19):
            shift_x, shift_y, shift_z = VELOCITIES[number]
            pulled = jnp.roll(relaxed[number], (shift_x, shift_y, shift_z), axis=(0, 1, 2))
            if shift_z == 1:
                pulled = pulled.at[:, :, 0].set(relaxed[opposite_of(number)][:, :, 0])
            if shift_z == -1:
                pulled = pulled.at[:, :, -1].set(relaxed[opposite_of(number)][:, :, -1])
            read.append(pulled)
        velocity_field = jnp.stack(velocity)
        empty_plane = jnp.zeros_like(velocity_field[..., :1])
        gradient = [[None, None, None] for row_index in range(3)]
        tensor_diffs = []
        for axis_number in range(3):
            ahead, behind = plus_minus(velocity_field, axis_number, empty_plane, empty_plane)
            for row_index in range(3):
                gradient[row_index][axis_number] = 0.5 * (ahead[row_index] - behind[row_index])
            tensor_ahead, tensor_behind = plus_minus(orientation, axis_number, orientation[..., :1], orientation[..., -1:])
            tensor_diffs.append(0.5 * (tensor_ahead - tensor_behind))
        advection = velocity[0] * tensor_diffs[0] + velocity[1] * tensor_diffs[1] + velocity[2] * tensor_diffs[2]
        rate_list = jeffery_rate([orientation[number] for number in range(6)], gradient)
        orientation = orientation + ORIENT_STEP * (jnp.stack(rate_list) - advection)
        populations = jnp.stack(read)
    density, velocity = fluid_moments(populations)
    flow_moments = jnp.stack([density] + velocity).astype(jnp.bfloat16)
    features = orientation.astype(jnp.bfloat16)
    block_count = CAP * N_GX * N_GY * N_GZ
    place_x, place_y, place_z = jnp.nonzero(slot_table >= 0, size=block_count)
    feature_blocks = features.reshape(COMPONENTS, NX, NY, NZB, CZ)
    picked = jnp.transpose(feature_blocks[:, place_x, place_y, place_z, :], (1, 0, 2))
    padded_count = -(-block_count // REFERENCE_GROUP) * REFERENCE_GROUP
    picked = jnp.concatenate([picked, jnp.zeros((padded_count - block_count, COMPONENTS, CZ), jnp.bfloat16)], axis=0)
    grouped = picked.reshape(padded_count // REFERENCE_GROUP, REFERENCE_GROUP, COMPONENTS, CZ)
    evaluated = lax.map(lambda one_group: network_group(one_group, w_in, b_in, w_mid, b_mid, w_out, b_out), grouped)
    evaluated = evaluated.reshape(padded_count, CLOSURE_TERMS, CZ)[:block_count]
    closure_blocks = jnp.zeros((CLOSURE_TERMS, NX, NY, NZB, CZ), jnp.bfloat16)
    closure_blocks = closure_blocks.at[:, place_x, place_y, place_z, :].set(jnp.transpose(evaluated, (1, 0, 2)))
    closure = closure_blocks.reshape(CLOSURE_TERMS, NX, NY, NZ)
    return flow_moments, closure
```

```python
import functools

import jax
import jax.numpy as jnp
from jax import lax
from jax.experimental import pallas as pl
from jax.experimental.pallas import tpu as pltpu
from jax.sharding import PartitionSpec as P


VELOCITIES = [
    (0, 0, 0),
    (1, 0, 0),
    (-1, 0, 0),
    (0, 1, 0),
    (0, -1, 0),
    (0, 0, 1),
    (0, 0, -1),
    (1, 1, 0),
    (-1, -1, 0),
    (1, -1, 0),
    (-1, 1, 0),
    (1, 0, 1),
    (-1, 0, -1),
    (1, 0, -1),
    (-1, 0, 1),
    (0, 1, 1),
    (0, -1, -1),
    (0, 1, -1),
    (0, -1, 1),
]
WEIGHTS = [1.0 / 3.0] + [1.0 / 18.0] * 6 + [1.0 / 36.0] * 12
OMEGA = 1.0 / 0.8
SHAPE_FACTOR = 0.95
ORIENT_STEP = 4.0
PAIRS = [(0, 0), (1, 1), (2, 2), (0, 1), (0, 2), (1, 2)]
ENTRY = [[0, 3, 4], [3, 1, 5], [4, 5, 2]]
TOWARD = {
    0: [i for i in range(19) if VELOCITIES[i][0] == -1],
    1: [i for i in range(19) if VELOCITIES[i][0] == 1],
}
KNOWN = {0: [i for i in range(19) if VELOCITIES[i][0] != 1], 1: [i for i in range(19) if VELOCITIES[i][0] != -1]}
MSG_WIDE = 23
MSG_ROWS = 1072
HALO_AT = 928
SIDE_AT = 1024
CORNER_AT = 1056
STATE = 38


def opposite(i):
    return 0 if i == 0 else (i + 1 if i % 2 == 1 else i - 1)


def lanes_of():
    return lax.broadcasted_iota(jnp.int32, (8, 128), 1)


def rows_of():
    return lax.broadcasted_iota(jnp.int32, (8, 128), 0)


def roll(v, shift, axis):
    shift = shift % v.shape[axis]
    return v if shift == 0 else pltpu.roll(v, shift, axis)


def add_all(terms):
    while len(terms) > 1:
        terms = [
            terms[k] + terms[k + 1] if k + 1 < len(terms) else terms[k] for k in range(0, len(terms), 2)
        ]
    return terms[0]


def moments(f, numbers):
    rho = add_all([f[i] for i in numbers])
    mom = []
    for ax in range(3):
        pos = [f[i] for i in numbers if VELOCITIES[i][ax] > 0]
        neg = [f[i] for i in numbers if VELOCITIES[i][ax] < 0]
        total = add_all(pos) if pos else None
        if neg:
            total = add_all(neg) * -1.0 if total is None else total - add_all(neg)
        mom.append(total)
    return rho, mom


def relax(f, rho, u, numbers):
    usq = 1.0 - 1.5 * (u[0] * u[0] + u[1] * u[1] + u[2] * u[2])
    scaled = {w: (w * OMEGA) * rho for w in sorted(set(WEIGHTS[i] for i in numbers))}
    out = {}
    for i in numbers:
        proj = None
        for ax in range(3):
            c = VELOCITIES[i][ax]
            if c != 0:
                if proj is None:
                    proj = u[ax] if c > 0 else -u[ax]
                else:
                    proj = proj + u[ax] if c > 0 else proj - u[ax]
        poly = usq if proj is None else usq + proj * (3.0 + 4.5 * proj)
        out[i] = f[i] * (1.0 - OMEGA) + scaled[WEIGHTS[i]] * poly
    return out


def plus(a, b):
    if a is None:
        return b
    if b is None:
        return a
    return a + b


def minus(a, b):
    if b is None:
        return a
    if a is None:
        return -b
    return a - b


def times(a, b):
    return None if a is None or b is None else a * b


def jeffery(a, g):
    half = [[None if g[j][k] is None else 0.5 * g[j][k] for k in range(3)] for j in range(3)]
    d = [[plus(half[j][k], half[k][j]) if j <= k else None for k in range(3)] for j in range(3)]
    w = [[minus(half[j][k], half[k][j]) if j < k else None for k in range(3)] for j in range(3)]
    full = lambda j, k: a[ENTRY[j][k]]
    strain = lambda j, k: d[min(j, k)][max(j, k)]

    def spin(j, k):
        if j == k:
            return None
        if j < k:
            return w[j][k]
        return None if w[k][j] is None else -w[k][j]

    contraction = None
    for j in range(3):
        contraction = plus(contraction, times(full(j, j), strain(j, j)))
    for j, k in ((0, 1), (0, 2), (1, 2)):
        cross = times(full(j, k), strain(j, k))
        contraction = plus(contraction, None if cross is None else 2.0 * cross)
    twice = 2.0 * contraction
    mix = [[plus(spin(j, k), times(strain(j, k), SHAPE_FACTOR)) for k in range(3)] for j in range(3)]
    z = [[None] * 3 for _ in range(3)]
    for j in range(3):
        for k in range(3):
            for m in range(3):
                z[j][k] = plus(z[j][k], times(full(j, m), mix[m][k]))
    scaled = SHAPE_FACTOR * twice
    return [plus(z[j][k], z[k][j]) - scaled * full(j, k) for j, k in PAIRS]


def put(ref, at, r, v):
    if r < 4:
        ref[at + (pl.ds(16 + 8 * r, 8), slice(None))] = v
    else:
        ref[at + (pl.ds(8, 8), slice(None))] = v
        ref[at + (pl.ds(48, 8), slice(None))] = v


def get(ref, at, r, dy=0):
    if r < 4:
        return ref[at + (pl.ds(16 + 8 * r + dy, 8), slice(None))]
    if dy == 0:
        return ref[at + (pl.ds(48, 8), slice(None))]
    return jnp.where(
        rows_of() < 4,
        ref[at + (pl.ds(48 + dy, 8), slice(None))],
        ref[at + (pl.ds(8 + dy, 8), slice(None))],
    )


def pull_z(own, side, dz, want_side=True):
    if dz == 0:
        return own, side
    lane = lanes_of()
    own_r, side_r = roll(own, dz, 1), roll(side, dz, 1)
    edge = lane == (0 if dz > 0 else 127)
    return jnp.where(edge, side_r, own_r), jnp.where(edge, own_r, side_r) if want_side else None


def walls():
    layer = lax.axis_index("gz")
    last = lax.axis_size("gz") - 1
    lane = lanes_of()
    low = lane == jnp.where(layer == 0, 0, -1)
    high = lane == jnp.where(layer == last, 127, -1)
    return low, high


def wall_of(i, low, high):
    dz = VELOCITIES[i][2]
    return None if dz == 0 else (low if dz > 0 else high)


def stream(ref, at_of, i, r, low, high, reflected, want_side=True):
    _, cy, cz = VELOCITIES[i]
    own = get(ref, at_of(0), r, -cy)
    side = get(ref, at_of(1), r, -cy) if (want_side or cz != 0) else None
    if cz == 0:
        return own, side
    own, side = pull_z(own, side, cz, want_side)
    return jnp.where(wall_of(i, low, high), reflected(), own), side


def central(ref, at_of, r, axis, low, high, outside, want_side=True):
    if axis == 1:
        out = []
        for t in (0, 1) if want_side else (0,):
            out.append(0.5 * (get(ref, at_of(t), r, 1) - get(ref, at_of(t), r, -1)))
        return out
    own, side = get(ref, at_of(0), r), get(ref, at_of(1), r)
    behind, behind_side = pull_z(own, side, 1, want_side)
    ahead, ahead_side = pull_z(own, side, -1, want_side)
    past = own if outside else jnp.zeros_like(own)
    diff = 0.5 * (jnp.where(high, past, ahead) - jnp.where(low, past, behind))
    return [diff, 0.5 * (ahead_side - behind_side)] if want_side else [diff]


def pack_z_kernel(pop, ori, zpack, low_rows, high_rows):
    lane = lax.broadcasted_iota(jnp.int32, (32, 128), 1)
    tiles = [jnp.zeros((32, 128), jnp.float32), jnp.zeros((32, 128), jnp.float32)]
    for f in range(25):
        for x in range(2):
            s = 2 * f + x
            src = pop if f < 19 else ori
            k = f if f < 19 else f - 19
            v = src[k, x]
            at = 4 * (s % 32)
            tiles[s // 32] = jnp.where((lane >= at) & (lane < at + 4), roll(v, at + 2, 1), tiles[s // 32])
            low_rows[pl.ds(2 * s, 2), :] = src[k, x, 0:2, :]
            high_rows[pl.ds(2 * s, 2), :] = src[k, x, 30:32, :]
    zpack[0] = tiles[0]
    zpack[1] = tiles[1]
    low_rows[100:104, :] = jnp.zeros((4, 128), jnp.float32)
    high_rows[100:104, :] = jnp.zeros((4, 128), jnp.float32)


def pack_y_kernel(from_minus, from_plus, low_in, high_in, sides, low_rows, high_rows):
    lane = lax.broadcasted_iota(jnp.int32, (32, 128), 1)
    low_rows[...] = low_in[...]
    high_rows[...] = high_in[...]
    for t in range(2):
        both = jnp.where(lane % 4 < 2, from_minus[t], from_plus[t])
        sides[t] = both
        low_rows[pl.ds(100 + 2 * t, 2), :] = sides[t, 0:2, :]
        high_rows[pl.ds(100 + 2 * t, 2), :] = sides[t, 30:32, :]


def step_one_kernel(pop, ori, sides, from_yminus, from_yplus, state, msg_low, msg_high, halo, fields, out):
    low, high = walls()
    lane, row = lanes_of(), rows_of()
    for s in range(52):
        halo[s, 0:2, :] = from_yplus[pl.ds(2 * s, 2), :]
        halo[s, 6:8, :] = from_yminus[pl.ds(2 * s, 2), :]

    def raw(f, x, t, r):
        s = 2 * f + x
        if t == 0:
            if r == 4:
                return halo[s]
            return pop[f, x, pl.ds(8 * r, 8), :] if f < 19 else ori[f - 19, x, pl.ds(8 * r, 8), :]
        packed = halo[50 + s // 32] if r == 4 else sides[s // 32, pl.ds(8 * r, 8), :]
        return roll(packed, -(4 * (s % 32) + 2), 1)

    numbers = list(range(19))
    for x in range(2):
        for t in range(2):
            for r in range(5):
                f = [raw(i, x, t, r) for i in numbers]
                rho, mom = moments(f, numbers)
                inv = 1.0 / rho
                u = [m * inv for m in mom]
                relaxed = relax(f, rho, u, numbers)
                for i in numbers:
                    put(fields, (i, x, t), r, relaxed[i])
                for j in range(3):
                    put(fields, (19 + j, x, t), r, u[j])
                for k in range(6):
                    put(fields, (22 + k, x, t), r, raw(19 + k, x, t, r))

    for x in range(2):
        for r in range(5):
            place = lambda f, xs=x: (lambda t: (f, xs, t))
            known = [{}, {}]
            for i in KNOWN[x]:
                xs = x - VELOCITIES[i][0]
                pair = stream(
                    fields, place(i, xs), i, r, low, high, lambda i=i: get(fields, (opposite(i), x, 0), r)
                )
                known[0][i], known[1][i] = pair
            grad = [[[None] * 3 for _ in range(3)] for _ in range(2)]
            sign = 0.5 if x == 0 else -0.5
            for j in range(3):
                by_y = central(fields, place(19 + j), r, 1, low, high, False)
                by_z = central(fields, place(19 + j), r, 2, low, high, False)
                for t in range(2):
                    grad[t][j][0] = sign * get(fields, (19 + j, 1 - x, t), r)
                    grad[t][j][1] = by_y[t]
                    grad[t][j][2] = by_z[t]
            u = [[get(fields, (19 + j, x, t), r) for j in range(3)] for t in range(2)]
            a = [[get(fields, (22 + k, x, t), r) for k in range(6)] for t in range(2)]
            advect = [[], []]
            for k in range(6):
                by_y = central(fields, place(22 + k), r, 1, low, high, True)
                by_z = central(fields, place(22 + k), r, 2, low, high, True)
                for t in range(2):
                    by_x = sign * get(fields, (22 + k, 1 - x, t), r)
                    advect[t].append(u[t][0] * by_x + u[t][1] * by_y[t] + u[t][2] * by_z[t])
            side_pack = jnp.zeros((8, 128), jnp.float32)
            for t in range(2):
                rate = jeffery(a[t], grad[t])
                part = [a[t][k] + ORIENT_STEP * (rate[k] - advect[t][k]) for k in range(6)]
                rho, mom = moments(known[t], KNOWN[x])
                outward = [get(fields, (i, x, t), r) for i in TOWARD[x]]
                keep = [known[t][i] for i in KNOWN[x]] + [rho] + mom + part + u[t] + a[t] + outward
                for k in range(STATE):
                    state[x, k, t, pl.ds(8 * r, 8), :] = keep[k]
                wide = outward + u[t] + a[t] + [rho] + mom + [known[t][i] for i in TOWARD[x]]
                if t == 1:
                    for k in range(MSG_WIDE):
                        at = 4 * k
                        side_pack = jnp.where((lane >= at) & (lane < at + 4), roll(wide[k], at + 2, 1), side_pack)
                elif r < 4:
                    for k, v in enumerate(wide + part):
                        out[x, pl.ds(32 * k + 8 * r, 8), :] = v
                else:
                    inner = (row >= 2) & (row < 6)
                    for k in range(0, MSG_WIDE, 2):
                        v = wide[k]
                        if k + 1 < MSG_WIDE:
                            v = jnp.where(inner, roll(wide[k + 1], 4, 0), v)
                        out[x, pl.ds(HALO_AT + 4 * k, 8), :] = v
            out[x, pl.ds(SIDE_AT + 8 * r if r < 4 else CORNER_AT, 8), :] = side_pack
    for x in range(2):
        out[x, pl.ds(CORNER_AT + 8, 8), :] = jnp.zeros((8, 128), jnp.float32)
    msg_low[...] = out[0].astype(jnp.bfloat16)
    msg_high[...] = out[1].astype(jnp.bfloat16)


def step_two_kernel(
    slots, state, from_low, from_high, w_one, w_mid, b_mid, w_out, b_out, flow, closure,
    got, fields, near, level, feats, spread, place,
):
    low, high = walls()
    got[0] = from_low[...].astype(jnp.float32)
    got[1] = from_high[...].astype(jnp.float32)
    for s in range(17):
        place[s] = 64
    for b in range(64):
        s = slots[b]
        place[jnp.where(s >= 0, s, 16)] = b

    def arrived(x, k, t, r):
        if t == 0 and r < 4:
            return got[x, pl.ds(32 * k + 8 * r, 8), :]
        if t == 0:
            v = got[x, pl.ds(HALO_AT + 8 * (k // 2), 8), :]
            return roll(v, 4, 0) if k % 2 else v
        v = got[x, pl.ds(SIDE_AT + 8 * r if r < 4 else CORNER_AT, 8), :]
        return roll(v, -(4 * k + 2), 1)

    kept = lambda x, k, t, r: state[x, k, t, pl.ds(8 * r, 8), :]
    for x in range(2):
        for t in range(2):
            for r in range(5):
                for k in range(5):
                    put(near, (x, k, t), r, arrived(x, k, t, r))
                    put(near, (x, 5 + k, t), r, kept(x, 33 + k, t, r))
    numbers = list(range(19))
    for x in range(2):
        come = TOWARD[1 - x]
        go = TOWARD[x]
        sign = -0.5 if x == 0 else 0.5
        for r in range(5):
            come_f, go_f = [{}, {}], [{}, {}]
            for k, i in enumerate(come):
                back = go.index(opposite(i))
                pair = stream(
                    near, lambda t, k=k: (x, k, t), i, r, low, high,
                    lambda back=back: get(near, (x, 5 + back, 0), r),
                )
                come_f[0][i], come_f[1][i] = pair
            for k, i in enumerate(go):
                back = come.index(opposite(i))
                pair = stream(
                    near, lambda t, k=k: (x, 5 + k, t), i, r, low, high,
                    lambda back=back: get(near, (x, back, 0), r),
                )
                go_f[0][i], go_f[1][i] = pair
            for t in range(2):
                f = {i: kept(x, k, t, r) for k, i in enumerate(KNOWN[x])}
                f.update(come_f[t])
                rho_new, mom_new = moments(come_f[t], come)
                rho = kept(x, 14, t, r) + rho_new
                mom = [kept(x, 15 + j, t, r) + mom_new[j] for j in range(3)]
                inv = 1.0 / rho
                u = [m * inv for m in mom]
                relaxed = relax(f, rho, u, numbers)
                for i in numbers:
                    put(fields, (i, x, t), r, relaxed[i])
                for j in range(3):
                    put(fields, (19 + j, x, t), r, u[j])
                u0 = [kept(x, 24 + j, t, r) for j in range(3)]
                a0 = [kept(x, 27 + k, t, r) for k in range(6)]
                u0n = [arrived(x, 5 + j, t, r) for j in range(3)]
                a0n = [arrived(x, 8 + k, t, r) for k in range(6)]
                rate = jeffery(a0, [[sign * u0n[j], None, None] for j in range(3)])
                drift = (sign * u0[0])
                for k in range(6):
                    a1 = kept(x, 18 + k, t, r) + ORIENT_STEP * (rate[k] - drift * a0n[k])
                    put(fields, (22 + k, x, t), r, a1)
                rho_new, mom_new = moments(go_f[t], go)
                rho = arrived(x, 14, t, r) + rho_new
                inv = 1.0 / rho
                u = [(arrived(x, 15 + j, t, r) + mom_new[j]) * inv for j in range(3)]
                f = {i: arrived(x, 18 + k, t, r) for k, i in enumerate(come)}
                relaxed = relax(f, rho, u, come)
                for k, i in enumerate(come):
                    put(fields, (28 + k, x, t), r, relaxed[i])
                if t == 0 and r < 4:
                    rate = jeffery(a0n, [[-sign * u0[j], None, None] for j in range(3)])
                    drift = -sign * u0n[0]
                    for j in range(3):
                        level[x, j, pl.ds(8 * r, 8), :] = u[j]
                    for k in range(6):
                        a1 = arrived(x, 23 + k, t, r) + ORIENT_STEP * (rate[k] - drift * a0[k])
                        level[x, 3 + k, pl.ds(8 * r, 8), :] = a1

    feats[...] = jnp.ones(feats.shape, jnp.float32)
    for x in range(2):
        for r in range(4):
            f = {}
            for i in numbers:
                xs = x - VELOCITIES[i][0]
                if 0 <= xs <= 1:
                    at_of = lambda t, i=i, xs=xs: (i, xs, t)
                else:
                    k = TOWARD[1 - x].index(i)
                    at_of = lambda t, k=k: (28 + k, x, t)
                f[i], _ = stream(
                    fields, at_of, i, r, low, high, lambda i=i: get(fields, (opposite(i), x, 0), r), False
                )
            rho, mom = moments(f, numbers)
            inv = 1.0 / rho
            final = [rho] + [m * inv for m in mom]
            for k in range(4):
                spread[pl.ds(k * 64 + x * 32 + 8 * r, 8), :] = final[k]
            sign = -0.5 if x == 0 else 0.5
            by_x = lambda k, n: sign * (level[x, n, pl.ds(8 * r, 8), :] - get(fields, (k, 1 - x, 0), r))
            grad = [[None] * 3 for _ in range(3)]
            for j in range(3):
                place_u = lambda t, j=j: (19 + j, x, t)
                grad[j][0] = by_x(19 + j, j)
                grad[j][1] = central(fields, place_u, r, 1, low, high, False, False)[0]
                grad[j][2] = central(fields, place_u, r, 2, low, high, False, False)[0]
            u = [get(fields, (19 + j, x, 0), r) for j in range(3)]
            a = [get(fields, (22 + k, x, 0), r) for k in range(6)]
            rate = jeffery(a, grad)
            for k in range(6):
                place_a = lambda t, k=k: (22 + k, x, t)
                advect = (
                    u[0] * by_x(22 + k, 3 + k)
                    + u[1] * central(fields, place_a, r, 1, low, high, True, False)[0]
                    + u[2] * central(fields, place_a, r, 2, low, high, True, False)[0]
                )
                new = a[k] + ORIENT_STEP * (rate[k] - advect)
                feats[pl.ds((x * 32 + 8 * r) * 8 + k, 8, 8), :] = new
    for k in range(4):
        for x in range(2):
            flow[k, x] = spread[pl.ds(k * 64 + x * 32, 32), :].astype(jnp.bfloat16)

    spread[...] = jnp.zeros(spread.shape, jnp.float32)
    ones = jnp.ones((8, 128), jnp.bfloat16)
    bias_mid = jnp.dot(b_mid[...], ones, preferred_element_type=jnp.float32)
    bias_out = jnp.dot(b_out[...], ones, preferred_element_type=jnp.float32)
    group = 2
    bias_mid = jnp.concatenate([bias_mid] * group, axis=1)
    for g in range(16 // group):
        at = [place[g * group + k] for k in range(group)]
        cells = [feats[pl.ds(pl.multiple_of(b * 8, 8), 8), :] for b in at]
        cells = jnp.concatenate(cells, axis=1).astype(jnp.bfloat16)
        v = jnp.dot(w_one[...], cells, preferred_element_type=jnp.float32)
        h = (v + v * jnp.tanh(v)).astype(jnp.bfloat16)
        v = jnp.dot(w_mid[...], h, preferred_element_type=jnp.float32) + bias_mid
        h = (v + v * jnp.tanh(v)).astype(jnp.bfloat16)
        v = jnp.dot(w_out[...], h, preferred_element_type=jnp.float32)
        for k in range(group):
            spread[pl.ds(pl.multiple_of(at[k] * 16, 16), 16), :] = v[:, 128 * k : 128 * k + 128] + bias_out
    for c in range(15):
        for x in range(2):
            closure[c, x] = spread[pl.ds(x * 512 + c, 32, 16), :].astype(jnp.bfloat16)


def split_bias(bias):
    high = lax.reduce_precision(bias, 8, 7)
    rest = lax.reduce_precision(bias - high, 8, 7)
    return jnp.stack([high, rest], axis=1).astype(jnp.bfloat16)


def local(populations, orientation, slot_table, w_in, b_in, w_mid, b_mid, w_out, b_out):
    f32, bf16 = jnp.float32, jnp.bfloat16
    shape = lambda *s, d=f32: jax.ShapeDtypeStruct(s, d)
    vmem = pl.BlockSpec(memory_space=pltpu.VMEM)
    smem = pl.BlockSpec(memory_space=pltpu.SMEM)
    params = pltpu.CompilerParams(vmem_limit_bytes=48 * 1024 * 1024)

    def ring(axis, step, wrap):
        n = lax.axis_size(axis)
        return [(i, (i + step) % n) for i in range(n) if wrap or 0 <= i + step < n]

    half_in = 0.5 * b_in
    half_mid = 0.5 * b_mid
    w_one = jnp.concatenate([(0.5 * w_in).T, split_bias(half_in)], axis=1)
    w_two = (0.5 * w_mid).T
    b_two = jnp.pad(split_bias(half_mid), ((0, 0), (0, 6)))
    w_three = jnp.pad(w_out.T, ((0, 1), (0, 0)))
    b_three = jnp.pad(split_bias(b_out), ((0, 1), (0, 6)))
    slots = slot_table.reshape(64)

    zpack, low_raw, high_raw = pl.pallas_call(
        pack_z_kernel,
        out_shape=(shape(2, 32, 128), shape(104, 128), shape(104, 128)),
        in_specs=[vmem] * 2,
        out_specs=(vmem,) * 3,
        compiler_params=params,
    )(populations, orientation)
    from_minus = lax.ppermute(zpack, "gz", ring("gz", 1, False))
    from_plus = lax.ppermute(zpack, "gz", ring("gz", -1, False))
    sides, low_rows, high_rows = pl.pallas_call(
        pack_y_kernel,
        out_shape=(shape(2, 32, 128), shape(104, 128), shape(104, 128)),
        in_specs=[vmem] * 4,
        out_specs=(vmem,) * 3,
        compiler_params=params,
    )(from_minus, from_plus, low_raw, high_raw)
    from_yminus = lax.ppermute(high_rows, "gy", ring("gy", 1, True))
    from_yplus = lax.ppermute(low_rows, "gy", ring("gy", -1, True))
    state, msg_low, msg_high = pl.pallas_call(
        step_one_kernel,
        out_shape=(
            shape(2, STATE, 2, 40, 128),
            shape(MSG_ROWS, 128, d=bf16),
            shape(MSG_ROWS, 128, d=bf16),
        ),
        in_specs=[vmem] * 5,
        out_specs=(vmem,) * 3,
        scratch_shapes=[
            pltpu.VMEM((52, 8, 128), f32),
            pltpu.VMEM((28, 2, 2, 64, 128), f32),
            pltpu.VMEM((2, MSG_ROWS, 128), f32),
        ],
        compiler_params=params,
    )(populations, orientation, sides, from_yminus, from_yplus)
    from_low = lax.ppermute(msg_high, "gx", ring("gx", 1, True))
    from_high = lax.ppermute(msg_low, "gx", ring("gx", -1, True))
    return pl.pallas_call(
        step_two_kernel,
        out_shape=(shape(4, 2, 32, 128, d=bf16), shape(15, 2, 32, 128, d=bf16)),
        in_specs=[smem] + [vmem] * 8,
        out_specs=(vmem,) * 2,
        scratch_shapes=[
            pltpu.VMEM((2, MSG_ROWS, 128), f32),
            pltpu.VMEM((33, 2, 2, 64, 128), f32),
            pltpu.VMEM((2, 10, 2, 64, 128), f32),
            pltpu.VMEM((2, 9, 32, 128), f32),
            pltpu.VMEM((65 * 8, 128), f32),
            pltpu.VMEM((65 * 16, 128), f32),
            pltpu.SMEM((17,), jnp.int32),
        ],
        compiler_params=params,
    )(slots, state, from_low, from_high, w_one, w_two, b_two, w_three, b_three)


def solution(mesh):
    grid = P(None, "gx", "gy", "gz")
    in_specs = (grid, grid, P("gx", "gy", "gz"), P(), P(), P(), P(), P(), P())
    return jax.shard_map(local, mesh=mesh, in_specs=in_specs, out_specs=(grid, grid), check_vma=False)
```

```python
import functools

import jax
import jax.numpy as jnp
from jax import lax
from jax.experimental import pallas as pl
from jax.experimental.pallas import tpu as pltpu
from jax.sharding import PartitionSpec as P


VELOCITIES = [
    (0, 0, 0),
    (1, 0, 0),
    (-1, 0, 0),
    (0, 1, 0),
    (0, -1, 0),
    (0, 0, 1),
    (0, 0, -1),
    (1, 1, 0),
    (-1, -1, 0),
    (1, -1, 0),
    (-1, 1, 0),
    (1, 0, 1),
    (-1, 0, -1),
    (1, 0, -1),
    (-1, 0, 1),
    (0, 1, 1),
    (0, -1, -1),
    (0, 1, -1),
    (0, -1, 1),
]
WEIGHTS = [1.0 / 3.0] + [1.0 / 18.0] * 6 + [1.0 / 36.0] * 12
OMEGA = 1.0 / 0.8
SHAPE_FACTOR = 0.95
ORIENT_STEP = 4.0
PAIRS = [(0, 0), (1, 1), (2, 2), (0, 1), (0, 2), (1, 2)]
ENTRY = [[0, 3, 4], [3, 1, 5], [4, 5, 2]]
TOWARD = {
    0: [i for i in range(19) if VELOCITIES[i][0] == -1],
    1: [i for i in range(19) if VELOCITIES[i][0] == 1],
}
KNOWN = {0: [i for i in range(19) if VELOCITIES[i][0] != 1], 1: [i for i in range(19) if VELOCITIES[i][0] != -1]}
MSG_WIDE = 23
MSG_ROWS = 1072
HALO_AT = 928
SIDE_AT = 1024
CORNER_AT = 1056
MIB = 1024 * 1024
LIMIT_PACK = 5375 * MIB // 100
LIMIT_OWN = 5270 * MIB // 100
LIMIT_WEIGHTS = 4900 * MIB // 100
STATE = 38


def opposite(i):
    return 0 if i == 0 else (i + 1 if i % 2 == 1 else i - 1)


def lanes_of():
    return lax.broadcasted_iota(jnp.int32, (8, 128), 1)


def rows_of():
    return lax.broadcasted_iota(jnp.int32, (8, 128), 0)


def roll(v, shift, axis):
    shift = shift % v.shape[axis]
    return v if shift == 0 else pltpu.roll(v, shift, axis)


def add_all(terms):
    while len(terms) > 1:
        terms = [
            terms[k] + terms[k + 1] if k + 1 < len(terms) else terms[k] for k in range(0, len(terms), 2)
        ]
    return terms[0]


def moments(f, numbers):
    rho = add_all([f[i] for i in numbers])
    mom = []
    for ax in range(3):
        pos = [f[i] for i in numbers if VELOCITIES[i][ax] > 0]
        neg = [f[i] for i in numbers if VELOCITIES[i][ax] < 0]
        total = add_all(pos) if pos else None
        if neg:
            total = add_all(neg) * -1.0 if total is None else total - add_all(neg)
        mom.append(total)
    return rho, mom


def relax(f, rho, u, numbers):
    usq = 1.0 - 1.5 * (u[0] * u[0] + u[1] * u[1] + u[2] * u[2])
    scaled = {w: (w * OMEGA) * rho for w in sorted(set(WEIGHTS[i] for i in numbers))}
    out = {}
    for i in numbers:
        proj = None
        for ax in range(3):
            c = VELOCITIES[i][ax]
            if c != 0:
                if proj is None:
                    proj = u[ax] if c > 0 else -u[ax]
                else:
                    proj = proj + u[ax] if c > 0 else proj - u[ax]
        poly = usq if proj is None else usq + proj * (3.0 + 4.5 * proj)
        out[i] = f[i] * (1.0 - OMEGA) + scaled[WEIGHTS[i]] * poly
    return out


def plus(a, b):
    if a is None:
        return b
    if b is None:
        return a
    return a + b


def minus(a, b):
    if b is None:
        return a
    if a is None:
        return -b
    return a - b


def times(a, b):
    return None if a is None or b is None else a * b


def jeffery(a, g):
    half = [[None if g[j][k] is None else 0.5 * g[j][k] for k in range(3)] for j in range(3)]
    d = [[plus(half[j][k], half[k][j]) if j <= k else None for k in range(3)] for j in range(3)]
    w = [[minus(half[j][k], half[k][j]) if j < k else None for k in range(3)] for j in range(3)]
    full = lambda j, k: a[ENTRY[j][k]]
    strain = lambda j, k: d[min(j, k)][max(j, k)]

    def spin(j, k):
        if j == k:
            return None
        if j < k:
            return w[j][k]
        return None if w[k][j] is None else -w[k][j]

    contraction = None
    for j in range(3):
        contraction = plus(contraction, times(full(j, j), strain(j, j)))
    for j, k in ((0, 1), (0, 2), (1, 2)):
        cross = times(full(j, k), strain(j, k))
        contraction = plus(contraction, None if cross is None else 2.0 * cross)
    twice = 2.0 * contraction
    mix = [[plus(spin(j, k), times(strain(j, k), SHAPE_FACTOR)) for k in range(3)] for j in range(3)]
    z = [[None] * 3 for _ in range(3)]
    for j in range(3):
        for k in range(3):
            for m in range(3):
                z[j][k] = plus(z[j][k], times(full(j, m), mix[m][k]))
    scaled = SHAPE_FACTOR * twice
    return [plus(z[j][k], z[k][j]) - scaled * full(j, k) for j, k in PAIRS]


def put(ref, at, r, v):
    if r < 4:
        ref[at + (pl.ds(16 + 8 * r, 8), slice(None))] = v
    else:
        ref[at + (pl.ds(8, 8), slice(None))] = v
        ref[at + (pl.ds(48, 8), slice(None))] = v


def get(ref, at, r, dy=0):
    if r < 4:
        return ref[at + (pl.ds(16 + 8 * r + dy, 8), slice(None))]
    if dy == 0:
        return ref[at + (pl.ds(48, 8), slice(None))]
    return jnp.where(
        rows_of() < 4,
        ref[at + (pl.ds(48 + dy, 8), slice(None))],
        ref[at + (pl.ds(8 + dy, 8), slice(None))],
    )


def pull_z(own, side, dz, want_side=True):
    if dz == 0:
        return own, side
    lane = lanes_of()
    own_r, side_r = roll(own, dz, 1), roll(side, dz, 1)
    edge = lane == (0 if dz > 0 else 127)
    return jnp.where(edge, side_r, own_r), jnp.where(edge, own_r, side_r) if want_side else None


def walls():
    layer = lax.axis_index("gz")
    last = lax.axis_size("gz") - 1
    lane = lanes_of()
    low = lane == jnp.where(layer == 0, 0, -1)
    high = lane == jnp.where(layer == last, 127, -1)
    return low, high


def wall_of(i, low, high):
    dz = VELOCITIES[i][2]
    return None if dz == 0 else (low if dz > 0 else high)


def stream(ref, at_of, i, r, low, high, reflected, want_side=True):
    _, cy, cz = VELOCITIES[i]
    own = get(ref, at_of(0), r, -cy)
    side = get(ref, at_of(1), r, -cy) if (want_side or cz != 0) else None
    if cz == 0:
        return own, side
    own, side = pull_z(own, side, cz, want_side)
    return jnp.where(wall_of(i, low, high), reflected(), own), side


def central(ref, at_of, r, axis, low, high, outside, want_side=True):
    if axis == 1:
        out = []
        for t in (0, 1) if want_side else (0,):
            out.append(0.5 * (get(ref, at_of(t), r, 1) - get(ref, at_of(t), r, -1)))
        return out
    own, side = get(ref, at_of(0), r), get(ref, at_of(1), r)
    behind, behind_side = pull_z(own, side, 1, want_side)
    ahead, ahead_side = pull_z(own, side, -1, want_side)
    past = own if outside else jnp.zeros_like(own)
    diff = 0.5 * (jnp.where(high, past, ahead) - jnp.where(low, past, behind))
    return [diff, 0.5 * (ahead_side - behind_side)] if want_side else [diff]


def fetch(pairs, sems):
    copies = [pltpu.make_async_copy(src, dst, sems.at[k]) for k, (src, dst) in enumerate(pairs)]
    for copy in copies:
        copy.start()
    return copies


def pack_z_kernel(pop_hbm, ori_hbm, zpack, low_rows, high_rows, pop, ori, sems):
    for copy in fetch([(pop_hbm, pop), (ori_hbm, ori)], sems):
        copy.wait()
    lane = lax.broadcasted_iota(jnp.int32, (32, 128), 1)
    tiles = [jnp.zeros((32, 128), jnp.float32), jnp.zeros((32, 128), jnp.float32)]
    for f in range(25):
        for x in range(2):
            s = 2 * f + x
            src = pop if f < 19 else ori
            k = f if f < 19 else f - 19
            v = src[k, x]
            at = 4 * (s % 32)
            tiles[s // 32] = jnp.where((lane >= at) & (lane < at + 4), roll(v, at + 2, 1), tiles[s // 32])
            low_rows[pl.ds(2 * s, 2), :] = src[k, x, 0:2, :]
            high_rows[pl.ds(2 * s, 2), :] = src[k, x, 30:32, :]
    zpack[0] = tiles[0]
    zpack[1] = tiles[1]
    low_rows[100:104, :] = jnp.zeros((4, 128), jnp.float32)
    high_rows[100:104, :] = jnp.zeros((4, 128), jnp.float32)


def own_kernel(pop_hbm, ori_hbm, after, own, pop, ori, sems):
    del after
    for copy in fetch([(pop_hbm, pop), (ori_hbm, ori)], sems):
        copy.wait()
    numbers = list(range(19))
    for x in range(2):
        for r in range(4):
            rows = pl.ds(8 * r, 8)
            f = [pop[i, x, rows, :] for i in numbers]
            rho, mom = moments(f, numbers)
            inv = 1.0 / rho
            u = [m * inv for m in mom]
            relaxed = relax(f, rho, u, numbers)
            for i in numbers:
                own[i, x, rows, :] = relaxed[i]
            for j in range(3):
                own[19 + j, x, rows, :] = u[j]
            for k in range(6):
                own[22 + k, x, rows, :] = ori[k, x, rows, :]


def pack_y_kernel(from_minus, from_plus, low_in, high_in, sides, low_rows, high_rows):
    lane = lax.broadcasted_iota(jnp.int32, (32, 128), 1)
    low_rows[...] = low_in[...]
    high_rows[...] = high_in[...]
    for t in range(2):
        both = jnp.where(lane % 4 < 2, from_minus[t], from_plus[t])
        sides[t] = both
        low_rows[pl.ds(100 + 2 * t, 2), :] = sides[t, 0:2, :]
        high_rows[pl.ds(100 + 2 * t, 2), :] = sides[t, 30:32, :]


def step_one_kernel(own, sides, from_yminus, from_yplus, state, msg_low, msg_high, halo, fields, out):
    low, high = walls()
    lane, row = lanes_of(), rows_of()
    for s in range(52):
        halo[s, 0:2, :] = from_yplus[pl.ds(2 * s, 2), :]
        halo[s, 6:8, :] = from_yminus[pl.ds(2 * s, 2), :]

    def raw(f, x, t, r):
        s = 2 * f + x
        if t == 0:
            return halo[s]
        packed = halo[50 + s // 32] if r == 4 else sides[s // 32, pl.ds(8 * r, 8), :]
        return roll(packed, -(4 * (s % 32) + 2), 1)

    numbers = list(range(19))
    for x in range(2):
        for t in range(2):
            for r in range(5):
                if t == 0 and r < 4:
                    for k in range(28):
                        put(fields, (k, x, t), r, own[k, x, pl.ds(8 * r, 8), :])
                    continue
                f = [raw(i, x, t, r) for i in numbers]
                rho, mom = moments(f, numbers)
                inv = 1.0 / rho
                u = [m * inv for m in mom]
                relaxed = relax(f, rho, u, numbers)
                for i in numbers:
                    put(fields, (i, x, t), r, relaxed[i])
                for j in range(3):
                    put(fields, (19 + j, x, t), r, u[j])
                for k in range(6):
                    put(fields, (22 + k, x, t), r, raw(19 + k, x, t, r))

    for x in range(2):
        for r in range(5):
            place = lambda f, xs=x: (lambda t: (f, xs, t))
            known = [{}, {}]
            for i in KNOWN[x]:
                xs = x - VELOCITIES[i][0]
                pair = stream(
                    fields, place(i, xs), i, r, low, high, lambda i=i: get(fields, (opposite(i), x, 0), r)
                )
                known[0][i], known[1][i] = pair
            grad = [[[None] * 3 for _ in range(3)] for _ in range(2)]
            sign = 0.5 if x == 0 else -0.5
            for j in range(3):
                by_y = central(fields, place(19 + j), r, 1, low, high, False)
                by_z = central(fields, place(19 + j), r, 2, low, high, False)
                for t in range(2):
                    grad[t][j][0] = sign * get(fields, (19 + j, 1 - x, t), r)
                    grad[t][j][1] = by_y[t]
                    grad[t][j][2] = by_z[t]
            u = [[get(fields, (19 + j, x, t), r) for j in range(3)] for t in range(2)]
            a = [[get(fields, (22 + k, x, t), r) for k in range(6)] for t in range(2)]
            advect = [[], []]
            for k in range(6):
                by_y = central(fields, place(22 + k), r, 1, low, high, True)
                by_z = central(fields, place(22 + k), r, 2, low, high, True)
                for t in range(2):
                    by_x = sign * get(fields, (22 + k, 1 - x, t), r)
                    advect[t].append(u[t][0] * by_x + u[t][1] * by_y[t] + u[t][2] * by_z[t])
            side_pack = jnp.zeros((8, 128), jnp.float32)
            for t in range(2):
                rate = jeffery(a[t], grad[t])
                part = [a[t][k] + ORIENT_STEP * (rate[k] - advect[t][k]) for k in range(6)]
                rho, mom = moments(known[t], KNOWN[x])
                outward = [get(fields, (i, x, t), r) for i in TOWARD[x]]
                keep = [known[t][i] for i in KNOWN[x]] + [rho] + mom + part + u[t] + a[t] + outward
                for k in range(STATE):
                    state[x, k, t, pl.ds(8 * r, 8), :] = keep[k]
                wide = outward + u[t] + a[t] + [rho] + mom + [known[t][i] for i in TOWARD[x]]
                if t == 1:
                    for k in range(MSG_WIDE):
                        at = 4 * k
                        side_pack = jnp.where((lane >= at) & (lane < at + 4), roll(wide[k], at + 2, 1), side_pack)
                elif r < 4:
                    for k, v in enumerate(wide + part):
                        out[x, pl.ds(32 * k + 8 * r, 8), :] = v
                else:
                    inner = (row >= 2) & (row < 6)
                    for k in range(0, MSG_WIDE, 2):
                        v = wide[k]
                        if k + 1 < MSG_WIDE:
                            v = jnp.where(inner, roll(wide[k + 1], 4, 0), v)
                        out[x, pl.ds(HALO_AT + 4 * k, 8), :] = v
            out[x, pl.ds(SIDE_AT + 8 * r if r < 4 else CORNER_AT, 8), :] = side_pack
    for x in range(2):
        out[x, pl.ds(CORNER_AT + 8, 8), :] = jnp.zeros((8, 128), jnp.float32)
    msg_low[...] = out[0].astype(jnp.bfloat16)
    msg_high[...] = out[1].astype(jnp.bfloat16)


def weights_kernel(
    w_in_hbm, b_in_hbm, w_mid_hbm, b_mid_hbm, w_out_hbm, b_out_hbm, w_one, w_two, bias_mid, w_three, bias_out,
    w_in, b_in, w_mid, b_mid, b_out, wide, sems,
):
    pairs = [
        (w_mid_hbm, w_mid),
        (w_in_hbm, w_in),
        (b_in_hbm, b_in),
        (b_mid_hbm, b_mid),
        (b_out_hbm, b_out),
        (w_out_hbm, w_three),
    ]
    for copy in fetch(pairs, sems):
        copy.wait()
    f32, bf16 = jnp.float32, jnp.bfloat16
    row = lax.broadcasted_iota(jnp.int32, (8, 512), 0)
    bias = jnp.broadcast_to(0.5 * b_in[...], (8, 512))
    first = bias.astype(bf16).astype(f32)
    rest = bias - first
    padded = jnp.concatenate([0.5 * w_in[...].astype(f32), jnp.zeros((2, 512), f32)], axis=0)
    stacked = jnp.where(row == 6, first, jnp.where(row == 7, rest, padded))
    w_one[...] = stacked.T.astype(bf16)
    w_two[...] = (0.5 * w_mid[...].astype(f32)).T.astype(bf16)
    bias_mid[...] = jnp.broadcast_to(jnp.broadcast_to(0.5 * b_mid[...], (8, 512)).T[:, 0:1], (512, 128))
    wide[...] = jnp.zeros(wide.shape, f32)
    wide[:, 0:15] = jnp.broadcast_to(b_out[...], (8, 15))
    bias_out[...] = jnp.broadcast_to(wide[...].T[0:16, 0:1], (16, 128))


def step_two_kernel(
    slots, state, from_low, from_high, w_one, w_mid, b_mid, w_out, b_out, flow, closure,
    got, fields, near, level, feats, spread, place,
):
    low, high = walls()
    got[0] = from_low[...].astype(jnp.float32)
    got[1] = from_high[...].astype(jnp.float32)
    for s in range(17):
        place[s] = 64
    for b in range(64):
        s = slots[b // 32, 0, b % 32]
        place[jnp.where(s >= 0, s, 16)] = b

    def arrived(x, k, t, r):
        if t == 0 and r < 4:
            return got[x, pl.ds(32 * k + 8 * r, 8), :]
        if t == 0:
            v = got[x, pl.ds(HALO_AT + 8 * (k // 2), 8), :]
            return roll(v, 4, 0) if k % 2 else v
        v = got[x, pl.ds(SIDE_AT + 8 * r if r < 4 else CORNER_AT, 8), :]
        return roll(v, -(4 * k + 2), 1)

    kept = lambda x, k, t, r: state[x, k, t, pl.ds(8 * r, 8), :]
    for x in range(2):
        for t in range(2):
            for r in range(5):
                for k in range(5):
                    put(near, (x, k, t), r, arrived(x, k, t, r))
                    put(near, (x, 5 + k, t), r, kept(x, 33 + k, t, r))
    numbers = list(range(19))
    for x in range(2):
        come = TOWARD[1 - x]
        go = TOWARD[x]
        sign = -0.5 if x == 0 else 0.5
        for r in range(5):
            come_f, go_f = [{}, {}], [{}, {}]
            for k, i in enumerate(come):
                back = go.index(opposite(i))
                pair = stream(
                    near, lambda t, k=k: (x, k, t), i, r, low, high,
                    lambda back=back: get(near, (x, 5 + back, 0), r),
                )
                come_f[0][i], come_f[1][i] = pair
            for k, i in enumerate(go):
                back = come.index(opposite(i))
                pair = stream(
                    near, lambda t, k=k: (x, 5 + k, t), i, r, low, high,
                    lambda back=back: get(near, (x, back, 0), r),
                )
                go_f[0][i], go_f[1][i] = pair
            for t in range(2):
                f = {i: kept(x, k, t, r) for k, i in enumerate(KNOWN[x])}
                f.update(come_f[t])
                rho_new, mom_new = moments(come_f[t], come)
                rho = kept(x, 14, t, r) + rho_new
                mom = [kept(x, 15 + j, t, r) + mom_new[j] for j in range(3)]
                inv = 1.0 / rho
                u = [m * inv for m in mom]
                relaxed = relax(f, rho, u, numbers)
                for i in numbers:
                    put(fields, (i, x, t), r, relaxed[i])
                for j in range(3):
                    put(fields, (19 + j, x, t), r, u[j])
                u0 = [kept(x, 24 + j, t, r) for j in range(3)]
                a0 = [kept(x, 27 + k, t, r) for k in range(6)]
                u0n = [arrived(x, 5 + j, t, r) for j in range(3)]
                a0n = [arrived(x, 8 + k, t, r) for k in range(6)]
                rate = jeffery(a0, [[sign * u0n[j], None, None] for j in range(3)])
                drift = (sign * u0[0])
                for k in range(6):
                    a1 = kept(x, 18 + k, t, r) + ORIENT_STEP * (rate[k] - drift * a0n[k])
                    put(fields, (22 + k, x, t), r, a1)
                rho_new, mom_new = moments(go_f[t], go)
                rho = arrived(x, 14, t, r) + rho_new
                inv = 1.0 / rho
                u = [(arrived(x, 15 + j, t, r) + mom_new[j]) * inv for j in range(3)]
                f = {i: arrived(x, 18 + k, t, r) for k, i in enumerate(come)}
                relaxed = relax(f, rho, u, come)
                for k, i in enumerate(come):
                    put(fields, (28 + k, x, t), r, relaxed[i])
                if t == 0 and r < 4:
                    rate = jeffery(a0n, [[-sign * u0[j], None, None] for j in range(3)])
                    drift = -sign * u0n[0]
                    for j in range(3):
                        level[x, j, pl.ds(8 * r, 8), :] = u[j]
                    for k in range(6):
                        a1 = arrived(x, 23 + k, t, r) + ORIENT_STEP * (rate[k] - drift * a0[k])
                        level[x, 3 + k, pl.ds(8 * r, 8), :] = a1

    feats[...] = jnp.ones(feats.shape, jnp.float32)
    for x in range(2):
        for r in range(4):
            f = {}
            for i in numbers:
                xs = x - VELOCITIES[i][0]
                if 0 <= xs <= 1:
                    at_of = lambda t, i=i, xs=xs: (i, xs, t)
                else:
                    k = TOWARD[1 - x].index(i)
                    at_of = lambda t, k=k: (28 + k, x, t)
                f[i], _ = stream(
                    fields, at_of, i, r, low, high, lambda i=i: get(fields, (opposite(i), x, 0), r), False
                )
            rho, mom = moments(f, numbers)
            inv = 1.0 / rho
            final = [rho] + [m * inv for m in mom]
            for k in range(4):
                spread[pl.ds(k * 64 + x * 32 + 8 * r, 8), :] = final[k]
            sign = -0.5 if x == 0 else 0.5
            by_x = lambda k, n: sign * (level[x, n, pl.ds(8 * r, 8), :] - get(fields, (k, 1 - x, 0), r))
            grad = [[None] * 3 for _ in range(3)]
            for j in range(3):
                place_u = lambda t, j=j: (19 + j, x, t)
                grad[j][0] = by_x(19 + j, j)
                grad[j][1] = central(fields, place_u, r, 1, low, high, False, False)[0]
                grad[j][2] = central(fields, place_u, r, 2, low, high, False, False)[0]
            u = [get(fields, (19 + j, x, 0), r) for j in range(3)]
            a = [get(fields, (22 + k, x, 0), r) for k in range(6)]
            rate = jeffery(a, grad)
            for k in range(6):
                place_a = lambda t, k=k: (22 + k, x, t)
                advect = (
                    u[0] * by_x(22 + k, 3 + k)
                    + u[1] * central(fields, place_a, r, 1, low, high, True, False)[0]
                    + u[2] * central(fields, place_a, r, 2, low, high, True, False)[0]
                )
                new = a[k] + ORIENT_STEP * (rate[k] - advect)
                feats[pl.ds((x * 32 + 8 * r) * 8 + k, 8, 8), :] = new
    for k in range(4):
        for x in range(2):
            flow[k, x] = spread[pl.ds(k * 64 + x * 32, 32), :].astype(jnp.bfloat16)

    spread[...] = jnp.zeros(spread.shape, jnp.float32)
    group = 8
    bias_mid = jnp.concatenate([b_mid[...]] * group, axis=1)
    for g in range(16 // group):
        at = [place[g * group + k] for k in range(group)]
        cells = [feats[pl.ds(pl.multiple_of(b * 8, 8), 8), :] for b in at]
        cells = jnp.concatenate(cells, axis=1).astype(jnp.bfloat16)
        v = jnp.dot(w_one[...], cells, preferred_element_type=jnp.float32)
        h = (v + v * jnp.tanh(v)).astype(jnp.bfloat16)
        v = jnp.dot(w_mid[...], h, preferred_element_type=jnp.float32) + bias_mid
        h = (v + v * jnp.tanh(v)).astype(jnp.bfloat16)
        v = jnp.dot(w_out[...], h, preferred_element_type=jnp.float32)
        for k in range(group):
            spread[pl.ds(pl.multiple_of(at[k] * 16, 16), 15), :] = v[:, 128 * k : 128 * k + 128] + b_out[0:15, :]
    for c in range(15):
        for x in range(2):
            closure[c, x] = spread[pl.ds(x * 512 + c, 32, 16), :].astype(jnp.bfloat16)


def local(populations, orientation, slot_table, w_in, b_in, w_mid, b_mid, w_out, b_out):
    f32, bf16 = jnp.float32, jnp.bfloat16
    shape = lambda *s, d=f32: jax.ShapeDtypeStruct(s, d)
    vmem = pl.BlockSpec(memory_space=pltpu.VMEM)
    smem = pl.BlockSpec(memory_space=pltpu.SMEM)
    params = pltpu.CompilerParams(vmem_limit_bytes=48 * 1024 * 1024)

    def ring(axis, step, wrap):
        n = lax.axis_size(axis)
        return [(i, (i + step) % n) for i in range(n) if wrap or 0 <= i + step < n]

    hbm = pl.BlockSpec(memory_space=pltpu.HBM)
    slots = jnp.transpose(slot_table, (0, 2, 1))
    w_one, w_two, bias_mid, w_three, bias_out = pl.pallas_call(
        weights_kernel,
        out_shape=(
            shape(512, 8, d=bf16),
            shape(512, 512, d=bf16),
            shape(512, 128),
            shape(15, 512, d=bf16),
            shape(16, 128),
        ),
        in_specs=[hbm] * 6,
        out_specs=(vmem,) * 5,
        scratch_shapes=[
            pltpu.VMEM((6, 512), bf16),
            pltpu.VMEM((1, 512), f32),
            pltpu.VMEM((512, 512), bf16),
            pltpu.VMEM((1, 512), f32),
            pltpu.VMEM((1, 15), f32),
            pltpu.VMEM((8, 128), f32),
            pltpu.SemaphoreType.DMA((6,)),
        ],
        compiler_params=pltpu.CompilerParams(vmem_limit_bytes=LIMIT_WEIGHTS),
    )(w_in, b_in.reshape(1, 512), w_mid, b_mid.reshape(1, 512), w_out.T, b_out.reshape(1, 15))
    raw_scratch = [pltpu.VMEM((19, 2, 32, 128), f32), pltpu.VMEM((6, 2, 32, 128), f32), pltpu.SemaphoreType.DMA((2,))]
    zpack, low_raw, high_raw = pl.pallas_call(
        pack_z_kernel,
        out_shape=(shape(2, 32, 128), shape(104, 128), shape(104, 128)),
        in_specs=[hbm] * 2,
        out_specs=(vmem,) * 3,
        scratch_shapes=raw_scratch,
        compiler_params=pltpu.CompilerParams(vmem_limit_bytes=LIMIT_PACK),
    )(populations, orientation)
    own = pl.pallas_call(
        own_kernel,
        out_shape=shape(28, 2, 32, 128),
        in_specs=[hbm] * 3,
        out_specs=vmem,
        scratch_shapes=raw_scratch,
        compiler_params=pltpu.CompilerParams(vmem_limit_bytes=LIMIT_OWN),
    )(populations, orientation, zpack)
    from_minus = lax.ppermute(zpack, "gz", ring("gz", 1, False))
    from_plus = lax.ppermute(zpack, "gz", ring("gz", -1, False))
    sides, low_rows, high_rows = pl.pallas_call(
        pack_y_kernel,
        out_shape=(shape(2, 32, 128), shape(104, 128), shape(104, 128)),
        in_specs=[vmem] * 4,
        out_specs=(vmem,) * 3,
        compiler_params=params,
    )(from_minus, from_plus, low_raw, high_raw)
    from_yminus = lax.ppermute(high_rows, "gy", ring("gy", 1, True))
    from_yplus = lax.ppermute(low_rows, "gy", ring("gy", -1, True))
    state, msg_low, msg_high = pl.pallas_call(
        step_one_kernel,
        out_shape=(
            shape(2, STATE, 2, 40, 128),
            shape(MSG_ROWS, 128, d=bf16),
            shape(MSG_ROWS, 128, d=bf16),
        ),
        in_specs=[vmem] * 4,
        out_specs=(vmem,) * 3,
        scratch_shapes=[
            pltpu.VMEM((52, 8, 128), f32),
            pltpu.VMEM((28, 2, 2, 64, 128), f32),
            pltpu.VMEM((2, MSG_ROWS, 128), f32),
        ],
        compiler_params=params,
    )(own, sides, from_yminus, from_yplus)
    from_low = lax.ppermute(msg_high, "gx", ring("gx", 1, True))
    from_high = lax.ppermute(msg_low, "gx", ring("gx", -1, True))
    return pl.pallas_call(
        step_two_kernel,
        out_shape=(shape(4, 2, 32, 128, d=bf16), shape(15, 2, 32, 128, d=bf16)),
        in_specs=[smem] + [vmem] * 8,
        out_specs=(vmem,) * 2,
        scratch_shapes=[
            pltpu.VMEM((2, MSG_ROWS, 128), f32),
            pltpu.VMEM((33, 2, 2, 64, 128), f32),
            pltpu.VMEM((2, 10, 2, 64, 128), f32),
            pltpu.VMEM((2, 9, 32, 128), f32),
            pltpu.VMEM((65 * 8, 128), f32),
            pltpu.VMEM((65 * 16, 128), f32),
            pltpu.SMEM((17,), jnp.int32),
        ],
        compiler_params=params,
    )(slots, state, from_low, from_high, w_one, w_two, bias_mid, w_three, bias_out)


def solution(mesh):
    grid = P(None, "gx", "gy", "gz")
    in_specs = (grid, grid, P("gx", "gy", "gz"), P(), P(), P(), P(), P(), P())
    return jax.shard_map(local, mesh=mesh, in_specs=in_specs, out_specs=(grid, grid), check_vma=False)
```

```python
import functools

import jax
import jax.numpy as jnp
from jax import lax
from jax.experimental import pallas as pl
from jax.experimental.pallas import tpu as pltpu
from jax.sharding import PartitionSpec as P


VELOCITIES = [
    (0, 0, 0),
    (1, 0, 0),
    (-1, 0, 0),
    (0, 1, 0),
    (0, -1, 0),
    (0, 0, 1),
    (0, 0, -1),
    (1, 1, 0),
    (-1, -1, 0),
    (1, -1, 0),
    (-1, 1, 0),
    (1, 0, 1),
    (-1, 0, -1),
    (1, 0, -1),
    (-1, 0, 1),
    (0, 1, 1),
    (0, -1, -1),
    (0, 1, -1),
    (0, -1, 1),
]
WEIGHTS = [1.0 / 3.0] + [1.0 / 18.0] * 6 + [1.0 / 36.0] * 12
OMEGA = 1.0 / 0.8
SHAPE_FACTOR = 0.95
ORIENT_STEP = 4.0
PAIRS = [(0, 0), (1, 1), (2, 2), (0, 1), (0, 2), (1, 2)]
ENTRY = [[0, 3, 4], [3, 1, 5], [4, 5, 2]]
TOWARD = {
    0: [i for i in range(19) if VELOCITIES[i][0] == -1],
    1: [i for i in range(19) if VELOCITIES[i][0] == 1],
}
KNOWN = {0: [i for i in range(19) if VELOCITIES[i][0] != 1], 1: [i for i in range(19) if VELOCITIES[i][0] != -1]}
MSG_WIDE = 23
MSG_ROWS = 1072
HALO_AT = 928
SIDE_AT = 1024
CORNER_AT = 1056
MIB = 1024 * 1024
LIMIT_PACK = 5375 * MIB // 100
COST_PACK = pl.CostEstimate(flops=10**10, bytes_accessed=10**7, transcendentals=0)
LIMIT_WEIGHTS = 4900 * MIB // 100
STATE = 38


def opposite(i):
    return 0 if i == 0 else (i + 1 if i % 2 == 1 else i - 1)


def lanes_of():
    return lax.broadcasted_iota(jnp.int32, (8, 128), 1)


def rows_of():
    return lax.broadcasted_iota(jnp.int32, (8, 128), 0)


def roll(v, shift, axis):
    shift = shift % v.shape[axis]
    return v if shift == 0 else pltpu.roll(v, shift, axis)


def add_all(terms):
    while len(terms) > 1:
        terms = [
            terms[k] + terms[k + 1] if k + 1 < len(terms) else terms[k] for k in range(0, len(terms), 2)
        ]
    return terms[0]


def moments(f, numbers):
    rho = add_all([f[i] for i in numbers])
    mom = []
    for ax in range(3):
        pos = [f[i] for i in numbers if VELOCITIES[i][ax] > 0]
        neg = [f[i] for i in numbers if VELOCITIES[i][ax] < 0]
        total = add_all(pos) if pos else None
        if neg:
            total = add_all(neg) * -1.0 if total is None else total - add_all(neg)
        mom.append(total)
    return rho, mom


def relax(f, rho, u, numbers):
    usq = 1.0 - 1.5 * (u[0] * u[0] + u[1] * u[1] + u[2] * u[2])
    scaled = {w: (w * OMEGA) * rho for w in sorted(set(WEIGHTS[i] for i in numbers))}
    out = {}
    for i in numbers:
        proj = None
        for ax in range(3):
            c = VELOCITIES[i][ax]
            if c != 0:
                if proj is None:
                    proj = u[ax] if c > 0 else -u[ax]
                else:
                    proj = proj + u[ax] if c > 0 else proj - u[ax]
        poly = usq if proj is None else usq + proj * (3.0 + 4.5 * proj)
        out[i] = f[i] * (1.0 - OMEGA) + scaled[WEIGHTS[i]] * poly
    return out


def plus(a, b):
    if a is None:
        return b
    if b is None:
        return a
    return a + b


def minus(a, b):
    if b is None:
        return a
    if a is None:
        return -b
    return a - b


def times(a, b):
    return None if a is None or b is None else a * b


def jeffery(a, g):
    half = [[None if g[j][k] is None else 0.5 * g[j][k] for k in range(3)] for j in range(3)]
    d = [[plus(half[j][k], half[k][j]) if j <= k else None for k in range(3)] for j in range(3)]
    w = [[minus(half[j][k], half[k][j]) if j < k else None for k in range(3)] for j in range(3)]
    full = lambda j, k: a[ENTRY[j][k]]
    strain = lambda j, k: d[min(j, k)][max(j, k)]

    def spin(j, k):
        if j == k:
            return None
        if j < k:
            return w[j][k]
        return None if w[k][j] is None else -w[k][j]

    contraction = None
    for j in range(3):
        contraction = plus(contraction, times(full(j, j), strain(j, j)))
    for j, k in ((0, 1), (0, 2), (1, 2)):
        cross = times(full(j, k), strain(j, k))
        contraction = plus(contraction, None if cross is None else 2.0 * cross)
    twice = 2.0 * contraction
    mix = [[plus(spin(j, k), times(strain(j, k), SHAPE_FACTOR)) for k in range(3)] for j in range(3)]
    z = [[None] * 3 for _ in range(3)]
    for j in range(3):
        for k in range(3):
            for m in range(3):
                z[j][k] = plus(z[j][k], times(full(j, m), mix[m][k]))
    scaled = SHAPE_FACTOR * twice
    return [plus(z[j][k], z[k][j]) - scaled * full(j, k) for j, k in PAIRS]


def put(ref, at, r, v):
    if r < 4:
        ref[at + (pl.ds(16 + 8 * r, 8), slice(None))] = v
    else:
        ref[at + (pl.ds(8, 8), slice(None))] = v
        ref[at + (pl.ds(48, 8), slice(None))] = v


def get(ref, at, r, dy=0):
    if r < 4:
        return ref[at + (pl.ds(16 + 8 * r + dy, 8), slice(None))]
    if dy == 0:
        return ref[at + (pl.ds(48, 8), slice(None))]
    return jnp.where(
        rows_of() < 4,
        ref[at + (pl.ds(48 + dy, 8), slice(None))],
        ref[at + (pl.ds(8 + dy, 8), slice(None))],
    )


def pull_z(own, side, dz, want_side=True):
    if dz == 0:
        return own, side
    lane = lanes_of()
    own_r, side_r = roll(own, dz, 1), roll(side, dz, 1)
    edge = lane == (0 if dz > 0 else 127)
    return jnp.where(edge, side_r, own_r), jnp.where(edge, own_r, side_r) if want_side else None


def walls():
    layer = lax.axis_index("gz")
    last = lax.axis_size("gz") - 1
    lane = lanes_of()
    low = lane == jnp.where(layer == 0, 0, -1)
    high = lane == jnp.where(layer == last, 127, -1)
    return low, high


def wall_of(i, low, high):
    dz = VELOCITIES[i][2]
    return None if dz == 0 else (low if dz > 0 else high)


def stream(ref, at_of, i, r, low, high, reflected, want_side=True):
    _, cy, cz = VELOCITIES[i]
    own = get(ref, at_of(0), r, -cy)
    side = get(ref, at_of(1), r, -cy) if (want_side or cz != 0) else None
    if cz == 0:
        return own, side
    own, side = pull_z(own, side, cz, want_side)
    return jnp.where(wall_of(i, low, high), reflected(), own), side


def central(ref, at_of, r, axis, low, high, outside, want_side=True):
    if axis == 1:
        out = []
        for t in (0, 1) if want_side else (0,):
            out.append(0.5 * (get(ref, at_of(t), r, 1) - get(ref, at_of(t), r, -1)))
        return out
    own, side = get(ref, at_of(0), r), get(ref, at_of(1), r)
    behind, behind_side = pull_z(own, side, 1, want_side)
    ahead, ahead_side = pull_z(own, side, -1, want_side)
    past = own if outside else jnp.zeros_like(own)
    diff = 0.5 * (jnp.where(high, past, ahead) - jnp.where(low, past, behind))
    return [diff, 0.5 * (ahead_side - behind_side)] if want_side else [diff]


def fetch(pairs, sems):
    copies = [pltpu.make_async_copy(src, dst, sems.at[k]) for k, (src, dst) in enumerate(pairs)]
    for copy in copies:
        copy.start()
    return copies


def pack_z_kernel(pop_hbm, ori_hbm, zpack, low_rows, high_rows, pop, ori, sems):
    for copy in fetch([(pop_hbm, pop), (ori_hbm, ori)], sems):
        copy.wait()
    lane = lax.broadcasted_iota(jnp.int32, (32, 128), 1)
    tiles = [jnp.zeros((32, 128), jnp.float32), jnp.zeros((32, 128), jnp.float32)]
    for f in range(25):
        for x in range(2):
            s = 2 * f + x
            src = pop if f < 19 else ori
            k = f if f < 19 else f - 19
            v = src[k, x]
            at = 4 * (s % 32)
            tiles[s // 32] = jnp.where((lane >= at) & (lane < at + 4), roll(v, at + 2, 1), tiles[s // 32])
            low_rows[pl.ds(2 * s, 2), :] = src[k, x, 0:2, :]
            high_rows[pl.ds(2 * s, 2), :] = src[k, x, 30:32, :]
    zpack[0] = tiles[0]
    zpack[1] = tiles[1]
    low_rows[100:104, :] = jnp.zeros((4, 128), jnp.float32)
    high_rows[100:104, :] = jnp.zeros((4, 128), jnp.float32)


def own_kernel(pop, ori, after, own, token):
    token[...] = jnp.zeros(token.shape, jnp.float32)
    numbers = list(range(19))
    for x in range(2):
        for r in range(4):
            rows = pl.ds(8 * r, 8)
            f = [pop[i, x, rows, :] for i in numbers]
            rho, mom = moments(f, numbers)
            inv = 1.0 / rho
            u = [m * inv for m in mom]
            relaxed = relax(f, rho, u, numbers)
            for i in numbers:
                own[i, x, rows, :] = relaxed[i]
            for j in range(3):
                own[19 + j, x, rows, :] = u[j]
            for k in range(6):
                own[22 + k, x, rows, :] = ori[k, x, rows, :]


def pack_y_kernel(from_minus, from_plus, low_in, high_in, token, sides, low_rows, high_rows):
    lane = lax.broadcasted_iota(jnp.int32, (32, 128), 1)
    low_rows[...] = low_in[...]
    high_rows[...] = high_in[...]
    for t in range(2):
        both = jnp.where(lane % 4 < 2, from_minus[t], from_plus[t])
        sides[t] = both
        low_rows[pl.ds(100 + 2 * t, 2), :] = sides[t, 0:2, :]
        high_rows[pl.ds(100 + 2 * t, 2), :] = sides[t, 30:32, :]


def step_one_kernel(own, sides, from_yminus, from_yplus, state, msg_low, msg_high, halo, fields, out):
    low, high = walls()
    lane, row = lanes_of(), rows_of()
    for s in range(52):
        halo[s, 0:2, :] = from_yplus[pl.ds(2 * s, 2), :]
        halo[s, 6:8, :] = from_yminus[pl.ds(2 * s, 2), :]

    def raw(f, x, t, r):
        s = 2 * f + x
        if t == 0:
            return halo[s]
        packed = halo[50 + s // 32] if r == 4 else sides[s // 32, pl.ds(8 * r, 8), :]
        return roll(packed, -(4 * (s % 32) + 2), 1)

    numbers = list(range(19))
    for x in range(2):
        for t in range(2):
            for r in range(5):
                if t == 0 and r < 4:
                    for k in range(28):
                        put(fields, (k, x, t), r, own[k, x, pl.ds(8 * r, 8), :])
                    continue
                f = [raw(i, x, t, r) for i in numbers]
                rho, mom = moments(f, numbers)
                inv = 1.0 / rho
                u = [m * inv for m in mom]
                relaxed = relax(f, rho, u, numbers)
                for i in numbers:
                    put(fields, (i, x, t), r, relaxed[i])
                for j in range(3):
                    put(fields, (19 + j, x, t), r, u[j])
                for k in range(6):
                    put(fields, (22 + k, x, t), r, raw(19 + k, x, t, r))

    for x in range(2):
        for r in range(5):
            place = lambda f, xs=x: (lambda t: (f, xs, t))
            known = [{}, {}]
            for i in KNOWN[x]:
                xs = x - VELOCITIES[i][0]
                pair = stream(
                    fields, place(i, xs), i, r, low, high, lambda i=i: get(fields, (opposite(i), x, 0), r)
                )
                known[0][i], known[1][i] = pair
            grad = [[[None] * 3 for _ in range(3)] for _ in range(2)]
            sign = 0.5 if x == 0 else -0.5
            for j in range(3):
                by_y = central(fields, place(19 + j), r, 1, low, high, False)
                by_z = central(fields, place(19 + j), r, 2, low, high, False)
                for t in range(2):
                    grad[t][j][0] = sign * get(fields, (19 + j, 1 - x, t), r)
                    grad[t][j][1] = by_y[t]
                    grad[t][j][2] = by_z[t]
            u = [[get(fields, (19 + j, x, t), r) for j in range(3)] for t in range(2)]
            a = [[get(fields, (22 + k, x, t), r) for k in range(6)] for t in range(2)]
            advect = [[], []]
            for k in range(6):
                by_y = central(fields, place(22 + k), r, 1, low, high, True)
                by_z = central(fields, place(22 + k), r, 2, low, high, True)
                for t in range(2):
                    by_x = sign * get(fields, (22 + k, 1 - x, t), r)
                    advect[t].append(u[t][0] * by_x + u[t][1] * by_y[t] + u[t][2] * by_z[t])
            side_pack = jnp.zeros((8, 128), jnp.float32)
            for t in range(2):
                rate = jeffery(a[t], grad[t])
                part = [a[t][k] + ORIENT_STEP * (rate[k] - advect[t][k]) for k in range(6)]
                rho, mom = moments(known[t], KNOWN[x])
                outward = [get(fields, (i, x, t), r) for i in TOWARD[x]]
                keep = [known[t][i] for i in KNOWN[x]] + [rho] + mom + part + u[t] + a[t] + outward
                for k in range(STATE):
                    state[x, k, t, pl.ds(8 * r, 8), :] = keep[k]
                wide = outward + u[t] + a[t] + [rho] + mom + [known[t][i] for i in TOWARD[x]]
                if t == 1:
                    for k in range(MSG_WIDE):
                        at = 4 * k
                        side_pack = jnp.where((lane >= at) & (lane < at + 4), roll(wide[k], at + 2, 1), side_pack)
                elif r < 4:
                    for k, v in enumerate(wide + part):
                        out[x, pl.ds(32 * k + 8 * r, 8), :] = v
                else:
                    inner = (row >= 2) & (row < 6)
                    for k in range(0, MSG_WIDE, 2):
                        v = wide[k]
                        if k + 1 < MSG_WIDE:
                            v = jnp.where(inner, roll(wide[k + 1], 4, 0), v)
                        out[x, pl.ds(HALO_AT + 4 * k, 8), :] = v
            out[x, pl.ds(SIDE_AT + 8 * r if r < 4 else CORNER_AT, 8), :] = side_pack
    for x in range(2):
        out[x, pl.ds(CORNER_AT + 8, 8), :] = jnp.zeros((8, 128), jnp.float32)
    msg_low[...] = out[0].astype(jnp.bfloat16)
    msg_high[...] = out[1].astype(jnp.bfloat16)


def weights_kernel(
    w_in_hbm, b_in_hbm, w_mid_hbm, b_mid_hbm, w_out_hbm, b_out_hbm, w_one, w_two, bias_mid, w_three, bias_out,
    w_in, b_in, w_mid, b_mid, b_out, wide, sems,
):
    pairs = [
        (w_mid_hbm, w_mid),
        (w_in_hbm, w_in),
        (b_in_hbm, b_in),
        (b_mid_hbm, b_mid),
        (b_out_hbm, b_out),
        (w_out_hbm, w_three),
    ]
    for copy in fetch(pairs, sems):
        copy.wait()
    f32, bf16 = jnp.float32, jnp.bfloat16
    row = lax.broadcasted_iota(jnp.int32, (8, 512), 0)
    bias = jnp.broadcast_to(0.5 * b_in[...], (8, 512))
    first = bias.astype(bf16).astype(f32)
    rest = bias - first
    padded = jnp.concatenate([0.5 * w_in[...].astype(f32), jnp.zeros((2, 512), f32)], axis=0)
    stacked = jnp.where(row == 6, first, jnp.where(row == 7, rest, padded))
    w_one[...] = stacked.T.astype(bf16)
    w_two[...] = (0.5 * w_mid[...].astype(f32)).T.astype(bf16)
    bias_mid[...] = jnp.broadcast_to(jnp.broadcast_to(0.5 * b_mid[...], (8, 512)).T[:, 0:1], (512, 128))
    wide[...] = jnp.zeros(wide.shape, f32)
    wide[:, 0:15] = jnp.broadcast_to(b_out[...], (8, 15))
    bias_out[...] = jnp.broadcast_to(wide[...].T[0:16, 0:1], (16, 128))


def step_two_kernel(
    slots, state, from_low, from_high, w_one, w_mid, b_mid, w_out, b_out, flow, closure,
    got, fields, near, level, feats, spread, place,
):
    low, high = walls()
    got[0] = from_low[...].astype(jnp.float32)
    got[1] = from_high[...].astype(jnp.float32)
    for s in range(17):
        place[s] = 64
    for b in range(64):
        s = slots[b // 32, 0, b % 32]
        place[jnp.where(s >= 0, s, 16)] = b

    def arrived(x, k, t, r):
        if t == 0 and r < 4:
            return got[x, pl.ds(32 * k + 8 * r, 8), :]
        if t == 0:
            v = got[x, pl.ds(HALO_AT + 8 * (k // 2), 8), :]
            return roll(v, 4, 0) if k % 2 else v
        v = got[x, pl.ds(SIDE_AT + 8 * r if r < 4 else CORNER_AT, 8), :]
        return roll(v, -(4 * k + 2), 1)

    kept = lambda x, k, t, r: state[x, k, t, pl.ds(8 * r, 8), :]
    for x in range(2):
        for t in range(2):
            for r in range(5):
                for k in range(5):
                    put(near, (x, k, t), r, arrived(x, k, t, r))
                    put(near, (x, 5 + k, t), r, kept(x, 33 + k, t, r))
    numbers = list(range(19))
    for x in range(2):
        come = TOWARD[1 - x]
        go = TOWARD[x]
        sign = -0.5 if x == 0 else 0.5
        for r in range(5):
            come_f, go_f = [{}, {}], [{}, {}]
            for k, i in enumerate(come):
                back = go.index(opposite(i))
                pair = stream(
                    near, lambda t, k=k: (x, k, t), i, r, low, high,
                    lambda back=back: get(near, (x, 5 + back, 0), r),
                )
                come_f[0][i], come_f[1][i] = pair
            for k, i in enumerate(go):
                back = come.index(opposite(i))
                pair = stream(
                    near, lambda t, k=k: (x, 5 + k, t), i, r, low, high,
                    lambda back=back: get(near, (x, back, 0), r),
                )
                go_f[0][i], go_f[1][i] = pair
            for t in range(2):
                f = {i: kept(x, k, t, r) for k, i in enumerate(KNOWN[x])}
                f.update(come_f[t])
                rho_new, mom_new = moments(come_f[t], come)
                rho = kept(x, 14, t, r) + rho_new
                mom = [kept(x, 15 + j, t, r) + mom_new[j] for j in range(3)]
                inv = 1.0 / rho
                u = [m * inv for m in mom]
                relaxed = relax(f, rho, u, numbers)
                for i in numbers:
                    put(fields, (i, x, t), r, relaxed[i])
                for j in range(3):
                    put(fields, (19 + j, x, t), r, u[j])
                u0 = [kept(x, 24 + j, t, r) for j in range(3)]
                a0 = [kept(x, 27 + k, t, r) for k in range(6)]
                u0n = [arrived(x, 5 + j, t, r) for j in range(3)]
                a0n = [arrived(x, 8 + k, t, r) for k in range(6)]
                rate = jeffery(a0, [[sign * u0n[j], None, None] for j in range(3)])
                drift = (sign * u0[0])
                for k in range(6):
                    a1 = kept(x, 18 + k, t, r) + ORIENT_STEP * (rate[k] - drift * a0n[k])
                    put(fields, (22 + k, x, t), r, a1)
                rho_new, mom_new = moments(go_f[t], go)
                rho = arrived(x, 14, t, r) + rho_new
                inv = 1.0 / rho
                u = [(arrived(x, 15 + j, t, r) + mom_new[j]) * inv for j in range(3)]
                f = {i: arrived(x, 18 + k, t, r) for k, i in enumerate(come)}
                relaxed = relax(f, rho, u, come)
                for k, i in enumerate(come):
                    put(fields, (28 + k, x, t), r, relaxed[i])
                if t == 0 and r < 4:
                    rate = jeffery(a0n, [[-sign * u0[j], None, None] for j in range(3)])
                    drift = -sign * u0n[0]
                    for j in range(3):
                        level[x, j, pl.ds(8 * r, 8), :] = u[j]
                    for k in range(6):
                        a1 = arrived(x, 23 + k, t, r) + ORIENT_STEP * (rate[k] - drift * a0[k])
                        level[x, 3 + k, pl.ds(8 * r, 8), :] = a1

    feats[...] = jnp.ones(feats.shape, jnp.float32)
    for x in range(2):
        for r in range(4):
            f = {}
            for i in numbers:
                xs = x - VELOCITIES[i][0]
                if 0 <= xs <= 1:
                    at_of = lambda t, i=i, xs=xs: (i, xs, t)
                else:
                    k = TOWARD[1 - x].index(i)
                    at_of = lambda t, k=k: (28 + k, x, t)
                f[i], _ = stream(
                    fields, at_of, i, r, low, high, lambda i=i: get(fields, (opposite(i), x, 0), r), False
                )
            rho, mom = moments(f, numbers)
            inv = 1.0 / rho
            final = [rho] + [m * inv for m in mom]
            for k in range(4):
                spread[pl.ds(k * 64 + x * 32 + 8 * r, 8), :] = final[k]
            sign = -0.5 if x == 0 else 0.5
            by_x = lambda k, n: sign * (level[x, n, pl.ds(8 * r, 8), :] - get(fields, (k, 1 - x, 0), r))
            grad = [[None] * 3 for _ in range(3)]
            for j in range(3):
                place_u = lambda t, j=j: (19 + j, x, t)
                grad[j][0] = by_x(19 + j, j)
                grad[j][1] = central(fields, place_u, r, 1, low, high, False, False)[0]
                grad[j][2] = central(fields, place_u, r, 2, low, high, False, False)[0]
            u = [get(fields, (19 + j, x, 0), r) for j in range(3)]
            a = [get(fields, (22 + k, x, 0), r) for k in range(6)]
            rate = jeffery(a, grad)
            for k in range(6):
                place_a = lambda t, k=k: (22 + k, x, t)
                advect = (
                    u[0] * by_x(22 + k, 3 + k)
                    + u[1] * central(fields, place_a, r, 1, low, high, True, False)[0]
                    + u[2] * central(fields, place_a, r, 2, low, high, True, False)[0]
                )
                new = a[k] + ORIENT_STEP * (rate[k] - advect)
                feats[pl.ds((x * 32 + 8 * r) * 8 + k, 8, 8), :] = new
    for k in range(4):
        for x in range(2):
            flow[k, x] = spread[pl.ds(k * 64 + x * 32, 32), :].astype(jnp.bfloat16)

    spread[...] = jnp.zeros(spread.shape, jnp.float32)
    group = 8
    bias_mid = jnp.concatenate([b_mid[...]] * group, axis=1)
    for g in range(16 // group):
        at = [place[g * group + k] for k in range(group)]
        cells = [feats[pl.ds(pl.multiple_of(b * 8, 8), 8), :] for b in at]
        cells = jnp.concatenate(cells, axis=1).astype(jnp.bfloat16)
        v = jnp.dot(w_one[...], cells, preferred_element_type=jnp.float32)
        h = (v + v * jnp.tanh(v)).astype(jnp.bfloat16)
        v = jnp.dot(w_mid[...], h, preferred_element_type=jnp.float32) + bias_mid
        h = (v + v * jnp.tanh(v)).astype(jnp.bfloat16)
        v = jnp.dot(w_out[...], h, preferred_element_type=jnp.float32)
        for k in range(group):
            spread[pl.ds(pl.multiple_of(at[k] * 16, 16), 15), :] = v[:, 128 * k : 128 * k + 128] + b_out[0:15, :]
    for c in range(15):
        for x in range(2):
            closure[c, x] = spread[pl.ds(x * 512 + c, 32, 16), :].astype(jnp.bfloat16)


def local(populations, orientation, slot_table, w_in, b_in, w_mid, b_mid, w_out, b_out):
    f32, bf16 = jnp.float32, jnp.bfloat16
    shape = lambda *s, d=f32: jax.ShapeDtypeStruct(s, d)
    vmem = pl.BlockSpec(memory_space=pltpu.VMEM)
    smem = pl.BlockSpec(memory_space=pltpu.SMEM)
    params = pltpu.CompilerParams(vmem_limit_bytes=48 * 1024 * 1024)

    def ring(axis, step, wrap):
        n = lax.axis_size(axis)
        return [(i, (i + step) % n) for i in range(n) if wrap or 0 <= i + step < n]

    hbm = pl.BlockSpec(memory_space=pltpu.HBM)
    slots = jnp.transpose(slot_table, (0, 2, 1))
    w_one, w_two, bias_mid, w_three, bias_out = pl.pallas_call(
        weights_kernel,
        out_shape=(
            shape(512, 8, d=bf16),
            shape(512, 512, d=bf16),
            shape(512, 128),
            shape(15, 512, d=bf16),
            shape(16, 128),
        ),
        in_specs=[hbm] * 6,
        out_specs=(vmem,) * 5,
        scratch_shapes=[
            pltpu.VMEM((6, 512), bf16),
            pltpu.VMEM((1, 512), f32),
            pltpu.VMEM((512, 512), bf16),
            pltpu.VMEM((1, 512), f32),
            pltpu.VMEM((1, 15), f32),
            pltpu.VMEM((8, 128), f32),
            pltpu.SemaphoreType.DMA((6,)),
        ],
        compiler_params=pltpu.CompilerParams(vmem_limit_bytes=LIMIT_WEIGHTS),
    )(w_in, b_in.reshape(1, 512), w_mid, b_mid.reshape(1, 512), w_out.T, b_out.reshape(1, 15))
    zpack, low_raw, high_raw = pl.pallas_call(
        pack_z_kernel,
        out_shape=(shape(2, 32, 128), shape(104, 128), shape(104, 128)),
        in_specs=[hbm] * 2,
        out_specs=(vmem,) * 3,
        scratch_shapes=[
            pltpu.VMEM((19, 2, 32, 128), f32),
            pltpu.VMEM((6, 2, 32, 128), f32),
            pltpu.SemaphoreType.DMA((2,)),
        ],
        compiler_params=pltpu.CompilerParams(vmem_limit_bytes=LIMIT_PACK),
        cost_estimate=COST_PACK,
    )(populations, orientation)
    own, token = pl.pallas_call(
        own_kernel,
        out_shape=(shape(28, 2, 32, 128), shape(8, 128)),
        in_specs=[vmem] * 3,
        out_specs=(vmem,) * 2,
        compiler_params=params,
    )(populations, orientation, zpack)
    from_minus = lax.ppermute(zpack, "gz", ring("gz", 1, False))
    from_plus = lax.ppermute(zpack, "gz", ring("gz", -1, False))
    sides, low_rows, high_rows = pl.pallas_call(
        pack_y_kernel,
        out_shape=(shape(2, 32, 128), shape(104, 128), shape(104, 128)),
        in_specs=[vmem] * 5,
        out_specs=(vmem,) * 3,
        compiler_params=params,
    )(from_minus, from_plus, low_raw, high_raw, token)
    from_yminus = lax.ppermute(high_rows, "gy", ring("gy", 1, True))
    from_yplus = lax.ppermute(low_rows, "gy", ring("gy", -1, True))
    state, msg_low, msg_high = pl.pallas_call(
        step_one_kernel,
        out_shape=(
            shape(2, STATE, 2, 40, 128),
            shape(MSG_ROWS, 128, d=bf16),
            shape(MSG_ROWS, 128, d=bf16),
        ),
        in_specs=[vmem] * 4,
        out_specs=(vmem,) * 3,
        scratch_shapes=[
            pltpu.VMEM((52, 8, 128), f32),
            pltpu.VMEM((28, 2, 2, 64, 128), f32),
            pltpu.VMEM((2, MSG_ROWS, 128), f32),
        ],
        compiler_params=params,
    )(own, sides, from_yminus, from_yplus)
    from_low = lax.ppermute(msg_high, "gx", ring("gx", 1, True))
    from_high = lax.ppermute(msg_low, "gx", ring("gx", -1, True))
    return pl.pallas_call(
        step_two_kernel,
        out_shape=(shape(4, 2, 32, 128, d=bf16), shape(15, 2, 32, 128, d=bf16)),
        in_specs=[smem] + [vmem] * 8,
        out_specs=(vmem,) * 2,
        scratch_shapes=[
            pltpu.VMEM((2, MSG_ROWS, 128), f32),
            pltpu.VMEM((33, 2, 2, 64, 128), f32),
            pltpu.VMEM((2, 10, 2, 64, 128), f32),
            pltpu.VMEM((2, 9, 32, 128), f32),
            pltpu.VMEM((65 * 8, 128), f32),
            pltpu.VMEM((65 * 16, 128), f32),
            pltpu.SMEM((17,), jnp.int32),
        ],
        compiler_params=params,
    )(slots, state, from_low, from_high, w_one, w_two, bias_mid, w_three, bias_out)


def solution(mesh):
    grid = P(None, "gx", "gy", "gz")
    in_specs = (grid, grid, P("gx", "gy", "gz"), P(), P(), P(), P(), P(), P())
    return jax.shard_map(local, mesh=mesh, in_specs=in_specs, out_specs=(grid, grid), check_vma=False)
```

```python
import functools

import jax
import jax.numpy as jnp
from jax import lax
from jax.experimental import pallas as pl
from jax.experimental.pallas import tpu as pltpu
from jax.sharding import PartitionSpec as P


VELOCITIES = [
    (0, 0, 0),
    (1, 0, 0),
    (-1, 0, 0),
    (0, 1, 0),
    (0, -1, 0),
    (0, 0, 1),
    (0, 0, -1),
    (1, 1, 0),
    (-1, -1, 0),
    (1, -1, 0),
    (-1, 1, 0),
    (1, 0, 1),
    (-1, 0, -1),
    (1, 0, -1),
    (-1, 0, 1),
    (0, 1, 1),
    (0, -1, -1),
    (0, 1, -1),
    (0, -1, 1),
]
WEIGHTS = [1.0 / 3.0] + [1.0 / 18.0] * 6 + [1.0 / 36.0] * 12
OMEGA = 1.0 / 0.8
SHAPE_FACTOR = 0.95
ORIENT_STEP = 4.0
PAIRS = [(0, 0), (1, 1), (2, 2), (0, 1), (0, 2), (1, 2)]
ENTRY = [[0, 3, 4], [3, 1, 5], [4, 5, 2]]
TOWARD = {
    0: [i for i in range(19) if VELOCITIES[i][0] == -1],
    1: [i for i in range(19) if VELOCITIES[i][0] == 1],
}
KNOWN = {0: [i for i in range(19) if VELOCITIES[i][0] != 1], 1: [i for i in range(19) if VELOCITIES[i][0] != -1]}
MSG_WIDE = 23
MSG_ROWS = 1072
HALO_AT = 928
SIDE_AT = 1024
CORNER_AT = 1056
MIB = 1024 * 1024
LIMIT_PACK = 5375 * MIB // 100
COST_PACK = pl.CostEstimate(flops=10**10, bytes_accessed=10**7, transcendentals=0)
LIMIT_WEIGHTS = 4900 * MIB // 100
STATE = 38


def opposite(i):
    return 0 if i == 0 else (i + 1 if i % 2 == 1 else i - 1)


def lanes_of():
    return lax.broadcasted_iota(jnp.int32, (8, 128), 1)


def rows_of():
    return lax.broadcasted_iota(jnp.int32, (8, 128), 0)


def roll(v, shift, axis):
    shift = shift % v.shape[axis]
    return v if shift == 0 else pltpu.roll(v, shift, axis)


def add_all(terms):
    while len(terms) > 1:
        terms = [
            terms[k] + terms[k + 1] if k + 1 < len(terms) else terms[k] for k in range(0, len(terms), 2)
        ]
    return terms[0]


def moments(f, numbers):
    rho = add_all([f[i] for i in numbers])
    mom = []
    for ax in range(3):
        pos = [f[i] for i in numbers if VELOCITIES[i][ax] > 0]
        neg = [f[i] for i in numbers if VELOCITIES[i][ax] < 0]
        total = add_all(pos) if pos else None
        if neg:
            total = add_all(neg) * -1.0 if total is None else total - add_all(neg)
        mom.append(total)
    return rho, mom


def relax(f, rho, u, numbers):
    usq = 1.0 - 1.5 * (u[0] * u[0] + u[1] * u[1] + u[2] * u[2])
    scaled = {w: (w * OMEGA) * rho for w in sorted(set(WEIGHTS[i] for i in numbers))}
    out = {}
    for i in numbers:
        proj = None
        for ax in range(3):
            c = VELOCITIES[i][ax]
            if c != 0:
                if proj is None:
                    proj = u[ax] if c > 0 else -u[ax]
                else:
                    proj = proj + u[ax] if c > 0 else proj - u[ax]
        poly = usq if proj is None else usq + proj * (3.0 + 4.5 * proj)
        out[i] = f[i] * (1.0 - OMEGA) + scaled[WEIGHTS[i]] * poly
    return out


def plus(a, b):
    if a is None:
        return b
    if b is None:
        return a
    return a + b


def minus(a, b):
    if b is None:
        return a
    if a is None:
        return -b
    return a - b


def times(a, b):
    return None if a is None or b is None else a * b


def jeffery(a, g):
    half = [[None if g[j][k] is None else 0.5 * g[j][k] for k in range(3)] for j in range(3)]
    d = [[plus(half[j][k], half[k][j]) if j <= k else None for k in range(3)] for j in range(3)]
    w = [[minus(half[j][k], half[k][j]) if j < k else None for k in range(3)] for j in range(3)]
    full = lambda j, k: a[ENTRY[j][k]]
    strain = lambda j, k: d[min(j, k)][max(j, k)]

    def spin(j, k):
        if j == k:
            return None
        if j < k:
            return w[j][k]
        return None if w[k][j] is None else -w[k][j]

    contraction = None
    for j in range(3):
        contraction = plus(contraction, times(full(j, j), strain(j, j)))
    for j, k in ((0, 1), (0, 2), (1, 2)):
        cross = times(full(j, k), strain(j, k))
        contraction = plus(contraction, None if cross is None else 2.0 * cross)
    twice = 2.0 * contraction
    mix = [[plus(spin(j, k), times(strain(j, k), SHAPE_FACTOR)) for k in range(3)] for j in range(3)]
    z = [[None] * 3 for _ in range(3)]
    for j in range(3):
        for k in range(3):
            for m in range(3):
                z[j][k] = plus(z[j][k], times(full(j, m), mix[m][k]))
    scaled = SHAPE_FACTOR * twice
    return [plus(z[j][k], z[k][j]) - scaled * full(j, k) for j, k in PAIRS]


def put(ref, at, r, v):
    if r < 4:
        ref[at + (pl.ds(16 + 8 * r, 8), slice(None))] = v
    else:
        ref[at + (pl.ds(8, 8), slice(None))] = v
        ref[at + (pl.ds(48, 8), slice(None))] = v


def get(ref, at, r, dy=0):
    if r < 4:
        return ref[at + (pl.ds(16 + 8 * r + dy, 8), slice(None))]
    if dy == 0:
        return ref[at + (pl.ds(48, 8), slice(None))]
    return jnp.where(
        rows_of() < 4,
        ref[at + (pl.ds(48 + dy, 8), slice(None))],
        ref[at + (pl.ds(8 + dy, 8), slice(None))],
    )


def pull_z(own, side, dz, want_side=True):
    if dz == 0:
        return own, side
    lane = lanes_of()
    own_r, side_r = roll(own, dz, 1), roll(side, dz, 1)
    edge = lane == (0 if dz > 0 else 127)
    return jnp.where(edge, side_r, own_r), jnp.where(edge, own_r, side_r) if want_side else None


def walls():
    layer = lax.axis_index("gz")
    last = lax.axis_size("gz") - 1
    lane = lanes_of()
    low = lane == jnp.where(layer == 0, 0, -1)
    high = lane == jnp.where(layer == last, 127, -1)
    return low, high


def wall_of(i, low, high):
    dz = VELOCITIES[i][2]
    return None if dz == 0 else (low if dz > 0 else high)


def stream(ref, at_of, i, r, low, high, reflected, want_side=True):
    _, cy, cz = VELOCITIES[i]
    own = get(ref, at_of(0), r, -cy)
    side = get(ref, at_of(1), r, -cy) if (want_side or cz != 0) else None
    if cz == 0:
        return own, side
    own, side = pull_z(own, side, cz, want_side)
    return jnp.where(wall_of(i, low, high), reflected(), own), side


def central(ref, at_of, r, axis, low, high, outside, want_side=True):
    if axis == 1:
        out = []
        for t in (0, 1) if want_side else (0,):
            out.append(0.5 * (get(ref, at_of(t), r, 1) - get(ref, at_of(t), r, -1)))
        return out
    own, side = get(ref, at_of(0), r), get(ref, at_of(1), r)
    behind, behind_side = pull_z(own, side, 1, want_side)
    ahead, ahead_side = pull_z(own, side, -1, want_side)
    past = own if outside else jnp.zeros_like(own)
    diff = 0.5 * (jnp.where(high, past, ahead) - jnp.where(low, past, behind))
    return [diff, 0.5 * (ahead_side - behind_side)] if want_side else [diff]


def fetch(pairs, sems):
    copies = [pltpu.make_async_copy(src, dst, sems.at[k]) for k, (src, dst) in enumerate(pairs)]
    for copy in copies:
        copy.start()
    return copies


def pack_z_kernel(pop_hbm, ori_hbm, zpack, low_rows, high_rows, pop, ori, sems):
    for copy in fetch([(pop_hbm, pop), (ori_hbm, ori)], sems):
        copy.wait()
    lane = lax.broadcasted_iota(jnp.int32, (32, 128), 1)
    tiles = [jnp.zeros((32, 128), jnp.float32), jnp.zeros((32, 128), jnp.float32)]
    for f in range(25):
        for x in range(2):
            s = 2 * f + x
            src = pop if f < 19 else ori
            k = f if f < 19 else f - 19
            v = src[k, x]
            at = 4 * (s % 32)
            tiles[s // 32] = jnp.where((lane >= at) & (lane < at + 4), roll(v, at + 2, 1), tiles[s // 32])
            low_rows[pl.ds(2 * s, 2), :] = src[k, x, 0:2, :]
            high_rows[pl.ds(2 * s, 2), :] = src[k, x, 30:32, :]
    zpack[0] = tiles[0]
    zpack[1] = tiles[1]
    low_rows[100:104, :] = jnp.zeros((4, 128), jnp.float32)
    high_rows[100:104, :] = jnp.zeros((4, 128), jnp.float32)


def own_kernel(pop, ori, after, own, token):
    token[...] = jnp.zeros(token.shape, jnp.float32)
    numbers = list(range(19))
    for x in range(2):
        for r in range(4):
            rows = pl.ds(8 * r, 8)
            f = [pop[i, x, rows, :] for i in numbers]
            rho, mom = moments(f, numbers)
            inv = 1.0 / rho
            u = [m * inv for m in mom]
            relaxed = relax(f, rho, u, numbers)
            for i in numbers:
                own[i, x, rows, :] = relaxed[i]
            for j in range(3):
                own[19 + j, x, rows, :] = u[j]
            for k in range(6):
                own[22 + k, x, rows, :] = ori[k, x, rows, :]


def pack_y_kernel(from_minus, from_plus, low_in, high_in, token, sides, low_rows, high_rows):
    lane = lax.broadcasted_iota(jnp.int32, (32, 128), 1)
    low_rows[...] = low_in[...]
    high_rows[...] = high_in[...]
    for t in range(2):
        both = jnp.where(lane % 4 < 2, from_minus[t], from_plus[t])
        sides[t] = both
        low_rows[pl.ds(100 + 2 * t, 2), :] = sides[t, 0:2, :]
        high_rows[pl.ds(100 + 2 * t, 2), :] = sides[t, 30:32, :]


def step_one_kernel(own, sides, from_yminus, from_yplus, state, msg_off, msg_on, halo, fields, out):
    low, high = walls()
    lane, row = lanes_of(), rows_of()
    for s in range(52):
        halo[s, 0:2, :] = from_yplus[pl.ds(2 * s, 2), :]
        halo[s, 6:8, :] = from_yminus[pl.ds(2 * s, 2), :]

    def raw(f, x, t, r):
        s = 2 * f + x
        if t == 0:
            return halo[s]
        packed = halo[50 + s // 32] if r == 4 else sides[s // 32, pl.ds(8 * r, 8), :]
        return roll(packed, -(4 * (s % 32) + 2), 1)

    numbers = list(range(19))
    for x in range(2):
        for t in range(2):
            for r in range(5):
                if t == 0 and r < 4:
                    for k in range(28):
                        put(fields, (k, x, t), r, own[k, x, pl.ds(8 * r, 8), :])
                    continue
                f = [raw(i, x, t, r) for i in numbers]
                rho, mom = moments(f, numbers)
                inv = 1.0 / rho
                u = [m * inv for m in mom]
                relaxed = relax(f, rho, u, numbers)
                for i in numbers:
                    put(fields, (i, x, t), r, relaxed[i])
                for j in range(3):
                    put(fields, (19 + j, x, t), r, u[j])
                for k in range(6):
                    put(fields, (22 + k, x, t), r, raw(19 + k, x, t, r))

    for x in range(2):
        for r in range(5):
            place = lambda f, xs=x: (lambda t: (f, xs, t))
            known = [{}, {}]
            for i in KNOWN[x]:
                xs = x - VELOCITIES[i][0]
                pair = stream(
                    fields, place(i, xs), i, r, low, high, lambda i=i: get(fields, (opposite(i), x, 0), r)
                )
                known[0][i], known[1][i] = pair
            grad = [[[None] * 3 for _ in range(3)] for _ in range(2)]
            sign = 0.5 if x == 0 else -0.5
            for j in range(3):
                by_y = central(fields, place(19 + j), r, 1, low, high, False)
                by_z = central(fields, place(19 + j), r, 2, low, high, False)
                for t in range(2):
                    grad[t][j][0] = sign * get(fields, (19 + j, 1 - x, t), r)
                    grad[t][j][1] = by_y[t]
                    grad[t][j][2] = by_z[t]
            u = [[get(fields, (19 + j, x, t), r) for j in range(3)] for t in range(2)]
            a = [[get(fields, (22 + k, x, t), r) for k in range(6)] for t in range(2)]
            advect = [[], []]
            for k in range(6):
                by_y = central(fields, place(22 + k), r, 1, low, high, True)
                by_z = central(fields, place(22 + k), r, 2, low, high, True)
                for t in range(2):
                    by_x = sign * get(fields, (22 + k, 1 - x, t), r)
                    advect[t].append(u[t][0] * by_x + u[t][1] * by_y[t] + u[t][2] * by_z[t])
            side_pack = jnp.zeros((8, 128), jnp.float32)
            for t in range(2):
                rate = jeffery(a[t], grad[t])
                part = [a[t][k] + ORIENT_STEP * (rate[k] - advect[t][k]) for k in range(6)]
                rho, mom = moments(known[t], KNOWN[x])
                outward = [get(fields, (i, x, t), r) for i in TOWARD[x]]
                keep = [known[t][i] for i in KNOWN[x]] + [rho] + mom + part + u[t] + a[t] + outward
                for k in range(STATE):
                    state[x, k, t, pl.ds(8 * r, 8), :] = keep[k]
                wide = outward + u[t] + a[t] + [rho] + mom + [known[t][i] for i in TOWARD[x]]
                if t == 1:
                    for k in range(MSG_WIDE):
                        at = 4 * k
                        side_pack = jnp.where((lane >= at) & (lane < at + 4), roll(wide[k], at + 2, 1), side_pack)
                elif r < 4:
                    for k, v in enumerate(wide + part):
                        out[x, pl.ds(32 * k + 8 * r, 8), :] = v
                else:
                    inner = (row >= 2) & (row < 6)
                    for k in range(0, MSG_WIDE, 2):
                        v = wide[k]
                        if k + 1 < MSG_WIDE:
                            v = jnp.where(inner, roll(wide[k + 1], 4, 0), v)
                        out[x, pl.ds(HALO_AT + 4 * k, 8), :] = v
            out[x, pl.ds(SIDE_AT + 8 * r if r < 4 else CORNER_AT, 8), :] = side_pack
    for x in range(2):
        out[x, pl.ds(CORNER_AT + 8, 8), :] = jnp.zeros((8, 128), jnp.float32)
    odd = lax.axis_index("gx") % 2
    msg_off[...] = out[odd].astype(jnp.bfloat16)
    msg_on[...] = out[1 - odd].astype(jnp.bfloat16)


def weights_kernel(
    w_in_hbm, b_in_hbm, w_mid_hbm, b_mid_hbm, w_out_hbm, b_out_hbm, w_one, w_two, bias_mid, w_three, bias_out,
    w_in, b_in, w_mid, b_mid, b_out, wide, sems,
):
    pairs = [
        (w_mid_hbm, w_mid),
        (w_in_hbm, w_in),
        (b_in_hbm, b_in),
        (b_mid_hbm, b_mid),
        (b_out_hbm, b_out),
        (w_out_hbm, w_three),
    ]
    for copy in fetch(pairs, sems):
        copy.wait()
    f32, bf16 = jnp.float32, jnp.bfloat16
    row = lax.broadcasted_iota(jnp.int32, (8, 512), 0)
    bias = jnp.broadcast_to(0.5 * b_in[...], (8, 512))
    first = bias.astype(bf16).astype(f32)
    rest = bias - first
    padded = jnp.concatenate([0.5 * w_in[...].astype(f32), jnp.zeros((2, 512), f32)], axis=0)
    stacked = jnp.where(row == 6, first, jnp.where(row == 7, rest, padded))
    w_one[...] = stacked.T.astype(bf16)
    w_two[...] = (0.5 * w_mid[...].astype(f32)).T.astype(bf16)
    bias_mid[...] = jnp.broadcast_to(jnp.broadcast_to(0.5 * b_mid[...], (8, 512)).T[:, 0:1], (512, 128))
    wide[...] = jnp.zeros(wide.shape, f32)
    wide[:, 0:15] = jnp.broadcast_to(b_out[...], (8, 15))
    bias_out[...] = jnp.broadcast_to(wide[...].T[0:16, 0:1], (16, 128))


def step_two_kernel(
    slots, state, from_off, from_on, w_one, w_mid, b_mid, w_out, b_out, flow, closure,
    got, fields, near, level, feats, spread, place,
):
    low, high = walls()
    odd = lax.axis_index("gx") % 2
    got[odd] = from_off[...].astype(jnp.float32)
    got[1 - odd] = from_on[...].astype(jnp.float32)
    for s in range(17):
        place[s] = 64
    for b in range(64):
        s = slots[b // 32, 0, b % 32]
        place[jnp.where(s >= 0, s, 16)] = b

    def arrived(x, k, t, r):
        if t == 0 and r < 4:
            return got[x, pl.ds(32 * k + 8 * r, 8), :]
        if t == 0:
            v = got[x, pl.ds(HALO_AT + 8 * (k // 2), 8), :]
            return roll(v, 4, 0) if k % 2 else v
        v = got[x, pl.ds(SIDE_AT + 8 * r if r < 4 else CORNER_AT, 8), :]
        return roll(v, -(4 * k + 2), 1)

    kept = lambda x, k, t, r: state[x, k, t, pl.ds(8 * r, 8), :]
    for x in range(2):
        for t in range(2):
            for r in range(5):
                for k in range(5):
                    put(near, (x, k, t), r, arrived(x, k, t, r))
                    put(near, (x, 5 + k, t), r, kept(x, 33 + k, t, r))
    numbers = list(range(19))
    for x in range(2):
        come = TOWARD[1 - x]
        go = TOWARD[x]
        sign = -0.5 if x == 0 else 0.5
        for r in range(5):
            come_f, go_f = [{}, {}], [{}, {}]
            for k, i in enumerate(come):
                back = go.index(opposite(i))
                pair = stream(
                    near, lambda t, k=k: (x, k, t), i, r, low, high,
                    lambda back=back: get(near, (x, 5 + back, 0), r),
                )
                come_f[0][i], come_f[1][i] = pair
            for k, i in enumerate(go):
                back = come.index(opposite(i))
                pair = stream(
                    near, lambda t, k=k: (x, 5 + k, t), i, r, low, high,
                    lambda back=back: get(near, (x, back, 0), r),
                )
                go_f[0][i], go_f[1][i] = pair
            for t in range(2):
                f = {i: kept(x, k, t, r) for k, i in enumerate(KNOWN[x])}
                f.update(come_f[t])
                rho_new, mom_new = moments(come_f[t], come)
                rho = kept(x, 14, t, r) + rho_new
                mom = [kept(x, 15 + j, t, r) + mom_new[j] for j in range(3)]
                inv = 1.0 / rho
                u = [m * inv for m in mom]
                relaxed = relax(f, rho, u, numbers)
                for i in numbers:
                    put(fields, (i, x, t), r, relaxed[i])
                for j in range(3):
                    put(fields, (19 + j, x, t), r, u[j])
                u0 = [kept(x, 24 + j, t, r) for j in range(3)]
                a0 = [kept(x, 27 + k, t, r) for k in range(6)]
                u0n = [arrived(x, 5 + j, t, r) for j in range(3)]
                a0n = [arrived(x, 8 + k, t, r) for k in range(6)]
                rate = jeffery(a0, [[sign * u0n[j], None, None] for j in range(3)])
                drift = (sign * u0[0])
                for k in range(6):
                    a1 = kept(x, 18 + k, t, r) + ORIENT_STEP * (rate[k] - drift * a0n[k])
                    put(fields, (22 + k, x, t), r, a1)
                rho_new, mom_new = moments(go_f[t], go)
                rho = arrived(x, 14, t, r) + rho_new
                inv = 1.0 / rho
                u = [(arrived(x, 15 + j, t, r) + mom_new[j]) * inv for j in range(3)]
                f = {i: arrived(x, 18 + k, t, r) for k, i in enumerate(come)}
                relaxed = relax(f, rho, u, come)
                for k, i in enumerate(come):
                    put(fields, (28 + k, x, t), r, relaxed[i])
                if t == 0 and r < 4:
                    rate = jeffery(a0n, [[-sign * u0[j], None, None] for j in range(3)])
                    drift = -sign * u0n[0]
                    for j in range(3):
                        level[x, j, pl.ds(8 * r, 8), :] = u[j]
                    for k in range(6):
                        a1 = arrived(x, 23 + k, t, r) + ORIENT_STEP * (rate[k] - drift * a0[k])
                        level[x, 3 + k, pl.ds(8 * r, 8), :] = a1

    feats[...] = jnp.ones(feats.shape, jnp.float32)
    for x in range(2):
        for r in range(4):
            f = {}
            for i in numbers:
                xs = x - VELOCITIES[i][0]
                if 0 <= xs <= 1:
                    at_of = lambda t, i=i, xs=xs: (i, xs, t)
                else:
                    k = TOWARD[1 - x].index(i)
                    at_of = lambda t, k=k: (28 + k, x, t)
                f[i], _ = stream(
                    fields, at_of, i, r, low, high, lambda i=i: get(fields, (opposite(i), x, 0), r), False
                )
            rho, mom = moments(f, numbers)
            inv = 1.0 / rho
            final = [rho] + [m * inv for m in mom]
            for k in range(4):
                spread[pl.ds(k * 64 + x * 32 + 8 * r, 8), :] = final[k]
            sign = -0.5 if x == 0 else 0.5
            by_x = lambda k, n: sign * (level[x, n, pl.ds(8 * r, 8), :] - get(fields, (k, 1 - x, 0), r))
            grad = [[None] * 3 for _ in range(3)]
            for j in range(3):
                place_u = lambda t, j=j: (19 + j, x, t)
                grad[j][0] = by_x(19 + j, j)
                grad[j][1] = central(fields, place_u, r, 1, low, high, False, False)[0]
                grad[j][2] = central(fields, place_u, r, 2, low, high, False, False)[0]
            u = [get(fields, (19 + j, x, 0), r) for j in range(3)]
            a = [get(fields, (22 + k, x, 0), r) for k in range(6)]
            rate = jeffery(a, grad)
            for k in range(6):
                place_a = lambda t, k=k: (22 + k, x, t)
                advect = (
                    u[0] * by_x(22 + k, 3 + k)
                    + u[1] * central(fields, place_a, r, 1, low, high, True, False)[0]
                    + u[2] * central(fields, place_a, r, 2, low, high, True, False)[0]
                )
                new = a[k] + ORIENT_STEP * (rate[k] - advect)
                feats[pl.ds((x * 32 + 8 * r) * 8 + k, 8, 8), :] = new
    for k in range(4):
        for x in range(2):
            flow[k, x] = spread[pl.ds(k * 64 + x * 32, 32), :].astype(jnp.bfloat16)

    spread[...] = jnp.zeros(spread.shape, jnp.float32)
    group = 8
    bias_mid = jnp.concatenate([b_mid[...]] * group, axis=1)
    for g in range(16 // group):
        at = [place[g * group + k] for k in range(group)]
        cells = [feats[pl.ds(pl.multiple_of(b * 8, 8), 8), :] for b in at]
        cells = jnp.concatenate(cells, axis=1).astype(jnp.bfloat16)
        v = jnp.dot(w_one[...], cells, preferred_element_type=jnp.float32)
        h = (v + v * jnp.tanh(v)).astype(jnp.bfloat16)
        v = jnp.dot(w_mid[...], h, preferred_element_type=jnp.float32) + bias_mid
        h = (v + v * jnp.tanh(v)).astype(jnp.bfloat16)
        v = jnp.dot(w_out[...], h, preferred_element_type=jnp.float32)
        for k in range(group):
            spread[pl.ds(pl.multiple_of(at[k] * 16, 16), 15), :] = v[:, 128 * k : 128 * k + 128] + b_out[0:15, :]
    for c in range(15):
        for x in range(2):
            closure[c, x] = spread[pl.ds(x * 512 + c, 32, 16), :].astype(jnp.bfloat16)


def local(populations, orientation, slot_table, w_in, b_in, w_mid, b_mid, w_out, b_out):
    f32, bf16 = jnp.float32, jnp.bfloat16
    shape = lambda *s, d=f32: jax.ShapeDtypeStruct(s, d)
    vmem = pl.BlockSpec(memory_space=pltpu.VMEM)
    smem = pl.BlockSpec(memory_space=pltpu.SMEM)
    params = pltpu.CompilerParams(vmem_limit_bytes=48 * 1024 * 1024)

    def ring(axis, step, wrap):
        n = lax.axis_size(axis)
        return [(i, (i + step) % n) for i in range(n) if wrap or 0 <= i + step < n]

    hbm = pl.BlockSpec(memory_space=pltpu.HBM)
    slots = jnp.transpose(slot_table, (0, 2, 1))
    w_one, w_two, bias_mid, w_three, bias_out = pl.pallas_call(
        weights_kernel,
        out_shape=(
            shape(512, 8, d=bf16),
            shape(512, 512, d=bf16),
            shape(512, 128),
            shape(15, 512, d=bf16),
            shape(16, 128),
        ),
        in_specs=[hbm] * 6,
        out_specs=(vmem,) * 5,
        scratch_shapes=[
            pltpu.VMEM((6, 512), bf16),
            pltpu.VMEM((1, 512), f32),
            pltpu.VMEM((512, 512), bf16),
            pltpu.VMEM((1, 512), f32),
            pltpu.VMEM((1, 15), f32),
            pltpu.VMEM((8, 128), f32),
            pltpu.SemaphoreType.DMA((6,)),
        ],
        compiler_params=pltpu.CompilerParams(vmem_limit_bytes=LIMIT_WEIGHTS),
    )(w_in, b_in.reshape(1, 512), w_mid, b_mid.reshape(1, 512), w_out.T, b_out.reshape(1, 15))
    zpack, low_raw, high_raw = pl.pallas_call(
        pack_z_kernel,
        out_shape=(shape(2, 32, 128), shape(104, 128), shape(104, 128)),
        in_specs=[hbm] * 2,
        out_specs=(vmem,) * 3,
        scratch_shapes=[
            pltpu.VMEM((19, 2, 32, 128), f32),
            pltpu.VMEM((6, 2, 32, 128), f32),
            pltpu.SemaphoreType.DMA((2,)),
        ],
        compiler_params=pltpu.CompilerParams(vmem_limit_bytes=LIMIT_PACK),
        cost_estimate=COST_PACK,
    )(populations, orientation)
    own, token = pl.pallas_call(
        own_kernel,
        out_shape=(shape(28, 2, 32, 128), shape(8, 128)),
        in_specs=[vmem] * 3,
        out_specs=(vmem,) * 2,
        compiler_params=params,
    )(populations, orientation, zpack)
    from_minus = lax.ppermute(zpack, "gz", ring("gz", 1, False))
    from_plus = lax.ppermute(zpack, "gz", ring("gz", -1, False))
    sides, low_rows, high_rows = pl.pallas_call(
        pack_y_kernel,
        out_shape=(shape(2, 32, 128), shape(104, 128), shape(104, 128)),
        in_specs=[vmem] * 5,
        out_specs=(vmem,) * 3,
        compiler_params=params,
    )(from_minus, from_plus, low_raw, high_raw, token)
    from_yminus = lax.ppermute(high_rows, "gy", ring("gy", 1, True))
    from_yplus = lax.ppermute(low_rows, "gy", ring("gy", -1, True))
    state, msg_off, msg_on = pl.pallas_call(
        step_one_kernel,
        out_shape=(
            shape(2, STATE, 2, 40, 128),
            shape(MSG_ROWS, 128, d=bf16),
            shape(MSG_ROWS, 128, d=bf16),
        ),
        in_specs=[vmem] * 4,
        out_specs=(vmem,) * 3,
        scratch_shapes=[
            pltpu.VMEM((52, 8, 128), f32),
            pltpu.VMEM((28, 2, 2, 64, 128), f32),
            pltpu.VMEM((2, MSG_ROWS, 128), f32),
        ],
        compiler_params=params,
    )(own, sides, from_yminus, from_yplus)
    x_count = lax.axis_size("gx")
    off_chip = [(i, (i + (1 if i % 2 else -1)) % x_count) for i in range(x_count)]
    on_chip = [(i, i + (-1 if i % 2 else 1)) for i in range(x_count)]
    from_off = lax.ppermute(msg_off, "gx", off_chip)
    from_on = lax.ppermute(msg_on, "gx", on_chip)
    return pl.pallas_call(
        step_two_kernel,
        out_shape=(shape(4, 2, 32, 128, d=bf16), shape(15, 2, 32, 128, d=bf16)),
        in_specs=[smem] + [vmem] * 8,
        out_specs=(vmem,) * 2,
        scratch_shapes=[
            pltpu.VMEM((2, MSG_ROWS, 128), f32),
            pltpu.VMEM((33, 2, 2, 64, 128), f32),
            pltpu.VMEM((2, 10, 2, 64, 128), f32),
            pltpu.VMEM((2, 9, 32, 128), f32),
            pltpu.VMEM((65 * 8, 128), f32),
            pltpu.VMEM((65 * 16, 128), f32),
            pltpu.SMEM((17,), jnp.int32),
        ],
        compiler_params=params,
    )(slots, state, from_off, from_on, w_one, w_two, bias_mid, w_three, bias_out)


def solution(mesh):
    grid = P(None, "gx", "gy", "gz")
    in_specs = (grid, grid, P("gx", "gy", "gz"), P(), P(), P(), P(), P(), P())
    return jax.shard_map(local, mesh=mesh, in_specs=in_specs, out_specs=(grid, grid), check_vma=False)
```

```python
import functools

import jax
import jax.numpy as jnp
from jax import lax
from jax.experimental import pallas as pl
from jax.experimental.pallas import tpu as pltpu
from jax.sharding import PartitionSpec as P


VELOCITIES = [
    (0, 0, 0),
    (1, 0, 0),
    (-1, 0, 0),
    (0, 1, 0),
    (0, -1, 0),
    (0, 0, 1),
    (0, 0, -1),
    (1, 1, 0),
    (-1, -1, 0),
    (1, -1, 0),
    (-1, 1, 0),
    (1, 0, 1),
    (-1, 0, -1),
    (1, 0, -1),
    (-1, 0, 1),
    (0, 1, 1),
    (0, -1, -1),
    (0, 1, -1),
    (0, -1, 1),
]
WEIGHTS = [1.0 / 3.0] + [1.0 / 18.0] * 6 + [1.0 / 36.0] * 12
OMEGA = 1.0 / 0.8
SHAPE_FACTOR = 0.95
ORIENT_STEP = 4.0
PAIRS = [(0, 0), (1, 1), (2, 2), (0, 1), (0, 2), (1, 2)]
ENTRY = [[0, 3, 4], [3, 1, 5], [4, 5, 2]]
TOWARD = {
    0: [i for i in range(19) if VELOCITIES[i][0] == -1],
    1: [i for i in range(19) if VELOCITIES[i][0] == 1],
}
KNOWN = {0: [i for i in range(19) if VELOCITIES[i][0] != 1], 1: [i for i in range(19) if VELOCITIES[i][0] != -1]}
MSG_WIDE = 23
MSG_ROWS = 1072
MID_ROWS = 480
SIDE_MID = 464
RIM_AT = 480
HALO_AT = 944
SIDE_RIM = 1040
CORNER_AT = 1056
MIB = 1024 * 1024
LIMIT_PACK = 5375 * MIB // 100
COST_PACK = pl.CostEstimate(flops=10**10, bytes_accessed=10**7, transcendentals=0)
LIMIT_WEIGHTS = 4900 * MIB // 100
STATE = 38


def opposite(i):
    return 0 if i == 0 else (i + 1 if i % 2 == 1 else i - 1)


def lanes_of():
    return lax.broadcasted_iota(jnp.int32, (8, 128), 1)


def rows_of():
    return lax.broadcasted_iota(jnp.int32, (8, 128), 0)


def roll(v, shift, axis):
    shift = shift % v.shape[axis]
    return v if shift == 0 else pltpu.roll(v, shift, axis)


def add_all(terms):
    while len(terms) > 1:
        terms = [
            terms[k] + terms[k + 1] if k + 1 < len(terms) else terms[k] for k in range(0, len(terms), 2)
        ]
    return terms[0]


def moments(f, numbers):
    rho = add_all([f[i] for i in numbers])
    mom = []
    for ax in range(3):
        pos = [f[i] for i in numbers if VELOCITIES[i][ax] > 0]
        neg = [f[i] for i in numbers if VELOCITIES[i][ax] < 0]
        total = add_all(pos) if pos else None
        if neg:
            total = add_all(neg) * -1.0 if total is None else total - add_all(neg)
        mom.append(total)
    return rho, mom


def relax(f, rho, u, numbers):
    usq = 1.0 - 1.5 * (u[0] * u[0] + u[1] * u[1] + u[2] * u[2])
    scaled = {w: (w * OMEGA) * rho for w in sorted(set(WEIGHTS[i] for i in numbers))}
    out = {}
    for i in numbers:
        proj = None
        for ax in range(3):
            c = VELOCITIES[i][ax]
            if c != 0:
                if proj is None:
                    proj = u[ax] if c > 0 else -u[ax]
                else:
                    proj = proj + u[ax] if c > 0 else proj - u[ax]
        poly = usq if proj is None else usq + proj * (3.0 + 4.5 * proj)
        out[i] = f[i] * (1.0 - OMEGA) + scaled[WEIGHTS[i]] * poly
    return out


def plus(a, b):
    if a is None:
        return b
    if b is None:
        return a
    return a + b


def minus(a, b):
    if b is None:
        return a
    if a is None:
        return -b
    return a - b


def times(a, b):
    return None if a is None or b is None else a * b


def jeffery(a, g):
    half = [[None if g[j][k] is None else 0.5 * g[j][k] for k in range(3)] for j in range(3)]
    d = [[plus(half[j][k], half[k][j]) if j <= k else None for k in range(3)] for j in range(3)]
    w = [[minus(half[j][k], half[k][j]) if j < k else None for k in range(3)] for j in range(3)]
    full = lambda j, k: a[ENTRY[j][k]]
    strain = lambda j, k: d[min(j, k)][max(j, k)]

    def spin(j, k):
        if j == k:
            return None
        if j < k:
            return w[j][k]
        return None if w[k][j] is None else -w[k][j]

    contraction = None
    for j in range(3):
        contraction = plus(contraction, times(full(j, j), strain(j, j)))
    for j, k in ((0, 1), (0, 2), (1, 2)):
        cross = times(full(j, k), strain(j, k))
        contraction = plus(contraction, None if cross is None else 2.0 * cross)
    twice = 2.0 * contraction
    mix = [[plus(spin(j, k), times(strain(j, k), SHAPE_FACTOR)) for k in range(3)] for j in range(3)]
    z = [[None] * 3 for _ in range(3)]
    for j in range(3):
        for k in range(3):
            for m in range(3):
                z[j][k] = plus(z[j][k], times(full(j, m), mix[m][k]))
    scaled = SHAPE_FACTOR * twice
    return [plus(z[j][k], z[k][j]) - scaled * full(j, k) for j, k in PAIRS]


def field_row(k, r):
    return 16 * k + 8 * (r - 1) if r in (1, 2) else RIM_AT + 16 * k + 8 * (r // 3)


def side_row(r):
    return SIDE_MID + 8 * (r - 1) if r in (1, 2) else (CORNER_AT if r == 4 else SIDE_RIM + 8 * (r // 3))


def state_row(r):
    return {1: 0, 2: 8, 0: 0, 3: 8, 4: 16}[r]


def put(ref, at, r, v):
    if r < 4:
        ref[at + (pl.ds(16 + 8 * r, 8), slice(None))] = v
    else:
        ref[at + (pl.ds(8, 8), slice(None))] = v
        ref[at + (pl.ds(48, 8), slice(None))] = v


def get(ref, at, r, dy=0):
    if r < 4:
        return ref[at + (pl.ds(16 + 8 * r + dy, 8), slice(None))]
    if dy == 0:
        return ref[at + (pl.ds(48, 8), slice(None))]
    return jnp.where(
        rows_of() < 4,
        ref[at + (pl.ds(48 + dy, 8), slice(None))],
        ref[at + (pl.ds(8 + dy, 8), slice(None))],
    )


def pull_z(own, side, dz, want_side=True):
    if dz == 0:
        return own, side
    lane = lanes_of()
    own_r, side_r = roll(own, dz, 1), roll(side, dz, 1)
    edge = lane == (0 if dz > 0 else 127)
    return jnp.where(edge, side_r, own_r), jnp.where(edge, own_r, side_r) if want_side else None


def walls():
    layer = lax.axis_index("gz")
    last = lax.axis_size("gz") - 1
    lane = lanes_of()
    low = lane == jnp.where(layer == 0, 0, -1)
    high = lane == jnp.where(layer == last, 127, -1)
    return low, high


def wall_of(i, low, high):
    dz = VELOCITIES[i][2]
    return None if dz == 0 else (low if dz > 0 else high)


def stream(ref, at_of, i, r, low, high, reflected, want_side=True):
    _, cy, cz = VELOCITIES[i]
    own = get(ref, at_of(0), r, -cy)
    side = get(ref, at_of(1), r, -cy) if (want_side or cz != 0) else None
    if cz == 0:
        return own, side
    own, side = pull_z(own, side, cz, want_side)
    return jnp.where(wall_of(i, low, high), reflected(), own), side


def central(ref, at_of, r, axis, low, high, outside, want_side=True):
    if axis == 1:
        out = []
        for t in (0, 1) if want_side else (0,):
            out.append(0.5 * (get(ref, at_of(t), r, 1) - get(ref, at_of(t), r, -1)))
        return out
    own, side = get(ref, at_of(0), r), get(ref, at_of(1), r)
    behind, behind_side = pull_z(own, side, 1, want_side)
    ahead, ahead_side = pull_z(own, side, -1, want_side)
    past = own if outside else jnp.zeros_like(own)
    diff = 0.5 * (jnp.where(high, past, ahead) - jnp.where(low, past, behind))
    return [diff, 0.5 * (ahead_side - behind_side)] if want_side else [diff]


def fetch(pairs, sems):
    copies = [pltpu.make_async_copy(src, dst, sems.at[k]) for k, (src, dst) in enumerate(pairs)]
    for copy in copies:
        copy.start()
    return copies


def pack_z_kernel(pop_hbm, ori_hbm, zpack, low_rows, high_rows, pop, ori, sems):
    for copy in fetch([(pop_hbm, pop), (ori_hbm, ori)], sems):
        copy.wait()
    lane = lax.broadcasted_iota(jnp.int32, (32, 128), 1)
    tiles = [jnp.zeros((32, 128), jnp.float32), jnp.zeros((32, 128), jnp.float32)]
    for f in range(25):
        for x in range(2):
            s = 2 * f + x
            src = pop if f < 19 else ori
            k = f if f < 19 else f - 19
            v = src[k, x]
            at = 4 * (s % 32)
            tiles[s // 32] = jnp.where((lane >= at) & (lane < at + 4), roll(v, at + 2, 1), tiles[s // 32])
            low_rows[pl.ds(2 * s, 2), :] = src[k, x, 0:2, :]
            high_rows[pl.ds(2 * s, 2), :] = src[k, x, 30:32, :]
    zpack[0] = tiles[0]
    zpack[1] = tiles[1]
    low_rows[100:104, :] = jnp.zeros((4, 128), jnp.float32)
    high_rows[100:104, :] = jnp.zeros((4, 128), jnp.float32)


def own_kernel(pop, ori, after, own, token):
    token[...] = jnp.zeros(token.shape, jnp.float32)
    numbers = list(range(19))
    for x in range(2):
        for r in range(4):
            rows = pl.ds(8 * r, 8)
            f = [pop[i, x, rows, :] for i in numbers]
            rho, mom = moments(f, numbers)
            inv = 1.0 / rho
            u = [m * inv for m in mom]
            relaxed = relax(f, rho, u, numbers)
            for i in numbers:
                own[i, x, rows, :] = relaxed[i]
            for j in range(3):
                own[19 + j, x, rows, :] = u[j]
            for k in range(6):
                own[22 + k, x, rows, :] = ori[k, x, rows, :]


def pack_y_kernel(from_minus, from_plus, low_in, high_in, token, sides, low_rows, high_rows):
    lane = lax.broadcasted_iota(jnp.int32, (32, 128), 1)
    low_rows[...] = low_in[...]
    high_rows[...] = high_in[...]
    for t in range(2):
        both = jnp.where(lane % 4 < 2, from_minus[t], from_plus[t])
        sides[t] = both
        low_rows[pl.ds(100 + 2 * t, 2), :] = sides[t, 0:2, :]
        high_rows[pl.ds(100 + 2 * t, 2), :] = sides[t, 30:32, :]


def collide_group(raw, fields, x, t, r):
    numbers = list(range(19))
    f = [raw(i) for i in numbers]
    rho, mom = moments(f, numbers)
    inv = 1.0 / rho
    u = [m * inv for m in mom]
    relaxed = relax(f, rho, u, numbers)
    for i in numbers:
        put(fields, (i, x, t), r, relaxed[i])
    for j in range(3):
        put(fields, (19 + j, x, t), r, u[j])
    for k in range(6):
        put(fields, (22 + k, x, t), r, raw(19 + k))


def advance_group(fields, state, out, x, r, low, high):
    lane, row = lanes_of(), rows_of()
    place = lambda f, xs=x: (lambda t: (f, xs, t))
    known = [{}, {}]
    for i in KNOWN[x]:
        xs = x - VELOCITIES[i][0]
        pair = stream(fields, place(i, xs), i, r, low, high, lambda i=i: get(fields, (opposite(i), x, 0), r))
        known[0][i], known[1][i] = pair
    grad = [[[None] * 3 for _ in range(3)] for _ in range(2)]
    sign = 0.5 if x == 0 else -0.5
    for j in range(3):
        by_y = central(fields, place(19 + j), r, 1, low, high, False)
        by_z = central(fields, place(19 + j), r, 2, low, high, False)
        for t in range(2):
            grad[t][j][0] = sign * get(fields, (19 + j, 1 - x, t), r)
            grad[t][j][1] = by_y[t]
            grad[t][j][2] = by_z[t]
    u = [[get(fields, (19 + j, x, t), r) for j in range(3)] for t in range(2)]
    a = [[get(fields, (22 + k, x, t), r) for k in range(6)] for t in range(2)]
    advect = [[], []]
    for k in range(6):
        by_y = central(fields, place(22 + k), r, 1, low, high, True)
        by_z = central(fields, place(22 + k), r, 2, low, high, True)
        for t in range(2):
            by_x = sign * get(fields, (22 + k, 1 - x, t), r)
            advect[t].append(u[t][0] * by_x + u[t][1] * by_y[t] + u[t][2] * by_z[t])
    side_pack = jnp.zeros((8, 128), jnp.float32)
    for t in range(2):
        rate = jeffery(a[t], grad[t])
        part = [a[t][k] + ORIENT_STEP * (rate[k] - advect[t][k]) for k in range(6)]
        rho, mom = moments(known[t], KNOWN[x])
        outward = [get(fields, (i, x, t), r) for i in TOWARD[x]]
        keep = [known[t][i] for i in KNOWN[x]] + [rho] + mom + part + u[t] + a[t] + outward
        for k in range(STATE):
            state[x, k, t, pl.ds(state_row(r), 8), :] = keep[k]
        wide = outward + u[t] + a[t] + [rho] + mom + [known[t][i] for i in TOWARD[x]]
        if t == 1:
            for k in range(MSG_WIDE):
                at = 4 * k
                side_pack = jnp.where((lane >= at) & (lane < at + 4), roll(wide[k], at + 2, 1), side_pack)
        elif r < 4:
            for k, v in enumerate(wide + part):
                out[x, pl.ds(field_row(k, r), 8), :] = v
        else:
            inner = (row >= 2) & (row < 6)
            for k in range(0, MSG_WIDE, 2):
                v = wide[k]
                if k + 1 < MSG_WIDE:
                    v = jnp.where(inner, roll(wide[k + 1], 4, 0), v)
                out[x, pl.ds(HALO_AT + 4 * k, 8), :] = v
    out[x, pl.ds(side_row(r), 8), :] = side_pack


def middle_kernel(own, sides, fields, state, message, out):
    low, high = walls()
    for x in range(2):
        for r in range(4):
            rows = pl.ds(8 * r, 8)
            for k in range(28):
                put(fields, (k, x, 0), r, own[k, x, rows, :])

            def raw(f):
                s = 2 * f + x
                return roll(sides[s // 32, rows, :], -(4 * (s % 32) + 2), 1)

            collide_group(raw, fields, x, 1, r)
    for x in range(2):
        for r in (1, 2):
            advance_group(fields, state, out, x, r, low, high)
    message[...] = out[...].astype(jnp.bfloat16)


def step_one_kernel(before, middle, from_yminus, from_yplus, fields, state, msg_low, msg_high, halo, out):
    del before
    low, high = walls()
    for s in range(52):
        halo[s, 0:2, :] = from_yplus[pl.ds(2 * s, 2), :]
        halo[s, 6:8, :] = from_yminus[pl.ds(2 * s, 2), :]
    for x in range(2):
        for t in range(2):

            def raw(f):
                s = 2 * f + x
                return halo[s] if t == 0 else roll(halo[50 + s // 32], -(4 * (s % 32) + 2), 1)

            collide_group(raw, fields, x, t, 4)
    for x in range(2):
        for r in (0, 3, 4):
            advance_group(fields, state, out, x, r, low, high)
        out[x, pl.ds(CORNER_AT + 8, 8), :] = jnp.zeros((8, 128), jnp.float32)
    for x, msg in enumerate((msg_low, msg_high)):
        msg[0:MID_ROWS, :] = middle[x]
        msg[MID_ROWS:MSG_ROWS, :] = out[x, MID_ROWS:MSG_ROWS, :].astype(jnp.bfloat16)


def weights_kernel(
    w_in_hbm, b_in_hbm, w_mid_hbm, b_mid_hbm, w_out_hbm, b_out_hbm, w_one, w_two, bias_mid, w_three, bias_out,
    w_in, b_in, w_mid, b_mid, b_out, wide, sems,
):
    pairs = [
        (w_mid_hbm, w_mid),
        (w_in_hbm, w_in),
        (b_in_hbm, b_in),
        (b_mid_hbm, b_mid),
        (b_out_hbm, b_out),
        (w_out_hbm, w_three),
    ]
    for copy in fetch(pairs, sems):
        copy.wait()
    f32, bf16 = jnp.float32, jnp.bfloat16
    row = lax.broadcasted_iota(jnp.int32, (8, 512), 0)
    bias = jnp.broadcast_to(0.5 * b_in[...], (8, 512))
    first = bias.astype(bf16).astype(f32)
    rest = bias - first
    padded = jnp.concatenate([0.5 * w_in[...].astype(f32), jnp.zeros((2, 512), f32)], axis=0)
    stacked = jnp.where(row == 6, first, jnp.where(row == 7, rest, padded))
    w_one[...] = stacked.T.astype(bf16)
    w_two[...] = (0.5 * w_mid[...].astype(f32)).T.astype(bf16)
    bias_mid[...] = jnp.broadcast_to(jnp.broadcast_to(0.5 * b_mid[...], (8, 512)).T[:, 0:1], (512, 128))
    wide[...] = jnp.zeros(wide.shape, f32)
    wide[:, 0:15] = jnp.broadcast_to(b_out[...], (8, 15))
    bias_out[...] = jnp.broadcast_to(wide[...].T[0:16, 0:1], (16, 128))


def step_two_kernel(
    slots, state_mid, state_rim, from_low, from_high, w_one, w_mid, b_mid, w_out, b_out, flow, closure,
    got, fields, near, level, feats, spread, place,
):
    low, high = walls()
    got[0] = from_low[...].astype(jnp.float32)
    got[1] = from_high[...].astype(jnp.float32)
    for s in range(17):
        place[s] = 64
    for b in range(64):
        s = slots[b // 32, 0, b % 32]
        place[jnp.where(s >= 0, s, 16)] = b

    def arrived(x, k, t, r):
        if t == 0 and r < 4:
            return got[x, pl.ds(field_row(k, r), 8), :]
        if t == 0:
            v = got[x, pl.ds(HALO_AT + 8 * (k // 2), 8), :]
            return roll(v, 4, 0) if k % 2 else v
        v = got[x, pl.ds(side_row(r), 8), :]
        return roll(v, -(4 * k + 2), 1)

    def kept(x, k, t, r):
        part = state_mid if r in (1, 2) else state_rim
        return part[x, k, t, pl.ds(state_row(r), 8), :]

    for x in range(2):
        for t in range(2):
            for r in range(5):
                for k in range(5):
                    put(near, (x, k, t), r, arrived(x, k, t, r))
                    put(near, (x, 5 + k, t), r, kept(x, 33 + k, t, r))
    numbers = list(range(19))
    for x in range(2):
        come = TOWARD[1 - x]
        go = TOWARD[x]
        sign = -0.5 if x == 0 else 0.5
        for r in range(5):
            come_f, go_f = [{}, {}], [{}, {}]
            for k, i in enumerate(come):
                back = go.index(opposite(i))
                pair = stream(
                    near, lambda t, k=k: (x, k, t), i, r, low, high,
                    lambda back=back: get(near, (x, 5 + back, 0), r),
                )
                come_f[0][i], come_f[1][i] = pair
            for k, i in enumerate(go):
                back = come.index(opposite(i))
                pair = stream(
                    near, lambda t, k=k: (x, 5 + k, t), i, r, low, high,
                    lambda back=back: get(near, (x, back, 0), r),
                )
                go_f[0][i], go_f[1][i] = pair
            for t in range(2):
                f = {i: kept(x, k, t, r) for k, i in enumerate(KNOWN[x])}
                f.update(come_f[t])
                rho_new, mom_new = moments(come_f[t], come)
                rho = kept(x, 14, t, r) + rho_new
                mom = [kept(x, 15 + j, t, r) + mom_new[j] for j in range(3)]
                inv = 1.0 / rho
                u = [m * inv for m in mom]
                relaxed = relax(f, rho, u, numbers)
                for i in numbers:
                    put(fields, (i, x, t), r, relaxed[i])
                for j in range(3):
                    put(fields, (19 + j, x, t), r, u[j])
                u0 = [kept(x, 24 + j, t, r) for j in range(3)]
                a0 = [kept(x, 27 + k, t, r) for k in range(6)]
                u0n = [arrived(x, 5 + j, t, r) for j in range(3)]
                a0n = [arrived(x, 8 + k, t, r) for k in range(6)]
                rate = jeffery(a0, [[sign * u0n[j], None, None] for j in range(3)])
                drift = (sign * u0[0])
                for k in range(6):
                    a1 = kept(x, 18 + k, t, r) + ORIENT_STEP * (rate[k] - drift * a0n[k])
                    put(fields, (22 + k, x, t), r, a1)
                rho_new, mom_new = moments(go_f[t], go)
                rho = arrived(x, 14, t, r) + rho_new
                inv = 1.0 / rho
                u = [(arrived(x, 15 + j, t, r) + mom_new[j]) * inv for j in range(3)]
                f = {i: arrived(x, 18 + k, t, r) for k, i in enumerate(come)}
                relaxed = relax(f, rho, u, come)
                for k, i in enumerate(come):
                    put(fields, (28 + k, x, t), r, relaxed[i])
                if t == 0 and r < 4:
                    rate = jeffery(a0n, [[-sign * u0[j], None, None] for j in range(3)])
                    drift = -sign * u0n[0]
                    for j in range(3):
                        level[x, j, pl.ds(8 * r, 8), :] = u[j]
                    for k in range(6):
                        a1 = arrived(x, 23 + k, t, r) + ORIENT_STEP * (rate[k] - drift * a0[k])
                        level[x, 3 + k, pl.ds(8 * r, 8), :] = a1

    feats[...] = jnp.ones(feats.shape, jnp.float32)
    for x in range(2):
        for r in range(4):
            f = {}
            for i in numbers:
                xs = x - VELOCITIES[i][0]
                if 0 <= xs <= 1:
                    at_of = lambda t, i=i, xs=xs: (i, xs, t)
                else:
                    k = TOWARD[1 - x].index(i)
                    at_of = lambda t, k=k: (28 + k, x, t)
                f[i], _ = stream(
                    fields, at_of, i, r, low, high, lambda i=i: get(fields, (opposite(i), x, 0), r), False
                )
            rho, mom = moments(f, numbers)
            inv = 1.0 / rho
            final = [rho] + [m * inv for m in mom]
            for k in range(4):
                spread[pl.ds(k * 64 + x * 32 + 8 * r, 8), :] = final[k]
            sign = -0.5 if x == 0 else 0.5
            by_x = lambda k, n: sign * (level[x, n, pl.ds(8 * r, 8), :] - get(fields, (k, 1 - x, 0), r))
            grad = [[None] * 3 for _ in range(3)]
            for j in range(3):
                place_u = lambda t, j=j: (19 + j, x, t)
                grad[j][0] = by_x(19 + j, j)
                grad[j][1] = central(fields, place_u, r, 1, low, high, False, False)[0]
                grad[j][2] = central(fields, place_u, r, 2, low, high, False, False)[0]
            u = [get(fields, (19 + j, x, 0), r) for j in range(3)]
            a = [get(fields, (22 + k, x, 0), r) for k in range(6)]
            rate = jeffery(a, grad)
            for k in range(6):
                place_a = lambda t, k=k: (22 + k, x, t)
                advect = (
                    u[0] * by_x(22 + k, 3 + k)
                    + u[1] * central(fields, place_a, r, 1, low, high, True, False)[0]
                    + u[2] * central(fields, place_a, r, 2, low, high, True, False)[0]
                )
                new = a[k] + ORIENT_STEP * (rate[k] - advect)
                feats[pl.ds((x * 32 + 8 * r) * 8 + k, 8, 8), :] = new
    for k in range(4):
        for x in range(2):
            flow[k, x] = spread[pl.ds(k * 64 + x * 32, 32), :].astype(jnp.bfloat16)

    spread[...] = jnp.zeros(spread.shape, jnp.float32)
    group = 8
    bias_mid = jnp.concatenate([b_mid[...]] * group, axis=1)
    for g in range(16 // group):
        at = [place[g * group + k] for k in range(group)]
        cells = [feats[pl.ds(pl.multiple_of(b * 8, 8), 8), :] for b in at]
        cells = jnp.concatenate(cells, axis=1).astype(jnp.bfloat16)
        v = jnp.dot(w_one[...], cells, preferred_element_type=jnp.float32)
        h = (v + v * jnp.tanh(v)).astype(jnp.bfloat16)
        v = jnp.dot(w_mid[...], h, preferred_element_type=jnp.float32) + bias_mid
        h = (v + v * jnp.tanh(v)).astype(jnp.bfloat16)
        v = jnp.dot(w_out[...], h, preferred_element_type=jnp.float32)
        for k in range(group):
            spread[pl.ds(pl.multiple_of(at[k] * 16, 16), 15), :] = v[:, 128 * k : 128 * k + 128] + b_out[0:15, :]
    for c in range(15):
        for x in range(2):
            closure[c, x] = spread[pl.ds(x * 512 + c, 32, 16), :].astype(jnp.bfloat16)


def local(populations, orientation, slot_table, w_in, b_in, w_mid, b_mid, w_out, b_out):
    f32, bf16 = jnp.float32, jnp.bfloat16
    shape = lambda *s, d=f32: jax.ShapeDtypeStruct(s, d)
    vmem = pl.BlockSpec(memory_space=pltpu.VMEM)
    smem = pl.BlockSpec(memory_space=pltpu.SMEM)
    params = pltpu.CompilerParams(vmem_limit_bytes=24 * MIB)

    def ring(axis, step, wrap):
        n = lax.axis_size(axis)
        return [(i, (i + step) % n) for i in range(n) if wrap or 0 <= i + step < n]

    hbm = pl.BlockSpec(memory_space=pltpu.HBM)
    slots = jnp.transpose(slot_table, (0, 2, 1))
    w_one, w_two, bias_mid, w_three, bias_out = pl.pallas_call(
        weights_kernel,
        out_shape=(
            shape(512, 8, d=bf16),
            shape(512, 512, d=bf16),
            shape(512, 128),
            shape(15, 512, d=bf16),
            shape(16, 128),
        ),
        in_specs=[hbm] * 6,
        out_specs=(vmem,) * 5,
        scratch_shapes=[
            pltpu.VMEM((6, 512), bf16),
            pltpu.VMEM((1, 512), f32),
            pltpu.VMEM((512, 512), bf16),
            pltpu.VMEM((1, 512), f32),
            pltpu.VMEM((1, 15), f32),
            pltpu.VMEM((8, 128), f32),
            pltpu.SemaphoreType.DMA((6,)),
        ],
        compiler_params=pltpu.CompilerParams(vmem_limit_bytes=LIMIT_WEIGHTS),
    )(w_in, b_in.reshape(1, 512), w_mid, b_mid.reshape(1, 512), w_out.T, b_out.reshape(1, 15))
    zpack, low_raw, high_raw = pl.pallas_call(
        pack_z_kernel,
        out_shape=(shape(2, 32, 128), shape(104, 128), shape(104, 128)),
        in_specs=[hbm] * 2,
        out_specs=(vmem,) * 3,
        scratch_shapes=[
            pltpu.VMEM((19, 2, 32, 128), f32),
            pltpu.VMEM((6, 2, 32, 128), f32),
            pltpu.SemaphoreType.DMA((2,)),
        ],
        compiler_params=pltpu.CompilerParams(vmem_limit_bytes=LIMIT_PACK),
        cost_estimate=COST_PACK,
    )(populations, orientation)
    own, token = pl.pallas_call(
        own_kernel,
        out_shape=(shape(28, 2, 32, 128), shape(8, 128)),
        in_specs=[vmem] * 3,
        out_specs=(vmem,) * 2,
        compiler_params=params,
    )(populations, orientation, zpack)
    from_minus = lax.ppermute(zpack, "gz", ring("gz", 1, False))
    from_plus = lax.ppermute(zpack, "gz", ring("gz", -1, False))
    sides, low_rows, high_rows = pl.pallas_call(
        pack_y_kernel,
        out_shape=(shape(2, 32, 128), shape(104, 128), shape(104, 128)),
        in_specs=[vmem] * 5,
        out_specs=(vmem,) * 3,
        compiler_params=params,
    )(from_minus, from_plus, low_raw, high_raw, token)
    fields_shape = shape(28, 2, 2, 64, 128)
    fields, state_mid, middle = pl.pallas_call(
        middle_kernel,
        out_shape=(fields_shape, shape(2, STATE, 2, 16, 128), shape(2, MID_ROWS, 128, d=bf16)),
        in_specs=[vmem] * 2,
        out_specs=(vmem,) * 3,
        scratch_shapes=[pltpu.VMEM((2, MID_ROWS, 128), f32)],
        compiler_params=params,
    )(own, sides)
    from_yminus = lax.ppermute(high_rows, "gy", ring("gy", 1, True))
    from_yplus = lax.ppermute(low_rows, "gy", ring("gy", -1, True))
    fields, state_rim, msg_low, msg_high = pl.pallas_call(
        step_one_kernel,
        out_shape=(
            fields_shape,
            shape(2, STATE, 2, 24, 128),
            shape(MSG_ROWS, 128, d=bf16),
            shape(MSG_ROWS, 128, d=bf16),
        ),
        in_specs=[vmem] * 4,
        out_specs=(vmem,) * 4,
        scratch_shapes=[pltpu.VMEM((52, 8, 128), f32), pltpu.VMEM((2, MSG_ROWS, 128), f32)],
        input_output_aliases={0: 0},
        compiler_params=params,
    )(fields, middle, from_yminus, from_yplus)
    from_low = lax.ppermute(msg_high, "gx", ring("gx", 1, True))
    from_high = lax.ppermute(msg_low, "gx", ring("gx", -1, True))
    return pl.pallas_call(
        step_two_kernel,
        out_shape=(shape(4, 2, 32, 128, d=bf16), shape(15, 2, 32, 128, d=bf16)),
        in_specs=[smem] + [vmem] * 9,
        out_specs=(vmem,) * 2,
        scratch_shapes=[
            pltpu.VMEM((2, MSG_ROWS, 128), f32),
            pltpu.VMEM((33, 2, 2, 64, 128), f32),
            pltpu.VMEM((2, 10, 2, 64, 128), f32),
            pltpu.VMEM((2, 9, 32, 128), f32),
            pltpu.VMEM((65 * 8, 128), f32),
            pltpu.VMEM((65 * 16, 128), f32),
            pltpu.SMEM((17,), jnp.int32),
        ],
        compiler_params=params,
    )(slots, state_mid, state_rim, from_low, from_high, w_one, w_two, bias_mid, w_three, bias_out)


def solution(mesh):
    grid = P(None, "gx", "gy", "gz")
    in_specs = (grid, grid, P("gx", "gy", "gz"), P(), P(), P(), P(), P(), P())
    return jax.shard_map(local, mesh=mesh, in_specs=in_specs, out_specs=(grid, grid), check_vma=False)
```

```python
import functools

import jax
import jax.numpy as jnp
from jax import lax
from jax.experimental import pallas as pl
from jax.experimental.pallas import tpu as pltpu
from jax.sharding import PartitionSpec as P


VELOCITIES = [
    (0, 0, 0),
    (1, 0, 0),
    (-1, 0, 0),
    (0, 1, 0),
    (0, -1, 0),
    (0, 0, 1),
    (0, 0, -1),
    (1, 1, 0),
    (-1, -1, 0),
    (1, -1, 0),
    (-1, 1, 0),
    (1, 0, 1),
    (-1, 0, -1),
    (1, 0, -1),
    (-1, 0, 1),
    (0, 1, 1),
    (0, -1, -1),
    (0, 1, -1),
    (0, -1, 1),
]
WEIGHTS = [1.0 / 3.0] + [1.0 / 18.0] * 6 + [1.0 / 36.0] * 12
OMEGA = 1.0 / 0.8
SHAPE_FACTOR = 0.95
ORIENT_STEP = 4.0
PAIRS = [(0, 0), (1, 1), (2, 2), (0, 1), (0, 2), (1, 2)]
ENTRY = [[0, 3, 4], [3, 1, 5], [4, 5, 2]]
TOWARD = {
    0: [i for i in range(19) if VELOCITIES[i][0] == -1],
    1: [i for i in range(19) if VELOCITIES[i][0] == 1],
}
KNOWN = {0: [i for i in range(19) if VELOCITIES[i][0] != 1], 1: [i for i in range(19) if VELOCITIES[i][0] != -1]}
MSG_WIDE = 23
MSG_ROWS = 1072
MID_ROWS = 480
SIDE_MID = 464
RIM_AT = 480
HALO_AT = 944
SIDE_RIM = 1040
CORNER_AT = 1056
MIB = 1024 * 1024
LIMIT_PACK = 5375 * MIB // 100
COST_PACK = pl.CostEstimate(flops=10**10, bytes_accessed=10**7, transcendentals=0)
LIMIT_WEIGHTS = 4900 * MIB // 100
STATE = 38


def opposite(i):
    return 0 if i == 0 else (i + 1 if i % 2 == 1 else i - 1)


def lanes_of():
    return lax.broadcasted_iota(jnp.int32, (8, 128), 1)


def rows_of():
    return lax.broadcasted_iota(jnp.int32, (8, 128), 0)


def roll(v, shift, axis):
    shift = shift % v.shape[axis]
    return v if shift == 0 else pltpu.roll(v, shift, axis)


def add_all(terms):
    while len(terms) > 1:
        terms = [
            terms[k] + terms[k + 1] if k + 1 < len(terms) else terms[k] for k in range(0, len(terms), 2)
        ]
    return terms[0]


def moments(f, numbers):
    rho = add_all([f[i] for i in numbers])
    mom = []
    for ax in range(3):
        pos = [f[i] for i in numbers if VELOCITIES[i][ax] > 0]
        neg = [f[i] for i in numbers if VELOCITIES[i][ax] < 0]
        total = add_all(pos) if pos else None
        if neg:
            total = add_all(neg) * -1.0 if total is None else total - add_all(neg)
        mom.append(total)
    return rho, mom


def relax(f, rho, u, numbers):
    usq = 1.0 - 1.5 * (u[0] * u[0] + u[1] * u[1] + u[2] * u[2])
    scaled = {w: (w * OMEGA) * rho for w in sorted(set(WEIGHTS[i] for i in numbers))}
    out = {}
    for i in numbers:
        proj = None
        for ax in range(3):
            c = VELOCITIES[i][ax]
            if c != 0:
                if proj is None:
                    proj = u[ax] if c > 0 else -u[ax]
                else:
                    proj = proj + u[ax] if c > 0 else proj - u[ax]
        poly = usq if proj is None else usq + proj * (3.0 + 4.5 * proj)
        out[i] = f[i] * (1.0 - OMEGA) + scaled[WEIGHTS[i]] * poly
    return out


def plus(a, b):
    if a is None:
        return b
    if b is None:
        return a
    return a + b


def minus(a, b):
    if b is None:
        return a
    if a is None:
        return -b
    return a - b


def times(a, b):
    return None if a is None or b is None else a * b


def jeffery(a, g):
    half = [[None if g[j][k] is None else 0.5 * g[j][k] for k in range(3)] for j in range(3)]
    d = [[plus(half[j][k], half[k][j]) if j <= k else None for k in range(3)] for j in range(3)]
    w = [[minus(half[j][k], half[k][j]) if j < k else None for k in range(3)] for j in range(3)]
    full = lambda j, k: a[ENTRY[j][k]]
    strain = lambda j, k: d[min(j, k)][max(j, k)]

    def spin(j, k):
        if j == k:
            return None
        if j < k:
            return w[j][k]
        return None if w[k][j] is None else -w[k][j]

    contraction = None
    for j in range(3):
        contraction = plus(contraction, times(full(j, j), strain(j, j)))
    for j, k in ((0, 1), (0, 2), (1, 2)):
        cross = times(full(j, k), strain(j, k))
        contraction = plus(contraction, None if cross is None else 2.0 * cross)
    twice = 2.0 * contraction
    mix = [[plus(spin(j, k), times(strain(j, k), SHAPE_FACTOR)) for k in range(3)] for j in range(3)]
    z = [[None] * 3 for _ in range(3)]
    for j in range(3):
        for k in range(3):
            for m in range(3):
                z[j][k] = plus(z[j][k], times(full(j, m), mix[m][k]))
    scaled = SHAPE_FACTOR * twice
    return [plus(z[j][k], z[k][j]) - scaled * full(j, k) for j, k in PAIRS]


def field_row(k, r):
    return 16 * k + 8 * (r - 1) if r in (1, 2) else RIM_AT + 16 * k + 8 * (r // 3)


def side_row(r):
    return SIDE_MID + 8 * (r - 1) if r in (1, 2) else (CORNER_AT if r == 4 else SIDE_RIM + 8 * (r // 3))


def state_row(r):
    return {1: 0, 2: 8, 0: 0, 3: 8, 4: 16}[r]


def put(ref, at, r, v):
    if r < 4:
        ref[at + (pl.ds(16 + 8 * r, 8), slice(None))] = v
    else:
        ref[at + (pl.ds(8, 8), slice(None))] = v
        ref[at + (pl.ds(48, 8), slice(None))] = v


def get(ref, at, r, dy=0):
    if r < 4:
        return ref[at + (pl.ds(16 + 8 * r + dy, 8), slice(None))]
    if dy == 0:
        return ref[at + (pl.ds(48, 8), slice(None))]
    return jnp.where(
        rows_of() < 4,
        ref[at + (pl.ds(48 + dy, 8), slice(None))],
        ref[at + (pl.ds(8 + dy, 8), slice(None))],
    )


def pull_z(own, side, dz, want_side=True):
    if dz == 0:
        return own, side
    lane = lanes_of()
    own_r, side_r = roll(own, dz, 1), roll(side, dz, 1)
    edge = lane == (0 if dz > 0 else 127)
    return jnp.where(edge, side_r, own_r), jnp.where(edge, own_r, side_r) if want_side else None


def walls():
    layer = lax.axis_index("gz")
    last = lax.axis_size("gz") - 1
    lane = lanes_of()
    low = lane == jnp.where(layer == 0, 0, -1)
    high = lane == jnp.where(layer == last, 127, -1)
    return low, high


def wall_of(i, low, high):
    dz = VELOCITIES[i][2]
    return None if dz == 0 else (low if dz > 0 else high)


def stream(ref, at_of, i, r, low, high, reflected, want_side=True):
    _, cy, cz = VELOCITIES[i]
    own = get(ref, at_of(0), r, -cy)
    side = get(ref, at_of(1), r, -cy) if (want_side or cz != 0) else None
    if cz == 0:
        return own, side
    own, side = pull_z(own, side, cz, want_side)
    return jnp.where(wall_of(i, low, high), reflected(), own), side


def central(ref, at_of, r, axis, low, high, outside, want_side=True):
    if axis == 1:
        out = []
        for t in (0, 1) if want_side else (0,):
            out.append(0.5 * (get(ref, at_of(t), r, 1) - get(ref, at_of(t), r, -1)))
        return out
    own, side = get(ref, at_of(0), r), get(ref, at_of(1), r)
    behind, behind_side = pull_z(own, side, 1, want_side)
    ahead, ahead_side = pull_z(own, side, -1, want_side)
    past = own if outside else jnp.zeros_like(own)
    diff = 0.5 * (jnp.where(high, past, ahead) - jnp.where(low, past, behind))
    return [diff, 0.5 * (ahead_side - behind_side)] if want_side else [diff]


def fetch(pairs, sems):
    copies = [pltpu.make_async_copy(src, dst, sems.at[k]) for k, (src, dst) in enumerate(pairs)]
    for copy in copies:
        copy.start()
    return copies


PIECES = [(0, 5), (5, 10), (10, 15), (15, 19)]


def pack_z_kernel(pop_hbm, ori_hbm, zlow, zhigh, low_rows, high_rows, pop, ori, sems):
    pairs = [(pop_hbm.at[pl.ds(a, b - a)], pop.at[pl.ds(a, b - a)]) for a, b in PIECES]
    copies = fetch(pairs + [(ori_hbm, ori)], sems)
    starts = [a for a, _ in PIECES] + [19]
    lane = lax.broadcasted_iota(jnp.int32, (32, 128), 1)
    low = jnp.zeros((32, 128), jnp.float32)
    high = jnp.zeros((32, 128), jnp.float32)
    for f in range(25):
        if f in starts:
            copies[starts.index(f)].wait()
        src = pop if f < 19 else ori
        k = f if f < 19 else f - 19
        for x in range(2):
            s = 2 * f + x
            at = 2 * s
            v = roll(src[k, x], at + 2, 1)
            high = jnp.where((lane >= at) & (lane < at + 2), v, high)
            low = jnp.where((lane >= at + 2) & (lane < at + 4), v, low)
            low_rows[pl.ds(2 * s, 2), :] = src[k, x, 0:2, :]
            high_rows[pl.ds(2 * s, 2), :] = src[k, x, 30:32, :]
    zlow[...] = low.astype(jnp.bfloat16)
    zhigh[...] = high.astype(jnp.bfloat16)
    low_rows[100:112, :] = jnp.zeros((12, 128), jnp.float32)
    high_rows[100:112, :] = jnp.zeros((12, 128), jnp.float32)


def unpack_z(from_minus, from_plus, s):
    shift = -(2 * s + 2)
    return jnp.where(lanes_of() < 64, roll(from_plus, shift, 1), roll(from_minus, shift, 1))


def pack_y_kernel(from_minus, from_plus, low_in, high_in, token, sides, low_rows, high_rows, low, high):
    del token
    low[...] = low_in[...]
    high[...] = high_in[...]
    for t, part in enumerate((from_minus, from_plus)):
        sides[t] = part[...].astype(jnp.float32)
        low[pl.ds(100 + 2 * t, 2), :] = sides[t, 0:2, :]
        high[pl.ds(100 + 2 * t, 2), :] = sides[t, 30:32, :]
    low_rows[...] = low[...].astype(jnp.bfloat16)
    high_rows[...] = high[...].astype(jnp.bfloat16)


def own_kernel(pop, ori, after, own, token):
    token[...] = jnp.zeros(token.shape, jnp.float32)
    numbers = list(range(19))
    for x in range(2):
        for r in range(4):
            rows = pl.ds(8 * r, 8)
            f = [pop[i, x, rows, :] for i in numbers]
            rho, mom = moments(f, numbers)
            inv = 1.0 / rho
            u = [m * inv for m in mom]
            relaxed = relax(f, rho, u, numbers)
            for i in numbers:
                own[i, x, rows, :] = relaxed[i]
            for j in range(3):
                own[19 + j, x, rows, :] = u[j]
            for k in range(6):
                own[22 + k, x, rows, :] = ori[k, x, rows, :]


def collide_group(raw, fields, x, t, r):
    numbers = list(range(19))
    f = [raw(i) for i in numbers]
    rho, mom = moments(f, numbers)
    inv = 1.0 / rho
    u = [m * inv for m in mom]
    relaxed = relax(f, rho, u, numbers)
    for i in numbers:
        put(fields, (i, x, t), r, relaxed[i])
    for j in range(3):
        put(fields, (19 + j, x, t), r, u[j])
    for k in range(6):
        put(fields, (22 + k, x, t), r, raw(19 + k))


def advance_group(fields, state, out, x, r, low, high):
    lane, row = lanes_of(), rows_of()
    place = lambda f, xs=x: (lambda t: (f, xs, t))
    known = [{}, {}]
    for i in KNOWN[x]:
        xs = x - VELOCITIES[i][0]
        pair = stream(fields, place(i, xs), i, r, low, high, lambda i=i: get(fields, (opposite(i), x, 0), r))
        known[0][i], known[1][i] = pair
    grad = [[[None] * 3 for _ in range(3)] for _ in range(2)]
    sign = 0.5 if x == 0 else -0.5
    for j in range(3):
        by_y = central(fields, place(19 + j), r, 1, low, high, False)
        by_z = central(fields, place(19 + j), r, 2, low, high, False)
        for t in range(2):
            grad[t][j][0] = sign * get(fields, (19 + j, 1 - x, t), r)
            grad[t][j][1] = by_y[t]
            grad[t][j][2] = by_z[t]
    u = [[get(fields, (19 + j, x, t), r) for j in range(3)] for t in range(2)]
    a = [[get(fields, (22 + k, x, t), r) for k in range(6)] for t in range(2)]
    advect = [[], []]
    for k in range(6):
        by_y = central(fields, place(22 + k), r, 1, low, high, True)
        by_z = central(fields, place(22 + k), r, 2, low, high, True)
        for t in range(2):
            by_x = sign * get(fields, (22 + k, 1 - x, t), r)
            advect[t].append(u[t][0] * by_x + u[t][1] * by_y[t] + u[t][2] * by_z[t])
    side_pack = jnp.zeros((8, 128), jnp.float32)
    for t in range(2):
        rate = jeffery(a[t], grad[t])
        part = [a[t][k] + ORIENT_STEP * (rate[k] - advect[t][k]) for k in range(6)]
        rho, mom = moments(known[t], KNOWN[x])
        outward = [get(fields, (i, x, t), r) for i in TOWARD[x]]
        keep = [known[t][i] for i in KNOWN[x]] + [rho] + mom + part + u[t] + a[t] + outward
        for k in range(STATE):
            state[x, k, t, pl.ds(state_row(r), 8), :] = keep[k]
        wide = outward + u[t] + a[t] + [rho] + mom + [known[t][i] for i in TOWARD[x]]
        if t == 1:
            for k in range(MSG_WIDE):
                at = 4 * k
                side_pack = jnp.where((lane >= at) & (lane < at + 4), roll(wide[k], at + 2, 1), side_pack)
        elif r < 4:
            for k, v in enumerate(wide + part):
                out[x, pl.ds(field_row(k, r), 8), :] = v
        else:
            inner = (row >= 2) & (row < 6)
            for k in range(0, MSG_WIDE, 2):
                v = wide[k]
                if k + 1 < MSG_WIDE:
                    v = jnp.where(inner, roll(wide[k + 1], 4, 0), v)
                out[x, pl.ds(HALO_AT + 4 * k, 8), :] = v
    out[x, pl.ds(side_row(r), 8), :] = side_pack


def middle_kernel(own, sides, fields, state, message, out):
    low, high = walls()
    for x in range(2):
        for r in range(4):
            rows = pl.ds(8 * r, 8)
            for k in range(28):
                put(fields, (k, x, 0), r, own[k, x, rows, :])

            def raw(f):
                return unpack_z(sides[0, rows, :], sides[1, rows, :], 2 * f + x)

            collide_group(raw, fields, x, 1, r)
    for x in range(2):
        for r in (1, 2):
            advance_group(fields, state, out, x, r, low, high)
    message[...] = out[...].astype(jnp.bfloat16)


def step_one_kernel(before, middle, from_yminus, from_yplus, fields, state, msg_low, msg_high, halo, out, got):
    del before
    low, high = walls()
    got[0] = from_yminus[...].astype(jnp.float32)
    got[1] = from_yplus[...].astype(jnp.float32)
    for s in range(52):
        halo[s, 0:2, :] = got[1, pl.ds(2 * s, 2), :]
        halo[s, 6:8, :] = got[0, pl.ds(2 * s, 2), :]
    for x in range(2):
        for t in range(2):

            def raw(f):
                s = 2 * f + x
                return halo[s] if t == 0 else unpack_z(halo[50], halo[51], s)

            collide_group(raw, fields, x, t, 4)
    for x in range(2):
        for r in (0, 3, 4):
            advance_group(fields, state, out, x, r, low, high)
        out[x, pl.ds(CORNER_AT + 8, 8), :] = jnp.zeros((8, 128), jnp.float32)
    for x, msg in enumerate((msg_low, msg_high)):
        msg[0:MID_ROWS, :] = middle[x]
        msg[MID_ROWS:MSG_ROWS, :] = out[x, MID_ROWS:MSG_ROWS, :].astype(jnp.bfloat16)


def weights_kernel(
    w_in_hbm, b_in_hbm, w_mid_hbm, b_mid_hbm, w_out_hbm, b_out_hbm, w_one, w_two, bias_mid, w_three, bias_out,
    w_in, b_in, w_mid, b_mid, b_out, wide, sems,
):
    pairs = [
        (w_mid_hbm, w_mid),
        (w_in_hbm, w_in),
        (b_in_hbm, b_in),
        (b_mid_hbm, b_mid),
        (b_out_hbm, b_out),
        (w_out_hbm, w_three),
    ]
    for copy in fetch(pairs, sems):
        copy.wait()
    f32, bf16 = jnp.float32, jnp.bfloat16
    row = lax.broadcasted_iota(jnp.int32, (8, 512), 0)
    bias = jnp.broadcast_to(0.5 * b_in[...], (8, 512))
    first = bias.astype(bf16).astype(f32)
    rest = bias - first
    padded = jnp.concatenate([0.5 * w_in[...].astype(f32), jnp.zeros((2, 512), f32)], axis=0)
    stacked = jnp.where(row == 6, first, jnp.where(row == 7, rest, padded))
    w_one[...] = stacked.T.astype(bf16)
    w_two[...] = (0.5 * w_mid[...].astype(f32)).T.astype(bf16)
    bias_mid[...] = jnp.broadcast_to(jnp.broadcast_to(0.5 * b_mid[...], (8, 512)).T[:, 0:1], (512, 128))
    wide[...] = jnp.zeros(wide.shape, f32)
    wide[:, 0:15] = jnp.broadcast_to(b_out[...], (8, 15))
    bias_out[...] = jnp.broadcast_to(wide[...].T[0:16, 0:1], (16, 128))


def step_two_kernel(
    slots, state_mid, state_rim, from_low, from_high, w_one, w_mid, b_mid, w_out, b_out, flow, closure,
    got, fields, near, level, feats, spread, place,
):
    low, high = walls()
    got[0] = from_low[...].astype(jnp.float32)
    got[1] = from_high[...].astype(jnp.float32)
    for s in range(17):
        place[s] = 64
    for b in range(64):
        s = slots[b // 32, 0, b % 32]
        place[jnp.where(s >= 0, s, 16)] = b

    def arrived(x, k, t, r):
        if t == 0 and r < 4:
            return got[x, pl.ds(field_row(k, r), 8), :]
        if t == 0:
            v = got[x, pl.ds(HALO_AT + 8 * (k // 2), 8), :]
            return roll(v, 4, 0) if k % 2 else v
        v = got[x, pl.ds(side_row(r), 8), :]
        return roll(v, -(4 * k + 2), 1)

    def kept(x, k, t, r):
        part = state_mid if r in (1, 2) else state_rim
        return part[x, k, t, pl.ds(state_row(r), 8), :]

    for x in range(2):
        for t in range(2):
            for r in range(5):
                for k in range(5):
                    put(near, (x, k, t), r, arrived(x, k, t, r))
                    put(near, (x, 5 + k, t), r, kept(x, 33 + k, t, r))
    numbers = list(range(19))
    for x in range(2):
        come = TOWARD[1 - x]
        go = TOWARD[x]
        sign = -0.5 if x == 0 else 0.5
        for r in range(5):
            come_f, go_f = [{}, {}], [{}, {}]
            for k, i in enumerate(come):
                back = go.index(opposite(i))
                pair = stream(
                    near, lambda t, k=k: (x, k, t), i, r, low, high,
                    lambda back=back: get(near, (x, 5 + back, 0), r),
                )
                come_f[0][i], come_f[1][i] = pair
            for k, i in enumerate(go):
                back = come.index(opposite(i))
                pair = stream(
                    near, lambda t, k=k: (x, 5 + k, t), i, r, low, high,
                    lambda back=back: get(near, (x, back, 0), r),
                )
                go_f[0][i], go_f[1][i] = pair
            for t in range(2):
                f = {i: kept(x, k, t, r) for k, i in enumerate(KNOWN[x])}
                f.update(come_f[t])
                rho_new, mom_new = moments(come_f[t], come)
                rho = kept(x, 14, t, r) + rho_new
                mom = [kept(x, 15 + j, t, r) + mom_new[j] for j in range(3)]
                inv = 1.0 / rho
                u = [m * inv for m in mom]
                relaxed = relax(f, rho, u, numbers)
                for i in numbers:
                    put(fields, (i, x, t), r, relaxed[i])
                for j in range(3):
                    put(fields, (19 + j, x, t), r, u[j])
                u0 = [kept(x, 24 + j, t, r) for j in range(3)]
                a0 = [kept(x, 27 + k, t, r) for k in range(6)]
                u0n = [arrived(x, 5 + j, t, r) for j in range(3)]
                a0n = [arrived(x, 8 + k, t, r) for k in range(6)]
                rate = jeffery(a0, [[sign * u0n[j], None, None] for j in range(3)])
                drift = (sign * u0[0])
                for k in range(6):
                    a1 = kept(x, 18 + k, t, r) + ORIENT_STEP * (rate[k] - drift * a0n[k])
                    put(fields, (22 + k, x, t), r, a1)
                rho_new, mom_new = moments(go_f[t], go)
                rho = arrived(x, 14, t, r) + rho_new
                inv = 1.0 / rho
                u = [(arrived(x, 15 + j, t, r) + mom_new[j]) * inv for j in range(3)]
                f = {i: arrived(x, 18 + k, t, r) for k, i in enumerate(come)}
                relaxed = relax(f, rho, u, come)
                for k, i in enumerate(come):
                    put(fields, (28 + k, x, t), r, relaxed[i])
                if t == 0 and r < 4:
                    rate = jeffery(a0n, [[-sign * u0[j], None, None] for j in range(3)])
                    drift = -sign * u0n[0]
                    for j in range(3):
                        level[x, j, pl.ds(8 * r, 8), :] = u[j]
                    for k in range(6):
                        a1 = arrived(x, 23 + k, t, r) + ORIENT_STEP * (rate[k] - drift * a0[k])
                        level[x, 3 + k, pl.ds(8 * r, 8), :] = a1

    feats[...] = jnp.ones(feats.shape, jnp.float32)
    for x in range(2):
        for r in range(4):
            f = {}
            for i in numbers:
                xs = x - VELOCITIES[i][0]
                if 0 <= xs <= 1:
                    at_of = lambda t, i=i, xs=xs: (i, xs, t)
                else:
                    k = TOWARD[1 - x].index(i)
                    at_of = lambda t, k=k: (28 + k, x, t)
                f[i], _ = stream(
                    fields, at_of, i, r, low, high, lambda i=i: get(fields, (opposite(i), x, 0), r), False
                )
            rho, mom = moments(f, numbers)
            inv = 1.0 / rho
            final = [rho] + [m * inv for m in mom]
            for k in range(4):
                spread[pl.ds(k * 64 + x * 32 + 8 * r, 8), :] = final[k]
            sign = -0.5 if x == 0 else 0.5
            by_x = lambda k, n: sign * (level[x, n, pl.ds(8 * r, 8), :] - get(fields, (k, 1 - x, 0), r))
            grad = [[None] * 3 for _ in range(3)]
            for j in range(3):
                place_u = lambda t, j=j: (19 + j, x, t)
                grad[j][0] = by_x(19 + j, j)
                grad[j][1] = central(fields, place_u, r, 1, low, high, False, False)[0]
                grad[j][2] = central(fields, place_u, r, 2, low, high, False, False)[0]
            u = [get(fields, (19 + j, x, 0), r) for j in range(3)]
            a = [get(fields, (22 + k, x, 0), r) for k in range(6)]
            rate = jeffery(a, grad)
            for k in range(6):
                place_a = lambda t, k=k: (22 + k, x, t)
                advect = (
                    u[0] * by_x(22 + k, 3 + k)
                    + u[1] * central(fields, place_a, r, 1, low, high, True, False)[0]
                    + u[2] * central(fields, place_a, r, 2, low, high, True, False)[0]
                )
                new = a[k] + ORIENT_STEP * (rate[k] - advect)
                feats[pl.ds((x * 32 + 8 * r) * 8 + k, 8, 8), :] = new
    for k in range(4):
        for x in range(2):
            flow[k, x] = spread[pl.ds(k * 64 + x * 32, 32), :].astype(jnp.bfloat16)

    spread[...] = jnp.zeros(spread.shape, jnp.float32)
    group = 8
    bias_mid = jnp.concatenate([b_mid[...]] * group, axis=1)
    for g in range(16 // group):
        at = [place[g * group + k] for k in range(group)]
        cells = [feats[pl.ds(pl.multiple_of(b * 8, 8), 8), :] for b in at]
        cells = jnp.concatenate(cells, axis=1).astype(jnp.bfloat16)
        v = jnp.dot(w_one[...], cells, preferred_element_type=jnp.float32)
        h = (v + v * jnp.tanh(v)).astype(jnp.bfloat16)
        v = jnp.dot(w_mid[...], h, preferred_element_type=jnp.float32) + bias_mid
        h = (v + v * jnp.tanh(v)).astype(jnp.bfloat16)
        v = jnp.dot(w_out[...], h, preferred_element_type=jnp.float32)
        for k in range(group):
            spread[pl.ds(pl.multiple_of(at[k] * 16, 16), 15), :] = v[:, 128 * k : 128 * k + 128] + b_out[0:15, :]
    for c in range(15):
        for x in range(2):
            closure[c, x] = spread[pl.ds(x * 512 + c, 32, 16), :].astype(jnp.bfloat16)


def local(populations, orientation, slot_table, w_in, b_in, w_mid, b_mid, w_out, b_out):
    f32, bf16 = jnp.float32, jnp.bfloat16
    shape = lambda *s, d=f32: jax.ShapeDtypeStruct(s, d)
    vmem = pl.BlockSpec(memory_space=pltpu.VMEM)
    smem = pl.BlockSpec(memory_space=pltpu.SMEM)
    params = pltpu.CompilerParams(vmem_limit_bytes=24 * MIB)

    def ring(axis, step, wrap):
        n = lax.axis_size(axis)
        return [(i, (i + step) % n) for i in range(n) if wrap or 0 <= i + step < n]

    hbm = pl.BlockSpec(memory_space=pltpu.HBM)
    slots = jnp.transpose(slot_table, (0, 2, 1))
    w_one, w_two, bias_mid, w_three, bias_out = pl.pallas_call(
        weights_kernel,
        out_shape=(
            shape(512, 8, d=bf16),
            shape(512, 512, d=bf16),
            shape(512, 128),
            shape(15, 512, d=bf16),
            shape(16, 128),
        ),
        in_specs=[hbm] * 6,
        out_specs=(vmem,) * 5,
        scratch_shapes=[
            pltpu.VMEM((6, 512), bf16),
            pltpu.VMEM((1, 512), f32),
            pltpu.VMEM((512, 512), bf16),
            pltpu.VMEM((1, 512), f32),
            pltpu.VMEM((1, 15), f32),
            pltpu.VMEM((8, 128), f32),
            pltpu.SemaphoreType.DMA((6,)),
        ],
        compiler_params=pltpu.CompilerParams(vmem_limit_bytes=LIMIT_WEIGHTS),
    )(w_in, b_in.reshape(1, 512), w_mid, b_mid.reshape(1, 512), w_out.T, b_out.reshape(1, 15))
    zlow, zhigh, low_raw, high_raw = pl.pallas_call(
        pack_z_kernel,
        out_shape=(shape(32, 128, d=bf16), shape(32, 128, d=bf16), shape(112, 128), shape(112, 128)),
        in_specs=[hbm] * 2,
        out_specs=(vmem,) * 4,
        scratch_shapes=[
            pltpu.VMEM((19, 2, 32, 128), f32),
            pltpu.VMEM((6, 2, 32, 128), f32),
            pltpu.SemaphoreType.DMA((5,)),
        ],
        compiler_params=pltpu.CompilerParams(vmem_limit_bytes=LIMIT_PACK),
        cost_estimate=COST_PACK,
    )(populations, orientation)
    own, token = pl.pallas_call(
        own_kernel,
        out_shape=(shape(28, 2, 32, 128), shape(8, 128)),
        in_specs=[vmem] * 3,
        out_specs=(vmem,) * 2,
        compiler_params=params,
    )(populations, orientation, low_raw)
    from_minus = lax.ppermute(zhigh, "gz", ring("gz", 1, False))
    from_plus = lax.ppermute(zlow, "gz", ring("gz", -1, False))
    sides, low_rows, high_rows = pl.pallas_call(
        pack_y_kernel,
        out_shape=(shape(2, 32, 128), shape(112, 128, d=bf16), shape(112, 128, d=bf16)),
        in_specs=[vmem] * 5,
        out_specs=(vmem,) * 3,
        scratch_shapes=[pltpu.VMEM((112, 128), f32), pltpu.VMEM((112, 128), f32)],
        compiler_params=params,
    )(from_minus, from_plus, low_raw, high_raw, token)
    fields_shape = shape(28, 2, 2, 64, 128)
    fields, state_mid, middle = pl.pallas_call(
        middle_kernel,
        out_shape=(fields_shape, shape(2, STATE, 2, 16, 128), shape(2, MID_ROWS, 128, d=bf16)),
        in_specs=[vmem] * 2,
        out_specs=(vmem,) * 3,
        scratch_shapes=[pltpu.VMEM((2, MID_ROWS, 128), f32)],
        compiler_params=params,
    )(own, sides)
    from_yminus = lax.ppermute(high_rows, "gy", ring("gy", 1, True))
    from_yplus = lax.ppermute(low_rows, "gy", ring("gy", -1, True))
    fields, state_rim, msg_low, msg_high = pl.pallas_call(
        step_one_kernel,
        out_shape=(
            fields_shape,
            shape(2, STATE, 2, 24, 128),
            shape(MSG_ROWS, 128, d=bf16),
            shape(MSG_ROWS, 128, d=bf16),
        ),
        in_specs=[vmem] * 4,
        out_specs=(vmem,) * 4,
        scratch_shapes=[
            pltpu.VMEM((52, 8, 128), f32),
            pltpu.VMEM((2, MSG_ROWS, 128), f32),
            pltpu.VMEM((2, 112, 128), f32),
        ],
        input_output_aliases={0: 0},
        compiler_params=params,
    )(fields, middle, from_yminus, from_yplus)
    from_low = lax.ppermute(msg_high, "gx", ring("gx", 1, True))
    from_high = lax.ppermute(msg_low, "gx", ring("gx", -1, True))
    return pl.pallas_call(
        step_two_kernel,
        out_shape=(shape(4, 2, 32, 128, d=bf16), shape(15, 2, 32, 128, d=bf16)),
        in_specs=[smem] + [vmem] * 9,
        out_specs=(vmem,) * 2,
        scratch_shapes=[
            pltpu.VMEM((2, MSG_ROWS, 128), f32),
            pltpu.VMEM((33, 2, 2, 64, 128), f32),
            pltpu.VMEM((2, 10, 2, 64, 128), f32),
            pltpu.VMEM((2, 9, 32, 128), f32),
            pltpu.VMEM((65 * 8, 128), f32),
            pltpu.VMEM((65 * 16, 128), f32),
            pltpu.SMEM((17,), jnp.int32),
        ],
        compiler_params=params,
    )(slots, state_mid, state_rim, from_low, from_high, w_one, w_two, bias_mid, w_three, bias_out)


def solution(mesh):
    grid = P(None, "gx", "gy", "gz")
    in_specs = (grid, grid, P("gx", "gy", "gz"), P(), P(), P(), P(), P(), P())
    return jax.shard_map(local, mesh=mesh, in_specs=in_specs, out_specs=(grid, grid), check_vma=False)
```

```python
import functools

import jax
import jax.numpy as jnp
from jax import lax
from jax.experimental import pallas as pl
from jax.experimental.pallas import tpu as pltpu
from jax.sharding import PartitionSpec as P


VELOCITIES = [
    (0, 0, 0),
    (1, 0, 0),
    (-1, 0, 0),
    (0, 1, 0),
    (0, -1, 0),
    (0, 0, 1),
    (0, 0, -1),
    (1, 1, 0),
    (-1, -1, 0),
    (1, -1, 0),
    (-1, 1, 0),
    (1, 0, 1),
    (-1, 0, -1),
    (1, 0, -1),
    (-1, 0, 1),
    (0, 1, 1),
    (0, -1, -1),
    (0, 1, -1),
    (0, -1, 1),
]
WEIGHTS = [1.0 / 3.0] + [1.0 / 18.0] * 6 + [1.0 / 36.0] * 12
OMEGA = 1.0 / 0.8
SHAPE_FACTOR = 0.95
ORIENT_STEP = 4.0
PAIRS = [(0, 0), (1, 1), (2, 2), (0, 1), (0, 2), (1, 2)]
ENTRY = [[0, 3, 4], [3, 1, 5], [4, 5, 2]]
TOWARD = {
    0: [i for i in range(19) if VELOCITIES[i][0] == -1],
    1: [i for i in range(19) if VELOCITIES[i][0] == 1],
}
KNOWN = {0: [i for i in range(19) if VELOCITIES[i][0] != 1], 1: [i for i in range(19) if VELOCITIES[i][0] != -1]}
MSG_WIDE = 23
MSG_ROWS = 1072
MID_ROWS = 480
SIDE_MID = 464
RIM_AT = 480
HALO_AT = 944
SIDE_RIM = 1040
CORNER_AT = 1056
MIB = 1024 * 1024
LIMIT_PACK = 5375 * MIB // 100
COST_PACK = pl.CostEstimate(flops=10**10, bytes_accessed=10**7, transcendentals=0)
LIMIT_WEIGHTS = 4900 * MIB // 100
STATE = 38


def opposite(i):
    return 0 if i == 0 else (i + 1 if i % 2 == 1 else i - 1)


def lanes_of():
    return lax.broadcasted_iota(jnp.int32, (8, 128), 1)


def rows_of():
    return lax.broadcasted_iota(jnp.int32, (8, 128), 0)


def roll(v, shift, axis):
    shift = shift % v.shape[axis]
    return v if shift == 0 else pltpu.roll(v, shift, axis)


def add_all(terms):
    while len(terms) > 1:
        terms = [
            terms[k] + terms[k + 1] if k + 1 < len(terms) else terms[k] for k in range(0, len(terms), 2)
        ]
    return terms[0]


def moments(f, numbers):
    rho = add_all([f[i] for i in numbers])
    mom = []
    for ax in range(3):
        pos = [f[i] for i in numbers if VELOCITIES[i][ax] > 0]
        neg = [f[i] for i in numbers if VELOCITIES[i][ax] < 0]
        total = add_all(pos) if pos else None
        if neg:
            total = add_all(neg) * -1.0 if total is None else total - add_all(neg)
        mom.append(total)
    return rho, mom


def relax(f, rho, u, numbers):
    usq = 1.0 - 1.5 * (u[0] * u[0] + u[1] * u[1] + u[2] * u[2])
    scaled = {w: (w * OMEGA) * rho for w in sorted(set(WEIGHTS[i] for i in numbers))}
    out = {}
    for i in numbers:
        proj = None
        for ax in range(3):
            c = VELOCITIES[i][ax]
            if c != 0:
                if proj is None:
                    proj = u[ax] if c > 0 else -u[ax]
                else:
                    proj = proj + u[ax] if c > 0 else proj - u[ax]
        poly = usq if proj is None else usq + proj * (3.0 + 4.5 * proj)
        out[i] = f[i] * (1.0 - OMEGA) + scaled[WEIGHTS[i]] * poly
    return out


def plus(a, b):
    if a is None:
        return b
    if b is None:
        return a
    return a + b


def minus(a, b):
    if b is None:
        return a
    if a is None:
        return -b
    return a - b


def times(a, b):
    return None if a is None or b is None else a * b


def jeffery(a, g):
    half = [[None if g[j][k] is None else 0.5 * g[j][k] for k in range(3)] for j in range(3)]
    d = [[plus(half[j][k], half[k][j]) if j <= k else None for k in range(3)] for j in range(3)]
    w = [[minus(half[j][k], half[k][j]) if j < k else None for k in range(3)] for j in range(3)]
    full = lambda j, k: a[ENTRY[j][k]]
    strain = lambda j, k: d[min(j, k)][max(j, k)]

    def spin(j, k):
        if j == k:
            return None
        if j < k:
            return w[j][k]
        return None if w[k][j] is None else -w[k][j]

    contraction = None
    for j in range(3):
        contraction = plus(contraction, times(full(j, j), strain(j, j)))
    for j, k in ((0, 1), (0, 2), (1, 2)):
        cross = times(full(j, k), strain(j, k))
        contraction = plus(contraction, None if cross is None else 2.0 * cross)
    twice = 2.0 * contraction
    mix = [[plus(spin(j, k), times(strain(j, k), SHAPE_FACTOR)) for k in range(3)] for j in range(3)]
    z = [[None] * 3 for _ in range(3)]
    for j in range(3):
        for k in range(3):
            for m in range(3):
                z[j][k] = plus(z[j][k], times(full(j, m), mix[m][k]))
    scaled = SHAPE_FACTOR * twice
    return [plus(z[j][k], z[k][j]) - scaled * full(j, k) for j, k in PAIRS]


def field_row(k, r):
    return 16 * k + 8 * (r - 1) if r in (1, 2) else RIM_AT + 16 * k + 8 * (r // 3)


def side_row(r):
    return SIDE_MID + 8 * (r - 1) if r in (1, 2) else (CORNER_AT if r == 4 else SIDE_RIM + 8 * (r // 3))


def state_row(r):
    return {1: 0, 2: 8, 0: 0, 3: 8, 4: 16}[r]


def put(ref, at, r, v):
    if r < 4:
        ref[at + (pl.ds(16 + 8 * r, 8), slice(None))] = v
    else:
        ref[at + (pl.ds(8, 8), slice(None))] = v
        ref[at + (pl.ds(48, 8), slice(None))] = v


def get(ref, at, r, dy=0):
    if r < 4:
        return ref[at + (pl.ds(16 + 8 * r + dy, 8), slice(None))]
    if dy == 0:
        return ref[at + (pl.ds(48, 8), slice(None))]
    return jnp.where(
        rows_of() < 4,
        ref[at + (pl.ds(48 + dy, 8), slice(None))],
        ref[at + (pl.ds(8 + dy, 8), slice(None))],
    )


def pull_z(own, side, dz, want_side=True):
    if dz == 0:
        return own, side
    lane = lanes_of()
    own_r, side_r = roll(own, dz, 1), roll(side, dz, 1)
    edge = lane == (0 if dz > 0 else 127)
    return jnp.where(edge, side_r, own_r), jnp.where(edge, own_r, side_r) if want_side else None


def walls():
    layer = lax.axis_index("gz")
    last = lax.axis_size("gz") - 1
    lane = lanes_of()
    low = lane == jnp.where(layer == 0, 0, -1)
    high = lane == jnp.where(layer == last, 127, -1)
    return low, high


def wall_of(i, low, high):
    dz = VELOCITIES[i][2]
    return None if dz == 0 else (low if dz > 0 else high)


def stream(ref, at_of, i, r, low, high, reflected, want_side=True):
    _, cy, cz = VELOCITIES[i]
    own = get(ref, at_of(0), r, -cy)
    side = get(ref, at_of(1), r, -cy) if (want_side or cz != 0) else None
    if cz == 0:
        return own, side
    own, side = pull_z(own, side, cz, want_side)
    return jnp.where(wall_of(i, low, high), reflected(), own), side


def central(ref, at_of, r, axis, low, high, outside, want_side=True):
    if axis == 1:
        out = []
        for t in (0, 1) if want_side else (0,):
            out.append(0.5 * (get(ref, at_of(t), r, 1) - get(ref, at_of(t), r, -1)))
        return out
    own, side = get(ref, at_of(0), r), get(ref, at_of(1), r)
    behind, behind_side = pull_z(own, side, 1, want_side)
    ahead, ahead_side = pull_z(own, side, -1, want_side)
    past = own if outside else jnp.zeros_like(own)
    diff = 0.5 * (jnp.where(high, past, ahead) - jnp.where(low, past, behind))
    return [diff, 0.5 * (ahead_side - behind_side)] if want_side else [diff]


def fetch(pairs, sems):
    copies = [pltpu.make_async_copy(src, dst, sems.at[k]) for k, (src, dst) in enumerate(pairs)]
    for copy in copies:
        copy.start()
    return copies


PIECES = [(0, 5), (5, 10), (10, 15), (15, 19)]


def pack_z_kernel(pop_hbm, ori_hbm, zlow, zhigh, low_rows, high_rows, pop, ori, sems):
    pairs = [(pop_hbm.at[pl.ds(a, b - a)], pop.at[pl.ds(a, b - a)]) for a, b in PIECES]
    copies = fetch(pairs + [(ori_hbm, ori)], sems)
    starts = [a for a, _ in PIECES] + [19]
    lane = lax.broadcasted_iota(jnp.int32, (32, 128), 1)
    low = jnp.zeros((32, 128), jnp.float32)
    high = jnp.zeros((32, 128), jnp.float32)
    for f in range(25):
        if f in starts:
            copies[starts.index(f)].wait()
        src = pop if f < 19 else ori
        k = f if f < 19 else f - 19
        for x in range(2):
            s = 2 * f + x
            at = 2 * s
            v = roll(src[k, x], at + 2, 1)
            high = jnp.where((lane >= at) & (lane < at + 2), v, high)
            low = jnp.where((lane >= at + 2) & (lane < at + 4), v, low)
            low_rows[pl.ds(2 * s, 2), :] = src[k, x, 0:2, :]
            high_rows[pl.ds(2 * s, 2), :] = src[k, x, 30:32, :]
    zlow[...] = low.astype(jnp.bfloat16)
    zhigh[...] = high.astype(jnp.bfloat16)
    low_rows[100:112, :] = jnp.zeros((12, 128), jnp.float32)
    high_rows[100:112, :] = jnp.zeros((12, 128), jnp.float32)


def unpack_z(from_minus, from_plus, s):
    shift = -(2 * s + 2)
    return jnp.where(lanes_of() < 64, roll(from_plus, shift, 1), roll(from_minus, shift, 1))


def pack_y_kernel(from_minus, from_plus, low_in, high_in, token, sides, low_rows, high_rows, low, high):
    del token
    low[...] = low_in[...]
    high[...] = high_in[...]
    for t, part in enumerate((from_minus, from_plus)):
        sides[t] = part[...].astype(jnp.float32)
        low[pl.ds(100 + 2 * t, 2), :] = sides[t, 0:2, :]
        high[pl.ds(100 + 2 * t, 2), :] = sides[t, 30:32, :]
    low_rows[...] = low[...].astype(jnp.bfloat16)
    high_rows[...] = high[...].astype(jnp.bfloat16)


def own_kernel(pop, ori, after, own, token):
    token[...] = jnp.zeros(token.shape, jnp.float32)
    numbers = list(range(19))
    for x in range(2):
        for r in range(4):
            rows = pl.ds(8 * r, 8)
            f = [pop[i, x, rows, :] for i in numbers]
            rho, mom = moments(f, numbers)
            inv = 1.0 / rho
            u = [m * inv for m in mom]
            relaxed = relax(f, rho, u, numbers)
            for i in numbers:
                own[i, x, rows, :] = relaxed[i]
            for j in range(3):
                own[19 + j, x, rows, :] = u[j]
            for k in range(6):
                own[22 + k, x, rows, :] = ori[k, x, rows, :]


def collide_group(raw, fields, x, t, r):
    numbers = list(range(19))
    f = [raw(i) for i in numbers]
    rho, mom = moments(f, numbers)
    inv = 1.0 / rho
    u = [m * inv for m in mom]
    relaxed = relax(f, rho, u, numbers)
    for i in numbers:
        put(fields, (i, x, t), r, relaxed[i])
    for j in range(3):
        put(fields, (19 + j, x, t), r, u[j])
    for k in range(6):
        put(fields, (22 + k, x, t), r, raw(19 + k))


def advance_group(fields, state, out, x, r, low, high):
    lane, row = lanes_of(), rows_of()
    place = lambda f, xs=x: (lambda t: (f, xs, t))
    known = [{}, {}]
    for i in KNOWN[x]:
        xs = x - VELOCITIES[i][0]
        pair = stream(fields, place(i, xs), i, r, low, high, lambda i=i: get(fields, (opposite(i), x, 0), r))
        known[0][i], known[1][i] = pair
    grad = [[[None] * 3 for _ in range(3)] for _ in range(2)]
    sign = 0.5 if x == 0 else -0.5
    for j in range(3):
        by_y = central(fields, place(19 + j), r, 1, low, high, False)
        by_z = central(fields, place(19 + j), r, 2, low, high, False)
        for t in range(2):
            grad[t][j][0] = sign * get(fields, (19 + j, 1 - x, t), r)
            grad[t][j][1] = by_y[t]
            grad[t][j][2] = by_z[t]
    u = [[get(fields, (19 + j, x, t), r) for j in range(3)] for t in range(2)]
    a = [[get(fields, (22 + k, x, t), r) for k in range(6)] for t in range(2)]
    advect = [[], []]
    for k in range(6):
        by_y = central(fields, place(22 + k), r, 1, low, high, True)
        by_z = central(fields, place(22 + k), r, 2, low, high, True)
        for t in range(2):
            by_x = sign * get(fields, (22 + k, 1 - x, t), r)
            advect[t].append(u[t][0] * by_x + u[t][1] * by_y[t] + u[t][2] * by_z[t])
    side_pack = jnp.zeros((8, 128), jnp.float32)
    for t in range(2):
        rate = jeffery(a[t], grad[t])
        part = [a[t][k] + ORIENT_STEP * (rate[k] - advect[t][k]) for k in range(6)]
        rho, mom = moments(known[t], KNOWN[x])
        outward = [get(fields, (i, x, t), r) for i in TOWARD[x]]
        keep = [known[t][i] for i in KNOWN[x]] + [rho] + mom + part + u[t] + a[t] + outward
        for k in range(STATE):
            state[x, k, t, pl.ds(state_row(r), 8), :] = keep[k]
        wide = outward + u[t] + a[t] + [rho] + mom + [known[t][i] for i in TOWARD[x]]
        if t == 1:
            for k in range(MSG_WIDE):
                at = 4 * k
                side_pack = jnp.where((lane >= at) & (lane < at + 4), roll(wide[k], at + 2, 1), side_pack)
        elif r < 4:
            for k, v in enumerate(wide + part):
                out[x, pl.ds(field_row(k, r), 8), :] = v
        else:
            inner = (row >= 2) & (row < 6)
            for k in range(0, MSG_WIDE, 2):
                v = wide[k]
                if k + 1 < MSG_WIDE:
                    v = jnp.where(inner, roll(wide[k + 1], 4, 0), v)
                out[x, pl.ds(HALO_AT + 4 * k, 8), :] = v
    out[x, pl.ds(side_row(r), 8), :] = side_pack


def middle_kernel(own, sides, fields, state, message, out):
    low, high = walls()
    for x in range(2):
        for r in range(4):
            rows = pl.ds(8 * r, 8)
            for k in range(28):
                put(fields, (k, x, 0), r, own[k, x, rows, :])

            def raw(f):
                return unpack_z(sides[0, rows, :], sides[1, rows, :], 2 * f + x)

            collide_group(raw, fields, x, 1, r)
    for x in range(2):
        for r in (1, 2):
            advance_group(fields, state, out, x, r, low, high)
    message[...] = out[...].astype(jnp.bfloat16)


def step_one_kernel(before, middle, from_yminus, from_yplus, fields, state, msg_off, msg_on, halo, out, got):
    del before
    low, high = walls()
    got[0] = from_yminus[...].astype(jnp.float32)
    got[1] = from_yplus[...].astype(jnp.float32)
    for s in range(52):
        halo[s, 0:2, :] = got[1, pl.ds(2 * s, 2), :]
        halo[s, 6:8, :] = got[0, pl.ds(2 * s, 2), :]
    for x in range(2):
        for t in range(2):

            def raw(f):
                s = 2 * f + x
                return halo[s] if t == 0 else unpack_z(halo[50], halo[51], s)

            collide_group(raw, fields, x, t, 4)
    for x in range(2):
        for r in (0, 3, 4):
            advance_group(fields, state, out, x, r, low, high)
        out[x, pl.ds(CORNER_AT + 8, 8), :] = jnp.zeros((8, 128), jnp.float32)
    odd = lax.axis_index("gx") % 2
    for x, msg in ((odd, msg_off), (1 - odd, msg_on)):
        msg[0:MID_ROWS, :] = middle[x]
        msg[MID_ROWS:MSG_ROWS, :] = out[x, MID_ROWS:MSG_ROWS, :].astype(jnp.bfloat16)


def weights_kernel(
    w_in_hbm, b_in_hbm, w_mid_hbm, b_mid_hbm, w_out_hbm, b_out_hbm, w_one, w_two, bias_mid, w_three, bias_out,
    w_in, b_in, w_mid, b_mid, b_out, wide, sems,
):
    pairs = [
        (w_mid_hbm, w_mid),
        (w_in_hbm, w_in),
        (b_in_hbm, b_in),
        (b_mid_hbm, b_mid),
        (b_out_hbm, b_out),
        (w_out_hbm, w_three),
    ]
    for copy in fetch(pairs, sems):
        copy.wait()
    f32, bf16 = jnp.float32, jnp.bfloat16
    row = lax.broadcasted_iota(jnp.int32, (8, 512), 0)
    bias = jnp.broadcast_to(0.5 * b_in[...], (8, 512))
    first = bias.astype(bf16).astype(f32)
    rest = bias - first
    padded = jnp.concatenate([0.5 * w_in[...].astype(f32), jnp.zeros((2, 512), f32)], axis=0)
    stacked = jnp.where(row == 6, first, jnp.where(row == 7, rest, padded))
    w_one[...] = stacked.T.astype(bf16)
    w_two[...] = (0.5 * w_mid[...].astype(f32)).T.astype(bf16)
    bias_mid[...] = jnp.broadcast_to(jnp.broadcast_to(0.5 * b_mid[...], (8, 512)).T[:, 0:1], (512, 128))
    wide[...] = jnp.zeros(wide.shape, f32)
    wide[:, 0:15] = jnp.broadcast_to(b_out[...], (8, 15))
    bias_out[...] = jnp.broadcast_to(wide[...].T[0:16, 0:1], (16, 128))


def step_two_kernel(
    slots, state_mid, state_rim, from_off, from_on, w_one, w_mid, b_mid, w_out, b_out, flow, closure,
    got, fields, near, level, feats, spread, place,
):
    low, high = walls()
    odd = lax.axis_index("gx") % 2
    got[odd] = from_off[...].astype(jnp.float32)
    got[1 - odd] = from_on[...].astype(jnp.float32)
    for s in range(17):
        place[s] = 64
    for b in range(64):
        s = slots[b // 32, 0, b % 32]
        place[jnp.where(s >= 0, s, 16)] = b

    def arrived(x, k, t, r):
        if t == 0 and r < 4:
            return got[x, pl.ds(field_row(k, r), 8), :]
        if t == 0:
            v = got[x, pl.ds(HALO_AT + 8 * (k // 2), 8), :]
            return roll(v, 4, 0) if k % 2 else v
        v = got[x, pl.ds(side_row(r), 8), :]
        return roll(v, -(4 * k + 2), 1)

    def kept(x, k, t, r):
        part = state_mid if r in (1, 2) else state_rim
        return part[x, k, t, pl.ds(state_row(r), 8), :]

    for x in range(2):
        for t in range(2):
            for r in range(5):
                for k in range(5):
                    put(near, (x, k, t), r, arrived(x, k, t, r))
                    put(near, (x, 5 + k, t), r, kept(x, 33 + k, t, r))
    numbers = list(range(19))
    for x in range(2):
        come = TOWARD[1 - x]
        go = TOWARD[x]
        sign = -0.5 if x == 0 else 0.5
        for r in range(5):
            come_f, go_f = [{}, {}], [{}, {}]
            for k, i in enumerate(come):
                back = go.index(opposite(i))
                pair = stream(
                    near, lambda t, k=k: (x, k, t), i, r, low, high,
                    lambda back=back: get(near, (x, 5 + back, 0), r),
                )
                come_f[0][i], come_f[1][i] = pair
            for k, i in enumerate(go):
                back = come.index(opposite(i))
                pair = stream(
                    near, lambda t, k=k: (x, 5 + k, t), i, r, low, high,
                    lambda back=back: get(near, (x, back, 0), r),
                )
                go_f[0][i], go_f[1][i] = pair
            for t in range(2):
                f = {i: kept(x, k, t, r) for k, i in enumerate(KNOWN[x])}
                f.update(come_f[t])
                rho_new, mom_new = moments(come_f[t], come)
                rho = kept(x, 14, t, r) + rho_new
                mom = [kept(x, 15 + j, t, r) + mom_new[j] for j in range(3)]
                inv = 1.0 / rho
                u = [m * inv for m in mom]
                relaxed = relax(f, rho, u, numbers)
                for i in numbers:
                    put(fields, (i, x, t), r, relaxed[i])
                for j in range(3):
                    put(fields, (19 + j, x, t), r, u[j])
                u0 = [kept(x, 24 + j, t, r) for j in range(3)]
                a0 = [kept(x, 27 + k, t, r) for k in range(6)]
                u0n = [arrived(x, 5 + j, t, r) for j in range(3)]
                a0n = [arrived(x, 8 + k, t, r) for k in range(6)]
                rate = jeffery(a0, [[sign * u0n[j], None, None] for j in range(3)])
                drift = (sign * u0[0])
                for k in range(6):
                    a1 = kept(x, 18 + k, t, r) + ORIENT_STEP * (rate[k] - drift * a0n[k])
                    put(fields, (22 + k, x, t), r, a1)
                rho_new, mom_new = moments(go_f[t], go)
                rho = arrived(x, 14, t, r) + rho_new
                inv = 1.0 / rho
                u = [(arrived(x, 15 + j, t, r) + mom_new[j]) * inv for j in range(3)]
                f = {i: arrived(x, 18 + k, t, r) for k, i in enumerate(come)}
                relaxed = relax(f, rho, u, come)
                for k, i in enumerate(come):
                    put(fields, (28 + k, x, t), r, relaxed[i])
                if t == 0 and r < 4:
                    rate = jeffery(a0n, [[-sign * u0[j], None, None] for j in range(3)])
                    drift = -sign * u0n[0]
                    for j in range(3):
                        level[x, j, pl.ds(8 * r, 8), :] = u[j]
                    for k in range(6):
                        a1 = arrived(x, 23 + k, t, r) + ORIENT_STEP * (rate[k] - drift * a0[k])
                        level[x, 3 + k, pl.ds(8 * r, 8), :] = a1

    feats[...] = jnp.ones(feats.shape, jnp.float32)
    for x in range(2):
        for r in range(4):
            f = {}
            for i in numbers:
                xs = x - VELOCITIES[i][0]
                if 0 <= xs <= 1:
                    at_of = lambda t, i=i, xs=xs: (i, xs, t)
                else:
                    k = TOWARD[1 - x].index(i)
                    at_of = lambda t, k=k: (28 + k, x, t)
                f[i], _ = stream(
                    fields, at_of, i, r, low, high, lambda i=i: get(fields, (opposite(i), x, 0), r), False
                )
            rho, mom = moments(f, numbers)
            inv = 1.0 / rho
            final = [rho] + [m * inv for m in mom]
            for k in range(4):
                spread[pl.ds(k * 64 + x * 32 + 8 * r, 8), :] = final[k]
            sign = -0.5 if x == 0 else 0.5
            by_x = lambda k, n: sign * (level[x, n, pl.ds(8 * r, 8), :] - get(fields, (k, 1 - x, 0), r))
            grad = [[None] * 3 for _ in range(3)]
            for j in range(3):
                place_u = lambda t, j=j: (19 + j, x, t)
                grad[j][0] = by_x(19 + j, j)
                grad[j][1] = central(fields, place_u, r, 1, low, high, False, False)[0]
                grad[j][2] = central(fields, place_u, r, 2, low, high, False, False)[0]
            u = [get(fields, (19 + j, x, 0), r) for j in range(3)]
            a = [get(fields, (22 + k, x, 0), r) for k in range(6)]
            rate = jeffery(a, grad)
            for k in range(6):
                place_a = lambda t, k=k: (22 + k, x, t)
                advect = (
                    u[0] * by_x(22 + k, 3 + k)
                    + u[1] * central(fields, place_a, r, 1, low, high, True, False)[0]
                    + u[2] * central(fields, place_a, r, 2, low, high, True, False)[0]
                )
                new = a[k] + ORIENT_STEP * (rate[k] - advect)
                feats[pl.ds((x * 32 + 8 * r) * 8 + k, 8, 8), :] = new
    for k in range(4):
        for x in range(2):
            flow[k, x] = spread[pl.ds(k * 64 + x * 32, 32), :].astype(jnp.bfloat16)

    spread[...] = jnp.zeros(spread.shape, jnp.float32)
    group = 8
    bias_mid = jnp.concatenate([b_mid[...]] * group, axis=1)
    for g in range(16 // group):
        at = [place[g * group + k] for k in range(group)]
        cells = [feats[pl.ds(pl.multiple_of(b * 8, 8), 8), :] for b in at]
        cells = jnp.concatenate(cells, axis=1).astype(jnp.bfloat16)
        v = jnp.dot(w_one[...], cells, preferred_element_type=jnp.float32)
        h = (v + v * jnp.tanh(v)).astype(jnp.bfloat16)
        v = jnp.dot(w_mid[...], h, preferred_element_type=jnp.float32) + bias_mid
        h = (v + v * jnp.tanh(v)).astype(jnp.bfloat16)
        v = jnp.dot(w_out[...], h, preferred_element_type=jnp.float32)
        for k in range(group):
            spread[pl.ds(pl.multiple_of(at[k] * 16, 16), 15), :] = v[:, 128 * k : 128 * k + 128] + b_out[0:15, :]
    for c in range(15):
        for x in range(2):
            closure[c, x] = spread[pl.ds(x * 512 + c, 32, 16), :].astype(jnp.bfloat16)


def local(populations, orientation, slot_table, w_in, b_in, w_mid, b_mid, w_out, b_out):
    f32, bf16 = jnp.float32, jnp.bfloat16
    shape = lambda *s, d=f32: jax.ShapeDtypeStruct(s, d)
    vmem = pl.BlockSpec(memory_space=pltpu.VMEM)
    smem = pl.BlockSpec(memory_space=pltpu.SMEM)
    params = pltpu.CompilerParams(vmem_limit_bytes=24 * MIB)

    def ring(axis, step, wrap):
        n = lax.axis_size(axis)
        return [(i, (i + step) % n) for i in range(n) if wrap or 0 <= i + step < n]

    hbm = pl.BlockSpec(memory_space=pltpu.HBM)
    slots = jnp.transpose(slot_table, (0, 2, 1))
    w_one, w_two, bias_mid, w_three, bias_out = pl.pallas_call(
        weights_kernel,
        out_shape=(
            shape(512, 8, d=bf16),
            shape(512, 512, d=bf16),
            shape(512, 128),
            shape(15, 512, d=bf16),
            shape(16, 128),
        ),
        in_specs=[hbm] * 6,
        out_specs=(vmem,) * 5,
        scratch_shapes=[
            pltpu.VMEM((6, 512), bf16),
            pltpu.VMEM((1, 512), f32),
            pltpu.VMEM((512, 512), bf16),
            pltpu.VMEM((1, 512), f32),
            pltpu.VMEM((1, 15), f32),
            pltpu.VMEM((8, 128), f32),
            pltpu.SemaphoreType.DMA((6,)),
        ],
        compiler_params=pltpu.CompilerParams(vmem_limit_bytes=LIMIT_WEIGHTS),
    )(w_in, b_in.reshape(1, 512), w_mid, b_mid.reshape(1, 512), w_out.T, b_out.reshape(1, 15))
    zlow, zhigh, low_raw, high_raw = pl.pallas_call(
        pack_z_kernel,
        out_shape=(shape(32, 128, d=bf16), shape(32, 128, d=bf16), shape(112, 128), shape(112, 128)),
        in_specs=[hbm] * 2,
        out_specs=(vmem,) * 4,
        scratch_shapes=[
            pltpu.VMEM((19, 2, 32, 128), f32),
            pltpu.VMEM((6, 2, 32, 128), f32),
            pltpu.SemaphoreType.DMA((5,)),
        ],
        compiler_params=pltpu.CompilerParams(vmem_limit_bytes=LIMIT_PACK),
        cost_estimate=COST_PACK,
    )(populations, orientation)
    own, token = pl.pallas_call(
        own_kernel,
        out_shape=(shape(28, 2, 32, 128), shape(8, 128)),
        in_specs=[vmem] * 3,
        out_specs=(vmem,) * 2,
        compiler_params=params,
    )(populations, orientation, low_raw)
    from_minus = lax.ppermute(zhigh, "gz", ring("gz", 1, False))
    from_plus = lax.ppermute(zlow, "gz", ring("gz", -1, False))
    sides, low_rows, high_rows = pl.pallas_call(
        pack_y_kernel,
        out_shape=(shape(2, 32, 128), shape(112, 128, d=bf16), shape(112, 128, d=bf16)),
        in_specs=[vmem] * 5,
        out_specs=(vmem,) * 3,
        scratch_shapes=[pltpu.VMEM((112, 128), f32), pltpu.VMEM((112, 128), f32)],
        compiler_params=params,
    )(from_minus, from_plus, low_raw, high_raw, token)
    fields_shape = shape(28, 2, 2, 64, 128)
    fields, state_mid, middle = pl.pallas_call(
        middle_kernel,
        out_shape=(fields_shape, shape(2, STATE, 2, 16, 128), shape(2, MID_ROWS, 128, d=bf16)),
        in_specs=[vmem] * 2,
        out_specs=(vmem,) * 3,
        scratch_shapes=[pltpu.VMEM((2, MID_ROWS, 128), f32)],
        compiler_params=params,
    )(own, sides)
    from_yminus = lax.ppermute(high_rows, "gy", ring("gy", 1, True))
    from_yplus = lax.ppermute(low_rows, "gy", ring("gy", -1, True))
    fields, state_rim, msg_off, msg_on = pl.pallas_call(
        step_one_kernel,
        out_shape=(
            fields_shape,
            shape(2, STATE, 2, 24, 128),
            shape(MSG_ROWS, 128, d=bf16),
            shape(MSG_ROWS, 128, d=bf16),
        ),
        in_specs=[vmem] * 4,
        out_specs=(vmem,) * 4,
        scratch_shapes=[
            pltpu.VMEM((52, 8, 128), f32),
            pltpu.VMEM((2, MSG_ROWS, 128), f32),
            pltpu.VMEM((2, 112, 128), f32),
        ],
        input_output_aliases={0: 0},
        compiler_params=params,
    )(fields, middle, from_yminus, from_yplus)
    x_count = lax.axis_size("gx")
    off_chip = [(i, (i + (1 if i % 2 else -1)) % x_count) for i in range(x_count)]
    on_chip = [(i, i + (-1 if i % 2 else 1)) for i in range(x_count)]
    from_on = lax.ppermute(msg_on, "gx", on_chip)
    from_off = lax.ppermute(msg_off, "gx", off_chip)
    return pl.pallas_call(
        step_two_kernel,
        out_shape=(shape(4, 2, 32, 128, d=bf16), shape(15, 2, 32, 128, d=bf16)),
        in_specs=[smem] + [vmem] * 9,
        out_specs=(vmem,) * 2,
        scratch_shapes=[
            pltpu.VMEM((2, MSG_ROWS, 128), f32),
            pltpu.VMEM((33, 2, 2, 64, 128), f32),
            pltpu.VMEM((2, 10, 2, 64, 128), f32),
            pltpu.VMEM((2, 9, 32, 128), f32),
            pltpu.VMEM((65 * 8, 128), f32),
            pltpu.VMEM((65 * 16, 128), f32),
            pltpu.SMEM((17,), jnp.int32),
        ],
        compiler_params=params,
    )(slots, state_mid, state_rim, from_off, from_on, w_one, w_two, bias_mid, w_three, bias_out)


def solution(mesh):
    grid = P(None, "gx", "gy", "gz")
    in_specs = (grid, grid, P("gx", "gy", "gz"), P(), P(), P(), P(), P(), P())
    return jax.shard_map(local, mesh=mesh, in_specs=in_specs, out_specs=(grid, grid), check_vma=False)
```

```python
import functools

import jax
import jax.numpy as jnp
from jax import lax
from jax.experimental import pallas as pl
from jax.experimental.pallas import tpu as pltpu
from jax.sharding import PartitionSpec as P


VELOCITIES = [
    (0, 0, 0),
    (1, 0, 0),
    (-1, 0, 0),
    (0, 1, 0),
    (0, -1, 0),
    (0, 0, 1),
    (0, 0, -1),
    (1, 1, 0),
    (-1, -1, 0),
    (1, -1, 0),
    (-1, 1, 0),
    (1, 0, 1),
    (-1, 0, -1),
    (1, 0, -1),
    (-1, 0, 1),
    (0, 1, 1),
    (0, -1, -1),
    (0, 1, -1),
    (0, -1, 1),
]
WEIGHTS = [1.0 / 3.0] + [1.0 / 18.0] * 6 + [1.0 / 36.0] * 12
OMEGA = 1.0 / 0.8
SHAPE_FACTOR = 0.95
ORIENT_STEP = 4.0
PAIRS = [(0, 0), (1, 1), (2, 2), (0, 1), (0, 2), (1, 2)]
ENTRY = [[0, 3, 4], [3, 1, 5], [4, 5, 2]]
TOWARD = {
    0: [i for i in range(19) if VELOCITIES[i][0] == -1],
    1: [i for i in range(19) if VELOCITIES[i][0] == 1],
}
KNOWN = {0: [i for i in range(19) if VELOCITIES[i][0] != 1], 1: [i for i in range(19) if VELOCITIES[i][0] != -1]}
MSG_WIDE = 23
MSG_ROWS = 1072
MID_ROWS = 480
SIDE_MID = 464
RIM_AT = 480
HALO_AT = 944
SIDE_RIM = 1040
CORNER_AT = 1056
MIB = 1024 * 1024
LIMIT_PACK = 5375 * MIB // 100
COST_PACK = pl.CostEstimate(flops=10**10, bytes_accessed=10**7, transcendentals=0)
LIMIT_WEIGHTS = 4900 * MIB // 100
STATE = 38


def opposite(i):
    return 0 if i == 0 else (i + 1 if i % 2 == 1 else i - 1)


def lanes_of():
    return lax.broadcasted_iota(jnp.int32, (8, 128), 1)


def rows_of():
    return lax.broadcasted_iota(jnp.int32, (8, 128), 0)


def roll(v, shift, axis):
    shift = shift % v.shape[axis]
    return v if shift == 0 else pltpu.roll(v, shift, axis)


def add_all(terms):
    while len(terms) > 1:
        terms = [
            terms[k] + terms[k + 1] if k + 1 < len(terms) else terms[k] for k in range(0, len(terms), 2)
        ]
    return terms[0]


def moments(f, numbers):
    rho = add_all([f[i] for i in numbers])
    mom = []
    for ax in range(3):
        pos = [f[i] for i in numbers if VELOCITIES[i][ax] > 0]
        neg = [f[i] for i in numbers if VELOCITIES[i][ax] < 0]
        total = add_all(pos) if pos else None
        if neg:
            total = add_all(neg) * -1.0 if total is None else total - add_all(neg)
        mom.append(total)
    return rho, mom


def relax(f, rho, u, numbers):
    usq = 1.0 - 1.5 * (u[0] * u[0] + u[1] * u[1] + u[2] * u[2])
    scaled = {w: (w * OMEGA) * rho for w in sorted(set(WEIGHTS[i] for i in numbers))}
    out = {}
    for i in numbers:
        proj = None
        for ax in range(3):
            c = VELOCITIES[i][ax]
            if c != 0:
                if proj is None:
                    proj = u[ax] if c > 0 else -u[ax]
                else:
                    proj = proj + u[ax] if c > 0 else proj - u[ax]
        poly = usq if proj is None else usq + proj * (3.0 + 4.5 * proj)
        out[i] = f[i] * (1.0 - OMEGA) + scaled[WEIGHTS[i]] * poly
    return out


def plus(a, b):
    if a is None:
        return b
    if b is None:
        return a
    return a + b


def minus(a, b):
    if b is None:
        return a
    if a is None:
        return -b
    return a - b


def times(a, b):
    return None if a is None or b is None else a * b


def jeffery(a, g):
    half = [[None if g[j][k] is None else 0.5 * g[j][k] for k in range(3)] for j in range(3)]
    d = [[plus(half[j][k], half[k][j]) if j <= k else None for k in range(3)] for j in range(3)]
    w = [[minus(half[j][k], half[k][j]) if j < k else None for k in range(3)] for j in range(3)]
    full = lambda j, k: a[ENTRY[j][k]]
    strain = lambda j, k: d[min(j, k)][max(j, k)]

    def spin(j, k):
        if j == k:
            return None
        if j < k:
            return w[j][k]
        return None if w[k][j] is None else -w[k][j]

    contraction = None
    for j in range(3):
        contraction = plus(contraction, times(full(j, j), strain(j, j)))
    for j, k in ((0, 1), (0, 2), (1, 2)):
        cross = times(full(j, k), strain(j, k))
        contraction = plus(contraction, None if cross is None else 2.0 * cross)
    twice = 2.0 * contraction
    mix = [[plus(spin(j, k), times(strain(j, k), SHAPE_FACTOR)) for k in range(3)] for j in range(3)]
    z = [[None] * 3 for _ in range(3)]
    for j in range(3):
        for k in range(3):
            for m in range(3):
                z[j][k] = plus(z[j][k], times(full(j, m), mix[m][k]))
    scaled = SHAPE_FACTOR * twice
    return [plus(z[j][k], z[k][j]) - scaled * full(j, k) for j, k in PAIRS]


def field_row(k, r):
    return 16 * k + 8 * (r - 1) if r in (1, 2) else RIM_AT + 16 * k + 8 * (r // 3)


def side_row(r):
    return SIDE_MID + 8 * (r - 1) if r in (1, 2) else (CORNER_AT if r == 4 else SIDE_RIM + 8 * (r // 3))


def state_row(r):
    return {1: 0, 2: 8, 0: 0, 3: 8, 4: 16}[r]


def put(ref, at, r, v):
    if r < 4:
        ref[at + (pl.ds(16 + 8 * r, 8), slice(None))] = v
    else:
        ref[at + (pl.ds(8, 8), slice(None))] = v
        ref[at + (pl.ds(48, 8), slice(None))] = v


def get(ref, at, r, dy=0):
    if r < 4:
        return ref[at + (pl.ds(16 + 8 * r + dy, 8), slice(None))]
    if dy == 0:
        return ref[at + (pl.ds(48, 8), slice(None))]
    return jnp.where(
        rows_of() < 4,
        ref[at + (pl.ds(48 + dy, 8), slice(None))],
        ref[at + (pl.ds(8 + dy, 8), slice(None))],
    )


def pull_z(own, side, dz, want_side=True):
    if dz == 0:
        return own, side
    lane = lanes_of()
    own_r, side_r = roll(own, dz, 1), roll(side, dz, 1)
    edge = lane == (0 if dz > 0 else 127)
    return jnp.where(edge, side_r, own_r), jnp.where(edge, own_r, side_r) if want_side else None


def walls():
    layer = lax.axis_index("gz")
    last = lax.axis_size("gz") - 1
    lane = lanes_of()
    low = lane == jnp.where(layer == 0, 0, -1)
    high = lane == jnp.where(layer == last, 127, -1)
    return low, high


def wall_of(i, low, high):
    dz = VELOCITIES[i][2]
    return None if dz == 0 else (low if dz > 0 else high)


def stream(ref, at_of, i, r, low, high, reflected, want_side=True):
    _, cy, cz = VELOCITIES[i]
    own = get(ref, at_of(0), r, -cy)
    side = get(ref, at_of(1), r, -cy) if (want_side or cz != 0) else None
    if cz == 0:
        return own, side
    own, side = pull_z(own, side, cz, want_side)
    return jnp.where(wall_of(i, low, high), reflected(), own), side


def central(ref, at_of, r, axis, low, high, outside, want_side=True):
    if axis == 1:
        out = []
        for t in (0, 1) if want_side else (0,):
            out.append(0.5 * (get(ref, at_of(t), r, 1) - get(ref, at_of(t), r, -1)))
        return out
    own, side = get(ref, at_of(0), r), get(ref, at_of(1), r)
    behind, behind_side = pull_z(own, side, 1, want_side)
    ahead, ahead_side = pull_z(own, side, -1, want_side)
    past = own if outside else jnp.zeros_like(own)
    diff = 0.5 * (jnp.where(high, past, ahead) - jnp.where(low, past, behind))
    return [diff, 0.5 * (ahead_side - behind_side)] if want_side else [diff]


def fetch(pairs, sems):
    copies = [pltpu.make_async_copy(src, dst, sems.at[k]) for k, (src, dst) in enumerate(pairs)]
    for copy in copies:
        copy.start()
    return copies


PIECES = [(0, 5), (5, 10), (10, 15), (15, 19)]


def pack_z_kernel(pop_hbm, ori_hbm, zlow, zhigh, low_rows, high_rows, pop, ori, sems):
    pairs = [(pop_hbm.at[pl.ds(a, b - a)], pop.at[pl.ds(a, b - a)]) for a, b in PIECES]
    copies = fetch(pairs + [(ori_hbm, ori)], sems)
    starts = [a for a, _ in PIECES] + [19]
    lane = lax.broadcasted_iota(jnp.int32, (32, 128), 1)
    low = jnp.zeros((32, 128), jnp.float32)
    high = jnp.zeros((32, 128), jnp.float32)
    for f in range(25):
        if f in starts:
            copies[starts.index(f)].wait()
        src = pop if f < 19 else ori
        k = f if f < 19 else f - 19
        for x in range(2):
            s = 2 * f + x
            at = 2 * s
            v = roll(src[k, x], at + 2, 1)
            high = jnp.where((lane >= at) & (lane < at + 2), v, high)
            low = jnp.where((lane >= at + 2) & (lane < at + 4), v, low)
            low_rows[pl.ds(2 * s, 2), :] = src[k, x, 0:2, :]
            high_rows[pl.ds(2 * s, 2), :] = src[k, x, 30:32, :]
    zlow[...] = low.astype(jnp.bfloat16)
    zhigh[...] = high.astype(jnp.bfloat16)
    low_rows[100:112, :] = jnp.zeros((12, 128), jnp.float32)
    high_rows[100:112, :] = jnp.zeros((12, 128), jnp.float32)


def unpack_z(from_minus, from_plus, s):
    shift = -(2 * s + 2)
    return jnp.where(lanes_of() < 64, roll(from_plus, shift, 1), roll(from_minus, shift, 1))


def pack_y_kernel(from_minus, from_plus, low_in, high_in, token, sides, low_rows, high_rows, low, high):
    del token
    low[...] = low_in[...]
    high[...] = high_in[...]
    for t, part in enumerate((from_minus, from_plus)):
        sides[t] = part[...].astype(jnp.float32)
        low[pl.ds(100 + 2 * t, 2), :] = sides[t, 0:2, :]
        high[pl.ds(100 + 2 * t, 2), :] = sides[t, 30:32, :]
    low_rows[...] = low[...].astype(jnp.bfloat16)
    high_rows[...] = high[...].astype(jnp.bfloat16)


def own_kernel(pop, ori, after, own, token):
    token[...] = jnp.zeros(token.shape, jnp.float32)
    numbers = list(range(19))
    for x in range(2):
        for r in range(4):
            rows = pl.ds(8 * r, 8)
            f = [pop[i, x, rows, :] for i in numbers]
            rho, mom = moments(f, numbers)
            inv = 1.0 / rho
            u = [m * inv for m in mom]
            relaxed = relax(f, rho, u, numbers)
            for i in numbers:
                own[i, x, rows, :] = relaxed[i]
            for j in range(3):
                own[19 + j, x, rows, :] = u[j]
            for k in range(6):
                own[22 + k, x, rows, :] = ori[k, x, rows, :]


def collide_group(raw, fields, x, t, r):
    numbers = list(range(19))
    f = [raw(i) for i in numbers]
    rho, mom = moments(f, numbers)
    inv = 1.0 / rho
    u = [m * inv for m in mom]
    relaxed = relax(f, rho, u, numbers)
    for i in numbers:
        put(fields, (i, x, t), r, relaxed[i])
    for j in range(3):
        put(fields, (19 + j, x, t), r, u[j])
    for k in range(6):
        put(fields, (22 + k, x, t), r, raw(19 + k))


def advance_group(fields, state, out, x, r, low, high):
    lane, row = lanes_of(), rows_of()
    place = lambda f, xs=x: (lambda t: (f, xs, t))
    known = [{}, {}]
    for i in KNOWN[x]:
        xs = x - VELOCITIES[i][0]
        pair = stream(fields, place(i, xs), i, r, low, high, lambda i=i: get(fields, (opposite(i), x, 0), r))
        known[0][i], known[1][i] = pair
    grad = [[[None] * 3 for _ in range(3)] for _ in range(2)]
    sign = 0.5 if x == 0 else -0.5
    for j in range(3):
        by_y = central(fields, place(19 + j), r, 1, low, high, False)
        by_z = central(fields, place(19 + j), r, 2, low, high, False)
        for t in range(2):
            grad[t][j][0] = sign * get(fields, (19 + j, 1 - x, t), r)
            grad[t][j][1] = by_y[t]
            grad[t][j][2] = by_z[t]
    u = [[get(fields, (19 + j, x, t), r) for j in range(3)] for t in range(2)]
    a = [[get(fields, (22 + k, x, t), r) for k in range(6)] for t in range(2)]
    advect = [[], []]
    for k in range(6):
        by_y = central(fields, place(22 + k), r, 1, low, high, True)
        by_z = central(fields, place(22 + k), r, 2, low, high, True)
        for t in range(2):
            by_x = sign * get(fields, (22 + k, 1 - x, t), r)
            advect[t].append(u[t][0] * by_x + u[t][1] * by_y[t] + u[t][2] * by_z[t])
    side_pack = jnp.zeros((8, 128), jnp.float32)
    for t in range(2):
        rate = jeffery(a[t], grad[t])
        part = [a[t][k] + ORIENT_STEP * (rate[k] - advect[t][k]) for k in range(6)]
        rho, mom = moments(known[t], KNOWN[x])
        outward = [get(fields, (i, x, t), r) for i in TOWARD[x]]
        keep = [known[t][i] for i in KNOWN[x]] + [rho] + mom + part + u[t] + a[t] + outward
        for k in range(STATE):
            state[x, k, t, pl.ds(state_row(r), 8), :] = keep[k]
        wide = outward + u[t] + a[t] + [rho] + mom + [known[t][i] for i in TOWARD[x]]
        if t == 1:
            for k in range(MSG_WIDE):
                at = 4 * k
                side_pack = jnp.where((lane >= at) & (lane < at + 4), roll(wide[k], at + 2, 1), side_pack)
        elif r < 4:
            for k, v in enumerate(wide + part):
                out[x, pl.ds(field_row(k, r), 8), :] = v
        else:
            inner = (row >= 2) & (row < 6)
            for k in range(0, MSG_WIDE, 2):
                v = wide[k]
                if k + 1 < MSG_WIDE:
                    v = jnp.where(inner, roll(wide[k + 1], 4, 0), v)
                out[x, pl.ds(HALO_AT + 4 * k, 8), :] = v
    out[x, pl.ds(side_row(r), 8), :] = side_pack


def middle_kernel(own, sides, fields, state, message, out):
    low, high = walls()
    for x in range(2):
        for r in range(4):
            rows = pl.ds(8 * r, 8)
            for k in range(28):
                put(fields, (k, x, 0), r, own[k, x, rows, :])

            def raw(f):
                return unpack_z(sides[0, rows, :], sides[1, rows, :], 2 * f + x)

            collide_group(raw, fields, x, 1, r)
    for x in range(2):
        for r in (1, 2):
            advance_group(fields, state, out, x, r, low, high)
    message[...] = out[...].astype(jnp.bfloat16)


def step_one_kernel(before, middle, from_yminus, from_yplus, fields, state, msg_off, msg_on, halo, out, got):
    del before
    low, high = walls()
    got[0] = from_yminus[...].astype(jnp.float32)
    got[1] = from_yplus[...].astype(jnp.float32)
    for s in range(52):
        halo[s, 0:2, :] = got[1, pl.ds(2 * s, 2), :]
        halo[s, 6:8, :] = got[0, pl.ds(2 * s, 2), :]
    for x in range(2):
        for t in range(2):

            def raw(f):
                s = 2 * f + x
                return halo[s] if t == 0 else unpack_z(halo[50], halo[51], s)

            collide_group(raw, fields, x, t, 4)
    for x in range(2):
        for r in (0, 3, 4):
            advance_group(fields, state, out, x, r, low, high)
        out[x, pl.ds(CORNER_AT + 8, 8), :] = jnp.zeros((8, 128), jnp.float32)
    odd = lax.axis_index("gx") % 2
    for x, msg in ((odd, msg_off), (1 - odd, msg_on)):
        msg[0:MID_ROWS, :] = middle[x]
        msg[MID_ROWS:MSG_ROWS, :] = out[x, MID_ROWS:MSG_ROWS, :].astype(jnp.bfloat16)


def weights_kernel(
    w_in_hbm, b_in_hbm, w_mid_hbm, b_mid_hbm, w_out_hbm, b_out_hbm, w_one, w_two, bias_mid, w_three, bias_out,
    w_in, b_in, w_mid, b_mid, b_out, wide, sems,
):
    pairs = [
        (w_mid_hbm, w_mid),
        (w_in_hbm, w_in),
        (b_in_hbm, b_in),
        (b_mid_hbm, b_mid),
        (b_out_hbm, b_out),
        (w_out_hbm, w_three),
    ]
    for copy in fetch(pairs, sems):
        copy.wait()
    f32, bf16 = jnp.float32, jnp.bfloat16
    row = lax.broadcasted_iota(jnp.int32, (8, 512), 0)
    bias = jnp.broadcast_to(0.5 * b_in[...], (8, 512))
    first = bias.astype(bf16).astype(f32)
    rest = bias - first
    padded = jnp.concatenate([0.5 * w_in[...].astype(f32), jnp.zeros((2, 512), f32)], axis=0)
    stacked = jnp.where(row == 6, first, jnp.where(row == 7, rest, padded))
    w_one[...] = stacked.T.astype(bf16)
    w_two[...] = (0.5 * w_mid[...].astype(f32)).T.astype(bf16)
    bias_mid[...] = jnp.broadcast_to(jnp.broadcast_to(0.5 * b_mid[...], (8, 512)).T[:, 0:1], (512, 128))
    wide[...] = jnp.zeros(wide.shape, f32)
    wide[:, 0:15] = jnp.broadcast_to(b_out[...], (8, 15))
    bias_out[...] = jnp.broadcast_to(wide[...].T[0:16, 0:1], (16, 128))


def step_two_kernel(
    slots, state_mid, state_rim, from_on, from_off, w_one, w_mid, b_mid, w_out, b_out, flow, closure,
    got, fields, near, level, feats, spread, place,
):
    low, high = walls()
    odd = lax.axis_index("gx") % 2
    got[odd] = from_off[...].astype(jnp.float32)
    got[1 - odd] = from_on[...].astype(jnp.float32)
    for s in range(17):
        place[s] = 64
    for b in range(64):
        s = slots[b // 32, 0, b % 32]
        place[jnp.where(s >= 0, s, 16)] = b

    def arrived(x, k, t, r):
        if t == 0 and r < 4:
            return got[x, pl.ds(field_row(k, r), 8), :]
        if t == 0:
            v = got[x, pl.ds(HALO_AT + 8 * (k // 2), 8), :]
            return roll(v, 4, 0) if k % 2 else v
        v = got[x, pl.ds(side_row(r), 8), :]
        return roll(v, -(4 * k + 2), 1)

    def kept(x, k, t, r):
        part = state_mid if r in (1, 2) else state_rim
        return part[x, k, t, pl.ds(state_row(r), 8), :]

    for x in range(2):
        for t in range(2):
            for r in range(5):
                for k in range(5):
                    put(near, (x, k, t), r, arrived(x, k, t, r))
                    put(near, (x, 5 + k, t), r, kept(x, 33 + k, t, r))
    numbers = list(range(19))
    for x in range(2):
        come = TOWARD[1 - x]
        go = TOWARD[x]
        sign = -0.5 if x == 0 else 0.5
        for r in range(5):
            come_f, go_f = [{}, {}], [{}, {}]
            for k, i in enumerate(come):
                back = go.index(opposite(i))
                pair = stream(
                    near, lambda t, k=k: (x, k, t), i, r, low, high,
                    lambda back=back: get(near, (x, 5 + back, 0), r),
                )
                come_f[0][i], come_f[1][i] = pair
            for k, i in enumerate(go):
                back = come.index(opposite(i))
                pair = stream(
                    near, lambda t, k=k: (x, 5 + k, t), i, r, low, high,
                    lambda back=back: get(near, (x, back, 0), r),
                )
                go_f[0][i], go_f[1][i] = pair
            for t in range(2):
                f = {i: kept(x, k, t, r) for k, i in enumerate(KNOWN[x])}
                f.update(come_f[t])
                rho_new, mom_new = moments(come_f[t], come)
                rho = kept(x, 14, t, r) + rho_new
                mom = [kept(x, 15 + j, t, r) + mom_new[j] for j in range(3)]
                inv = 1.0 / rho
                u = [m * inv for m in mom]
                relaxed = relax(f, rho, u, numbers)
                for i in numbers:
                    put(fields, (i, x, t), r, relaxed[i])
                for j in range(3):
                    put(fields, (19 + j, x, t), r, u[j])
                u0 = [kept(x, 24 + j, t, r) for j in range(3)]
                a0 = [kept(x, 27 + k, t, r) for k in range(6)]
                u0n = [arrived(x, 5 + j, t, r) for j in range(3)]
                a0n = [arrived(x, 8 + k, t, r) for k in range(6)]
                rate = jeffery(a0, [[sign * u0n[j], None, None] for j in range(3)])
                drift = (sign * u0[0])
                for k in range(6):
                    a1 = kept(x, 18 + k, t, r) + ORIENT_STEP * (rate[k] - drift * a0n[k])
                    put(fields, (22 + k, x, t), r, a1)
                rho_new, mom_new = moments(go_f[t], go)
                rho = arrived(x, 14, t, r) + rho_new
                inv = 1.0 / rho
                u = [(arrived(x, 15 + j, t, r) + mom_new[j]) * inv for j in range(3)]
                f = {i: arrived(x, 18 + k, t, r) for k, i in enumerate(come)}
                relaxed = relax(f, rho, u, come)
                for k, i in enumerate(come):
                    put(fields, (28 + k, x, t), r, relaxed[i])
                if t == 0 and r < 4:
                    rate = jeffery(a0n, [[-sign * u0[j], None, None] for j in range(3)])
                    drift = -sign * u0n[0]
                    for j in range(3):
                        level[x, j, pl.ds(8 * r, 8), :] = u[j]
                    for k in range(6):
                        a1 = arrived(x, 23 + k, t, r) + ORIENT_STEP * (rate[k] - drift * a0[k])
                        level[x, 3 + k, pl.ds(8 * r, 8), :] = a1

    feats[...] = jnp.ones(feats.shape, jnp.float32)
    for x in range(2):
        for r in range(4):
            f = {}
            for i in numbers:
                xs = x - VELOCITIES[i][0]
                if 0 <= xs <= 1:
                    at_of = lambda t, i=i, xs=xs: (i, xs, t)
                else:
                    k = TOWARD[1 - x].index(i)
                    at_of = lambda t, k=k: (28 + k, x, t)
                f[i], _ = stream(
                    fields, at_of, i, r, low, high, lambda i=i: get(fields, (opposite(i), x, 0), r), False
                )
            rho, mom = moments(f, numbers)
            inv = 1.0 / rho
            final = [rho] + [m * inv for m in mom]
            for k in range(4):
                spread[pl.ds(k * 64 + x * 32 + 8 * r, 8), :] = final[k]
            sign = -0.5 if x == 0 else 0.5
            by_x = lambda k, n: sign * (level[x, n, pl.ds(8 * r, 8), :] - get(fields, (k, 1 - x, 0), r))
            grad = [[None] * 3 for _ in range(3)]
            for j in range(3):
                place_u = lambda t, j=j: (19 + j, x, t)
                grad[j][0] = by_x(19 + j, j)
                grad[j][1] = central(fields, place_u, r, 1, low, high, False, False)[0]
                grad[j][2] = central(fields, place_u, r, 2, low, high, False, False)[0]
            u = [get(fields, (19 + j, x, 0), r) for j in range(3)]
            a = [get(fields, (22 + k, x, 0), r) for k in range(6)]
            rate = jeffery(a, grad)
            for k in range(6):
                place_a = lambda t, k=k: (22 + k, x, t)
                advect = (
                    u[0] * by_x(22 + k, 3 + k)
                    + u[1] * central(fields, place_a, r, 1, low, high, True, False)[0]
                    + u[2] * central(fields, place_a, r, 2, low, high, True, False)[0]
                )
                new = a[k] + ORIENT_STEP * (rate[k] - advect)
                feats[pl.ds((x * 32 + 8 * r) * 8 + k, 8, 8), :] = new
    for k in range(4):
        for x in range(2):
            flow[k, x] = spread[pl.ds(k * 64 + x * 32, 32), :].astype(jnp.bfloat16)

    spread[...] = jnp.zeros(spread.shape, jnp.float32)
    group = 8
    bias_mid = jnp.concatenate([b_mid[...]] * group, axis=1)
    for g in range(16 // group):
        at = [place[g * group + k] for k in range(group)]
        cells = [feats[pl.ds(pl.multiple_of(b * 8, 8), 8), :] for b in at]
        cells = jnp.concatenate(cells, axis=1).astype(jnp.bfloat16)
        v = jnp.dot(w_one[...], cells, preferred_element_type=jnp.float32)
        h = (v + v * jnp.tanh(v)).astype(jnp.bfloat16)
        v = jnp.dot(w_mid[...], h, preferred_element_type=jnp.float32) + bias_mid
        h = (v + v * jnp.tanh(v)).astype(jnp.bfloat16)
        v = jnp.dot(w_out[...], h, preferred_element_type=jnp.float32)
        for k in range(group):
            spread[pl.ds(pl.multiple_of(at[k] * 16, 16), 15), :] = v[:, 128 * k : 128 * k + 128] + b_out[0:15, :]
    for c in range(15):
        for x in range(2):
            closure[c, x] = spread[pl.ds(x * 512 + c, 32, 16), :].astype(jnp.bfloat16)


def local(populations, orientation, slot_table, w_in, b_in, w_mid, b_mid, w_out, b_out):
    f32, bf16 = jnp.float32, jnp.bfloat16
    shape = lambda *s, d=f32: jax.ShapeDtypeStruct(s, d)
    vmem = pl.BlockSpec(memory_space=pltpu.VMEM)
    smem = pl.BlockSpec(memory_space=pltpu.SMEM)
    params = pltpu.CompilerParams(vmem_limit_bytes=24 * MIB)

    def ring(axis, step, wrap):
        n = lax.axis_size(axis)
        return [(i, (i + step) % n) for i in range(n) if wrap or 0 <= i + step < n]

    hbm = pl.BlockSpec(memory_space=pltpu.HBM)
    slots = jnp.transpose(slot_table, (0, 2, 1))
    w_one, w_two, bias_mid, w_three, bias_out = pl.pallas_call(
        weights_kernel,
        out_shape=(
            shape(512, 8, d=bf16),
            shape(512, 512, d=bf16),
            shape(512, 128),
            shape(15, 512, d=bf16),
            shape(16, 128),
        ),
        in_specs=[hbm] * 6,
        out_specs=(vmem,) * 5,
        scratch_shapes=[
            pltpu.VMEM((6, 512), bf16),
            pltpu.VMEM((1, 512), f32),
            pltpu.VMEM((512, 512), bf16),
            pltpu.VMEM((1, 512), f32),
            pltpu.VMEM((1, 15), f32),
            pltpu.VMEM((8, 128), f32),
            pltpu.SemaphoreType.DMA((6,)),
        ],
        compiler_params=pltpu.CompilerParams(vmem_limit_bytes=LIMIT_WEIGHTS),
    )(w_in, b_in.reshape(1, 512), w_mid, b_mid.reshape(1, 512), w_out.T, b_out.reshape(1, 15))
    zlow, zhigh, low_raw, high_raw = pl.pallas_call(
        pack_z_kernel,
        out_shape=(shape(32, 128, d=bf16), shape(32, 128, d=bf16), shape(112, 128), shape(112, 128)),
        in_specs=[hbm] * 2,
        out_specs=(vmem,) * 4,
        scratch_shapes=[
            pltpu.VMEM((19, 2, 32, 128), f32),
            pltpu.VMEM((6, 2, 32, 128), f32),
            pltpu.SemaphoreType.DMA((5,)),
        ],
        compiler_params=pltpu.CompilerParams(vmem_limit_bytes=LIMIT_PACK),
        cost_estimate=COST_PACK,
    )(populations, orientation)
    own, token = pl.pallas_call(
        own_kernel,
        out_shape=(shape(28, 2, 32, 128), shape(8, 128)),
        in_specs=[vmem] * 3,
        out_specs=(vmem,) * 2,
        compiler_params=params,
    )(populations, orientation, low_raw)
    from_minus = lax.ppermute(zhigh, "gz", ring("gz", 1, False))
    from_plus = lax.ppermute(zlow, "gz", ring("gz", -1, False))
    sides, low_rows, high_rows = pl.pallas_call(
        pack_y_kernel,
        out_shape=(shape(2, 32, 128), shape(112, 128, d=bf16), shape(112, 128, d=bf16)),
        in_specs=[vmem] * 5,
        out_specs=(vmem,) * 3,
        scratch_shapes=[pltpu.VMEM((112, 128), f32), pltpu.VMEM((112, 128), f32)],
        compiler_params=params,
    )(from_minus, from_plus, low_raw, high_raw, token)
    fields_shape = shape(28, 2, 2, 64, 128)
    fields, state_mid, middle = pl.pallas_call(
        middle_kernel,
        out_shape=(fields_shape, shape(2, STATE, 2, 16, 128), shape(2, MID_ROWS, 128, d=bf16)),
        in_specs=[vmem] * 2,
        out_specs=(vmem,) * 3,
        scratch_shapes=[pltpu.VMEM((2, MID_ROWS, 128), f32)],
        compiler_params=params,
    )(own, sides)
    from_yminus = lax.ppermute(high_rows, "gy", ring("gy", 1, True))
    from_yplus = lax.ppermute(low_rows, "gy", ring("gy", -1, True))
    fields, state_rim, msg_off, msg_on = pl.pallas_call(
        step_one_kernel,
        out_shape=(
            fields_shape,
            shape(2, STATE, 2, 24, 128),
            shape(MSG_ROWS, 128, d=bf16),
            shape(MSG_ROWS, 128, d=bf16),
        ),
        in_specs=[vmem] * 4,
        out_specs=(vmem,) * 4,
        scratch_shapes=[
            pltpu.VMEM((52, 8, 128), f32),
            pltpu.VMEM((2, MSG_ROWS, 128), f32),
            pltpu.VMEM((2, 112, 128), f32),
        ],
        input_output_aliases={0: 0},
        compiler_params=params,
    )(fields, middle, from_yminus, from_yplus)
    x_count = lax.axis_size("gx")
    off_chip = [(i, (i + (1 if i % 2 else -1)) % x_count) for i in range(x_count)]
    on_chip = [(i, i + (-1 if i % 2 else 1)) for i in range(x_count)]
    from_on = lax.ppermute(msg_on, "gx", on_chip)
    from_off = lax.ppermute(msg_off, "gx", off_chip)
    return pl.pallas_call(
        step_two_kernel,
        out_shape=(shape(4, 2, 32, 128, d=bf16), shape(15, 2, 32, 128, d=bf16)),
        in_specs=[smem] + [vmem] * 9,
        out_specs=(vmem,) * 2,
        scratch_shapes=[
            pltpu.VMEM((2, MSG_ROWS, 128), f32),
            pltpu.VMEM((33, 2, 2, 64, 128), f32),
            pltpu.VMEM((2, 10, 2, 64, 128), f32),
            pltpu.VMEM((2, 9, 32, 128), f32),
            pltpu.VMEM((65 * 8, 128), f32),
            pltpu.VMEM((65 * 16, 128), f32),
            pltpu.SMEM((17,), jnp.int32),
        ],
        compiler_params=params,
    )(slots, state_mid, state_rim, from_on, from_off, w_one, w_two, bias_mid, w_three, bias_out)


def solution(mesh):
    grid = P(None, "gx", "gy", "gz")
    in_specs = (grid, grid, P("gx", "gy", "gz"), P(), P(), P(), P(), P(), P())
    return jax.shard_map(local, mesh=mesh, in_specs=in_specs, out_specs=(grid, grid), check_vma=False)
```

```python
import functools

import jax
import jax.numpy as jnp
from jax import lax
from jax.experimental import pallas as pl
from jax.experimental.pallas import tpu as pltpu
from jax.sharding import PartitionSpec as P


VELOCITIES = [
    (0, 0, 0),
    (1, 0, 0),
    (-1, 0, 0),
    (0, 1, 0),
    (0, -1, 0),
    (0, 0, 1),
    (0, 0, -1),
    (1, 1, 0),
    (-1, -1, 0),
    (1, -1, 0),
    (-1, 1, 0),
    (1, 0, 1),
    (-1, 0, -1),
    (1, 0, -1),
    (-1, 0, 1),
    (0, 1, 1),
    (0, -1, -1),
    (0, 1, -1),
    (0, -1, 1),
]
WEIGHTS = [1.0 / 3.0] + [1.0 / 18.0] * 6 + [1.0 / 36.0] * 12
OMEGA = 1.0 / 0.8
SHAPE_FACTOR = 0.95
ORIENT_STEP = 4.0
PAIRS = [(0, 0), (1, 1), (2, 2), (0, 1), (0, 2), (1, 2)]
ENTRY = [[0, 3, 4], [3, 1, 5], [4, 5, 2]]
TOWARD = {
    0: [i for i in range(19) if VELOCITIES[i][0] == -1],
    1: [i for i in range(19) if VELOCITIES[i][0] == 1],
}
KNOWN = {0: [i for i in range(19) if VELOCITIES[i][0] != 1], 1: [i for i in range(19) if VELOCITIES[i][0] != -1]}
MSG_WIDE = 23
MSG_ROWS = 1072
MID_ROWS = 480
SIDE_MID = 464
RIM_AT = 480
HALO_AT = 944
SIDE_RIM = 1040
CORNER_AT = 1056
MIB = 1024 * 1024
LIMIT_PACK = 5375 * MIB // 100
COST_PACK = pl.CostEstimate(flops=10**10, bytes_accessed=10**7, transcendentals=0)
LIMIT_WEIGHTS = 4900 * MIB // 100
STATE = 38


def opposite(i):
    return 0 if i == 0 else (i + 1 if i % 2 == 1 else i - 1)


def lanes_of():
    return lax.broadcasted_iota(jnp.int32, (8, 128), 1)


def rows_of():
    return lax.broadcasted_iota(jnp.int32, (8, 128), 0)


def roll(v, shift, axis):
    shift = shift % v.shape[axis]
    return v if shift == 0 else pltpu.roll(v, shift, axis)


def add_all(terms):
    while len(terms) > 1:
        terms = [
            terms[k] + terms[k + 1] if k + 1 < len(terms) else terms[k] for k in range(0, len(terms), 2)
        ]
    return terms[0]


def moments(f, numbers):
    rho = add_all([f[i] for i in numbers])
    mom = []
    for ax in range(3):
        pos = [f[i] for i in numbers if VELOCITIES[i][ax] > 0]
        neg = [f[i] for i in numbers if VELOCITIES[i][ax] < 0]
        total = add_all(pos) if pos else None
        if neg:
            total = add_all(neg) * -1.0 if total is None else total - add_all(neg)
        mom.append(total)
    return rho, mom


def relax(f, rho, u, numbers):
    usq = 1.0 - 1.5 * (u[0] * u[0] + u[1] * u[1] + u[2] * u[2])
    scaled = {w: (w * OMEGA) * rho for w in sorted(set(WEIGHTS[i] for i in numbers))}
    out = {}
    for i in numbers:
        proj = None
        for ax in range(3):
            c = VELOCITIES[i][ax]
            if c != 0:
                if proj is None:
                    proj = u[ax] if c > 0 else -u[ax]
                else:
                    proj = proj + u[ax] if c > 0 else proj - u[ax]
        poly = usq if proj is None else usq + proj * (3.0 + 4.5 * proj)
        out[i] = f[i] * (1.0 - OMEGA) + scaled[WEIGHTS[i]] * poly
    return out


def plus(a, b):
    if a is None:
        return b
    if b is None:
        return a
    return a + b


def minus(a, b):
    if b is None:
        return a
    if a is None:
        return -b
    return a - b


def times(a, b):
    return None if a is None or b is None else a * b


def jeffery(a, g):
    half = [[None if g[j][k] is None else 0.5 * g[j][k] for k in range(3)] for j in range(3)]
    d = [[plus(half[j][k], half[k][j]) if j <= k else None for k in range(3)] for j in range(3)]
    w = [[minus(half[j][k], half[k][j]) if j < k else None for k in range(3)] for j in range(3)]
    full = lambda j, k: a[ENTRY[j][k]]
    strain = lambda j, k: d[min(j, k)][max(j, k)]

    def spin(j, k):
        if j == k:
            return None
        if j < k:
            return w[j][k]
        return None if w[k][j] is None else -w[k][j]

    contraction = None
    for j in range(3):
        contraction = plus(contraction, times(full(j, j), strain(j, j)))
    for j, k in ((0, 1), (0, 2), (1, 2)):
        cross = times(full(j, k), strain(j, k))
        contraction = plus(contraction, None if cross is None else 2.0 * cross)
    twice = 2.0 * contraction
    mix = [[plus(spin(j, k), times(strain(j, k), SHAPE_FACTOR)) for k in range(3)] for j in range(3)]
    z = [[None] * 3 for _ in range(3)]
    for j in range(3):
        for k in range(3):
            for m in range(3):
                z[j][k] = plus(z[j][k], times(full(j, m), mix[m][k]))
    scaled = SHAPE_FACTOR * twice
    return [plus(z[j][k], z[k][j]) - scaled * full(j, k) for j, k in PAIRS]


def field_row(k, r):
    return 16 * k + 8 * (r - 1) if r in (1, 2) else RIM_AT + 16 * k + 8 * (r // 3)


def side_row(r):
    return SIDE_MID + 8 * (r - 1) if r in (1, 2) else (CORNER_AT if r == 4 else SIDE_RIM + 8 * (r // 3))


def state_row(r):
    return {1: 0, 2: 8, 0: 0, 3: 8, 4: 16}[r]


def put(ref, at, r, v):
    if r < 4:
        ref[at + (pl.ds(16 + 8 * r, 8), slice(None))] = v
    else:
        ref[at + (pl.ds(8, 8), slice(None))] = v
        ref[at + (pl.ds(48, 8), slice(None))] = v


def get(ref, at, r, dy=0):
    if r < 4:
        return ref[at + (pl.ds(16 + 8 * r + dy, 8), slice(None))]
    if dy == 0:
        return ref[at + (pl.ds(48, 8), slice(None))]
    return jnp.where(
        rows_of() < 4,
        ref[at + (pl.ds(48 + dy, 8), slice(None))],
        ref[at + (pl.ds(8 + dy, 8), slice(None))],
    )


def pull_z(own, side, dz, want_side=True):
    if dz == 0:
        return own, side
    lane = lanes_of()
    own_r, side_r = roll(own, dz, 1), roll(side, dz, 1)
    edge = lane == (0 if dz > 0 else 127)
    return jnp.where(edge, side_r, own_r), jnp.where(edge, own_r, side_r) if want_side else None


def walls():
    layer = lax.axis_index("gz")
    last = lax.axis_size("gz") - 1
    lane = lanes_of()
    low = lane == jnp.where(layer == 0, 0, -1)
    high = lane == jnp.where(layer == last, 127, -1)
    return low, high


def wall_of(i, low, high):
    dz = VELOCITIES[i][2]
    return None if dz == 0 else (low if dz > 0 else high)


def stream(ref, at_of, i, r, low, high, reflected, want_side=True):
    _, cy, cz = VELOCITIES[i]
    own = get(ref, at_of(0), r, -cy)
    side = get(ref, at_of(1), r, -cy) if (want_side or cz != 0) else None
    if cz == 0:
        return own, side
    own, side = pull_z(own, side, cz, want_side)
    return jnp.where(wall_of(i, low, high), reflected(), own), side


def central(ref, at_of, r, axis, low, high, outside, want_side=True):
    if axis == 1:
        out = []
        for t in (0, 1) if want_side else (0,):
            out.append(0.5 * (get(ref, at_of(t), r, 1) - get(ref, at_of(t), r, -1)))
        return out
    own, side = get(ref, at_of(0), r), get(ref, at_of(1), r)
    behind, behind_side = pull_z(own, side, 1, want_side)
    ahead, ahead_side = pull_z(own, side, -1, want_side)
    past = own if outside else jnp.zeros_like(own)
    diff = 0.5 * (jnp.where(high, past, ahead) - jnp.where(low, past, behind))
    return [diff, 0.5 * (ahead_side - behind_side)] if want_side else [diff]


def fetch(pairs, sems):
    copies = [pltpu.make_async_copy(src, dst, sems.at[k]) for k, (src, dst) in enumerate(pairs)]
    for copy in copies:
        copy.start()
    return copies


PIECES = [(0, 5), (5, 10), (10, 15), (15, 19)]


def pack_z_kernel(pop_hbm, ori_hbm, zlow, zhigh, pop, ori, sems):
    pairs = [(pop_hbm.at[pl.ds(a, b - a)], pop.at[pl.ds(a, b - a)]) for a, b in PIECES]
    copies = fetch(pairs + [(ori_hbm, ori)], sems)
    starts = [a for a, _ in PIECES] + [19]
    lane = lax.broadcasted_iota(jnp.int32, (32, 128), 1)
    low = jnp.zeros((32, 128), jnp.float32)
    high = jnp.zeros((32, 128), jnp.float32)
    for f in range(25):
        if f in starts:
            copies[starts.index(f)].wait()
        src = pop if f < 19 else ori
        k = f if f < 19 else f - 19
        for x in range(2):
            s = 2 * f + x
            at = 2 * s
            v = roll(src[k, x], at + 2, 1)
            high = jnp.where((lane >= at) & (lane < at + 2), v, high)
            low = jnp.where((lane >= at + 2) & (lane < at + 4), v, low)
    zlow[...] = low.astype(jnp.bfloat16)
    zhigh[...] = high.astype(jnp.bfloat16)


def unpack_z(from_minus, from_plus, s):
    shift = -(2 * s + 2)
    return jnp.where(lanes_of() < 64, roll(from_plus, shift, 1), roll(from_minus, shift, 1))


def pack_y_kernel(from_minus, from_plus, low_in, high_in, sides, low_rows, high_rows, low, high):
    low[...] = low_in[...]
    high[...] = high_in[...]
    for t, part in enumerate((from_minus, from_plus)):
        sides[t] = part[...].astype(jnp.float32)
        low[pl.ds(100 + 2 * t, 2), :] = sides[t, 0:2, :]
        high[pl.ds(100 + 2 * t, 2), :] = sides[t, 30:32, :]
    low_rows[...] = low[...].astype(jnp.bfloat16)
    high_rows[...] = high[...].astype(jnp.bfloat16)


def own_kernel(pop, ori, after, own, low_rows, high_rows):
    del after
    for f in range(25):
        src = pop if f < 19 else ori
        k = f if f < 19 else f - 19
        for x in range(2):
            rows = pl.ds(2 * (2 * f + x), 2)
            low_rows[rows, :] = src[k, x, 0:2, :]
            high_rows[rows, :] = src[k, x, 30:32, :]
    low_rows[100:112, :] = jnp.zeros((12, 128), jnp.float32)
    high_rows[100:112, :] = jnp.zeros((12, 128), jnp.float32)
    numbers = list(range(19))
    for x in range(2):
        for r in range(4):
            rows = pl.ds(8 * r, 8)
            f = [pop[i, x, rows, :] for i in numbers]
            rho, mom = moments(f, numbers)
            inv = 1.0 / rho
            u = [m * inv for m in mom]
            relaxed = relax(f, rho, u, numbers)
            for i in numbers:
                own[i, x, rows, :] = relaxed[i]
            for j in range(3):
                own[19 + j, x, rows, :] = u[j]
            for k in range(6):
                own[22 + k, x, rows, :] = ori[k, x, rows, :]


def collide_group(raw, fields, x, t, r):
    numbers = list(range(19))
    f = [raw(i) for i in numbers]
    rho, mom = moments(f, numbers)
    inv = 1.0 / rho
    u = [m * inv for m in mom]
    relaxed = relax(f, rho, u, numbers)
    for i in numbers:
        put(fields, (i, x, t), r, relaxed[i])
    for j in range(3):
        put(fields, (19 + j, x, t), r, u[j])
    for k in range(6):
        put(fields, (22 + k, x, t), r, raw(19 + k))


def advance_group(fields, state, out, x, r, low, high):
    lane, row = lanes_of(), rows_of()
    place = lambda f, xs=x: (lambda t: (f, xs, t))
    known = [{}, {}]
    for i in KNOWN[x]:
        xs = x - VELOCITIES[i][0]
        pair = stream(fields, place(i, xs), i, r, low, high, lambda i=i: get(fields, (opposite(i), x, 0), r))
        known[0][i], known[1][i] = pair
    grad = [[[None] * 3 for _ in range(3)] for _ in range(2)]
    sign = 0.5 if x == 0 else -0.5
    for j in range(3):
        by_y = central(fields, place(19 + j), r, 1, low, high, False)
        by_z = central(fields, place(19 + j), r, 2, low, high, False)
        for t in range(2):
            grad[t][j][0] = sign * get(fields, (19 + j, 1 - x, t), r)
            grad[t][j][1] = by_y[t]
            grad[t][j][2] = by_z[t]
    u = [[get(fields, (19 + j, x, t), r) for j in range(3)] for t in range(2)]
    a = [[get(fields, (22 + k, x, t), r) for k in range(6)] for t in range(2)]
    advect = [[], []]
    for k in range(6):
        by_y = central(fields, place(22 + k), r, 1, low, high, True)
        by_z = central(fields, place(22 + k), r, 2, low, high, True)
        for t in range(2):
            by_x = sign * get(fields, (22 + k, 1 - x, t), r)
            advect[t].append(u[t][0] * by_x + u[t][1] * by_y[t] + u[t][2] * by_z[t])
    side_pack = jnp.zeros((8, 128), jnp.float32)
    for t in range(2):
        rate = jeffery(a[t], grad[t])
        part = [a[t][k] + ORIENT_STEP * (rate[k] - advect[t][k]) for k in range(6)]
        rho, mom = moments(known[t], KNOWN[x])
        outward = [get(fields, (i, x, t), r) for i in TOWARD[x]]
        keep = [known[t][i] for i in KNOWN[x]] + [rho] + mom + part + u[t] + a[t] + outward
        for k in range(STATE):
            state[x, k, t, pl.ds(state_row(r), 8), :] = keep[k]
        wide = outward + u[t] + a[t] + [rho] + mom + [known[t][i] for i in TOWARD[x]]
        if t == 1:
            for k in range(MSG_WIDE):
                at = 4 * k
                side_pack = jnp.where((lane >= at) & (lane < at + 4), roll(wide[k], at + 2, 1), side_pack)
        elif r < 4:
            for k, v in enumerate(wide + part):
                out[x, pl.ds(field_row(k, r), 8), :] = v
        else:
            inner = (row >= 2) & (row < 6)
            for k in range(0, MSG_WIDE, 2):
                v = wide[k]
                if k + 1 < MSG_WIDE:
                    v = jnp.where(inner, roll(wide[k + 1], 4, 0), v)
                out[x, pl.ds(HALO_AT + 4 * k, 8), :] = v
    out[x, pl.ds(side_row(r), 8), :] = side_pack


def middle_kernel(own, sides, fields, state, message, out):
    low, high = walls()
    for x in range(2):
        for r in range(4):
            rows = pl.ds(8 * r, 8)
            for k in range(28):
                put(fields, (k, x, 0), r, own[k, x, rows, :])

            def raw(f):
                return unpack_z(sides[0, rows, :], sides[1, rows, :], 2 * f + x)

            collide_group(raw, fields, x, 1, r)
    for x in range(2):
        for r in (1, 2):
            advance_group(fields, state, out, x, r, low, high)
    message[...] = out[...].astype(jnp.bfloat16)


def step_one_kernel(before, middle, from_yminus, from_yplus, fields, state, msg_low, msg_high, halo, out, got):
    del before
    low, high = walls()
    got[0] = from_yminus[...].astype(jnp.float32)
    got[1] = from_yplus[...].astype(jnp.float32)
    for s in range(52):
        halo[s, 0:2, :] = got[1, pl.ds(2 * s, 2), :]
        halo[s, 6:8, :] = got[0, pl.ds(2 * s, 2), :]
    for x in range(2):
        for t in range(2):

            def raw(f):
                s = 2 * f + x
                return halo[s] if t == 0 else unpack_z(halo[50], halo[51], s)

            collide_group(raw, fields, x, t, 4)
    for x in range(2):
        for r in (0, 3, 4):
            advance_group(fields, state, out, x, r, low, high)
        out[x, pl.ds(CORNER_AT + 8, 8), :] = jnp.zeros((8, 128), jnp.float32)
    for x, msg in enumerate((msg_low, msg_high)):
        msg[0:MID_ROWS, :] = middle[x]
        msg[MID_ROWS:MSG_ROWS, :] = out[x, MID_ROWS:MSG_ROWS, :].astype(jnp.bfloat16)


def weights_kernel(
    w_in_hbm, b_in_hbm, w_mid_hbm, b_mid_hbm, w_out_hbm, b_out_hbm, w_one, w_two, bias_mid, w_three, bias_out,
    w_in, b_in, w_mid, b_mid, b_out, wide, sems,
):
    pairs = [
        (w_mid_hbm, w_mid),
        (w_in_hbm, w_in),
        (b_in_hbm, b_in),
        (b_mid_hbm, b_mid),
        (b_out_hbm, b_out),
        (w_out_hbm, w_three),
    ]
    for copy in fetch(pairs, sems):
        copy.wait()
    f32, bf16 = jnp.float32, jnp.bfloat16
    row = lax.broadcasted_iota(jnp.int32, (8, 512), 0)
    bias = jnp.broadcast_to(0.5 * b_in[...], (8, 512))
    first = bias.astype(bf16).astype(f32)
    rest = bias - first
    padded = jnp.concatenate([0.5 * w_in[...].astype(f32), jnp.zeros((2, 512), f32)], axis=0)
    stacked = jnp.where(row == 6, first, jnp.where(row == 7, rest, padded))
    w_one[...] = stacked.T.astype(bf16)
    w_two[...] = (0.5 * w_mid[...].astype(f32)).T.astype(bf16)
    bias_mid[...] = jnp.broadcast_to(jnp.broadcast_to(0.5 * b_mid[...], (8, 512)).T[:, 0:1], (512, 128))
    wide[...] = jnp.zeros(wide.shape, f32)
    wide[:, 0:15] = jnp.broadcast_to(b_out[...], (8, 15))
    bias_out[...] = jnp.broadcast_to(wide[...].T[0:16, 0:1], (16, 128))


def step_two_kernel(
    slots_hbm, state_mid, state_rim, from_low, from_high, w_one, w_mid, b_mid, w_out, b_out, flow, closure,
    got, fields, near, level, feats, spread, place, slots, sem,
):
    low, high = walls()
    got[0] = from_low[...].astype(jnp.float32)
    got[1] = from_high[...].astype(jnp.float32)
    slots_copy = pltpu.make_async_copy(slots_hbm, slots, sem)
    slots_copy.start()

    def arrived(x, k, t, r):
        if t == 0 and r < 4:
            return got[x, pl.ds(field_row(k, r), 8), :]
        if t == 0:
            v = got[x, pl.ds(HALO_AT + 8 * (k // 2), 8), :]
            return roll(v, 4, 0) if k % 2 else v
        v = got[x, pl.ds(side_row(r), 8), :]
        return roll(v, -(4 * k + 2), 1)

    def kept(x, k, t, r):
        part = state_mid if r in (1, 2) else state_rim
        return part[x, k, t, pl.ds(state_row(r), 8), :]

    for x in range(2):
        for t in range(2):
            for r in range(5):
                for k in range(5):
                    put(near, (x, k, t), r, arrived(x, k, t, r))
                    put(near, (x, 5 + k, t), r, kept(x, 33 + k, t, r))
    numbers = list(range(19))
    for x in range(2):
        come = TOWARD[1 - x]
        go = TOWARD[x]
        sign = -0.5 if x == 0 else 0.5
        for r in range(5):
            come_f, go_f = [{}, {}], [{}, {}]
            for k, i in enumerate(come):
                back = go.index(opposite(i))
                pair = stream(
                    near, lambda t, k=k: (x, k, t), i, r, low, high,
                    lambda back=back: get(near, (x, 5 + back, 0), r),
                )
                come_f[0][i], come_f[1][i] = pair
            for k, i in enumerate(go):
                back = come.index(opposite(i))
                pair = stream(
                    near, lambda t, k=k: (x, 5 + k, t), i, r, low, high,
                    lambda back=back: get(near, (x, back, 0), r),
                )
                go_f[0][i], go_f[1][i] = pair
            for t in range(2):
                f = {i: kept(x, k, t, r) for k, i in enumerate(KNOWN[x])}
                f.update(come_f[t])
                rho_new, mom_new = moments(come_f[t], come)
                rho = kept(x, 14, t, r) + rho_new
                mom = [kept(x, 15 + j, t, r) + mom_new[j] for j in range(3)]
                inv = 1.0 / rho
                u = [m * inv for m in mom]
                relaxed = relax(f, rho, u, numbers)
                for i in numbers:
                    put(fields, (i, x, t), r, relaxed[i])
                for j in range(3):
                    put(fields, (19 + j, x, t), r, u[j])
                u0 = [kept(x, 24 + j, t, r) for j in range(3)]
                a0 = [kept(x, 27 + k, t, r) for k in range(6)]
                u0n = [arrived(x, 5 + j, t, r) for j in range(3)]
                a0n = [arrived(x, 8 + k, t, r) for k in range(6)]
                rate = jeffery(a0, [[sign * u0n[j], None, None] for j in range(3)])
                drift = (sign * u0[0])
                for k in range(6):
                    a1 = kept(x, 18 + k, t, r) + ORIENT_STEP * (rate[k] - drift * a0n[k])
                    put(fields, (22 + k, x, t), r, a1)
                rho_new, mom_new = moments(go_f[t], go)
                rho = arrived(x, 14, t, r) + rho_new
                inv = 1.0 / rho
                u = [(arrived(x, 15 + j, t, r) + mom_new[j]) * inv for j in range(3)]
                f = {i: arrived(x, 18 + k, t, r) for k, i in enumerate(come)}
                relaxed = relax(f, rho, u, come)
                for k, i in enumerate(come):
                    put(fields, (28 + k, x, t), r, relaxed[i])
                if t == 0 and r < 4:
                    rate = jeffery(a0n, [[-sign * u0[j], None, None] for j in range(3)])
                    drift = -sign * u0n[0]
                    for j in range(3):
                        level[x, j, pl.ds(8 * r, 8), :] = u[j]
                    for k in range(6):
                        a1 = arrived(x, 23 + k, t, r) + ORIENT_STEP * (rate[k] - drift * a0[k])
                        level[x, 3 + k, pl.ds(8 * r, 8), :] = a1

    slots_copy.wait()
    for s in range(17):
        place[s] = 64
    for b in range(64):
        s = slots[b // 32, 0, b % 32]
        place[jnp.where(s >= 0, s, 16)] = b
    feats[...] = jnp.ones(feats.shape, jnp.float32)
    for x in range(2):
        for r in range(4):
            f = {}
            for i in numbers:
                xs = x - VELOCITIES[i][0]
                if 0 <= xs <= 1:
                    at_of = lambda t, i=i, xs=xs: (i, xs, t)
                else:
                    k = TOWARD[1 - x].index(i)
                    at_of = lambda t, k=k: (28 + k, x, t)
                f[i], _ = stream(
                    fields, at_of, i, r, low, high, lambda i=i: get(fields, (opposite(i), x, 0), r), False
                )
            rho, mom = moments(f, numbers)
            inv = 1.0 / rho
            final = [rho] + [m * inv for m in mom]
            for k in range(4):
                spread[pl.ds(k * 64 + x * 32 + 8 * r, 8), :] = final[k]
            sign = -0.5 if x == 0 else 0.5
            by_x = lambda k, n: sign * (level[x, n, pl.ds(8 * r, 8), :] - get(fields, (k, 1 - x, 0), r))
            grad = [[None] * 3 for _ in range(3)]
            for j in range(3):
                place_u = lambda t, j=j: (19 + j, x, t)
                grad[j][0] = by_x(19 + j, j)
                grad[j][1] = central(fields, place_u, r, 1, low, high, False, False)[0]
                grad[j][2] = central(fields, place_u, r, 2, low, high, False, False)[0]
            u = [get(fields, (19 + j, x, 0), r) for j in range(3)]
            a = [get(fields, (22 + k, x, 0), r) for k in range(6)]
            rate = jeffery(a, grad)
            for k in range(6):
                place_a = lambda t, k=k: (22 + k, x, t)
                advect = (
                    u[0] * by_x(22 + k, 3 + k)
                    + u[1] * central(fields, place_a, r, 1, low, high, True, False)[0]
                    + u[2] * central(fields, place_a, r, 2, low, high, True, False)[0]
                )
                new = a[k] + ORIENT_STEP * (rate[k] - advect)
                feats[pl.ds((x * 32 + 8 * r) * 8 + k, 8, 8), :] = new
    for k in range(4):
        for x in range(2):
            flow[k, x] = spread[pl.ds(k * 64 + x * 32, 32), :].astype(jnp.bfloat16)

    spread[...] = jnp.zeros(spread.shape, jnp.float32)
    group = 8
    bias_mid = jnp.concatenate([b_mid[...]] * group, axis=1)
    for g in range(16 // group):
        at = [place[g * group + k] for k in range(group)]
        cells = [feats[pl.ds(pl.multiple_of(b * 8, 8), 8), :] for b in at]
        cells = jnp.concatenate(cells, axis=1).astype(jnp.bfloat16)
        v = jnp.dot(w_one[...], cells, preferred_element_type=jnp.float32)
        h = (v + v * jnp.tanh(v)).astype(jnp.bfloat16)
        v = jnp.dot(w_mid[...], h, preferred_element_type=jnp.float32) + bias_mid
        h = (v + v * jnp.tanh(v)).astype(jnp.bfloat16)
        v = jnp.dot(w_out[...], h, preferred_element_type=jnp.float32)
        for k in range(group):
            spread[pl.ds(pl.multiple_of(at[k] * 16, 16), 15), :] = v[:, 128 * k : 128 * k + 128] + b_out[0:15, :]
    for c in range(15):
        for x in range(2):
            closure[c, x] = spread[pl.ds(x * 512 + c, 32, 16), :].astype(jnp.bfloat16)


def local(populations, orientation, slot_table, w_in, b_in, w_mid, b_mid, w_out, b_out):
    f32, bf16 = jnp.float32, jnp.bfloat16
    shape = lambda *s, d=f32: jax.ShapeDtypeStruct(s, d)
    vmem = pl.BlockSpec(memory_space=pltpu.VMEM)
    params = pltpu.CompilerParams(vmem_limit_bytes=24 * MIB)

    def ring(axis, step, wrap):
        n = lax.axis_size(axis)
        return [(i, (i + step) % n) for i in range(n) if wrap or 0 <= i + step < n]

    hbm = pl.BlockSpec(memory_space=pltpu.HBM)
    slots = jnp.transpose(slot_table, (0, 2, 1))
    w_one, w_two, bias_mid, w_three, bias_out = pl.pallas_call(
        weights_kernel,
        out_shape=(
            shape(512, 8, d=bf16),
            shape(512, 512, d=bf16),
            shape(512, 128),
            shape(15, 512, d=bf16),
            shape(16, 128),
        ),
        in_specs=[hbm] * 6,
        out_specs=(vmem,) * 5,
        scratch_shapes=[
            pltpu.VMEM((6, 512), bf16),
            pltpu.VMEM((1, 512), f32),
            pltpu.VMEM((512, 512), bf16),
            pltpu.VMEM((1, 512), f32),
            pltpu.VMEM((1, 15), f32),
            pltpu.VMEM((8, 128), f32),
            pltpu.SemaphoreType.DMA((6,)),
        ],
        compiler_params=pltpu.CompilerParams(vmem_limit_bytes=LIMIT_WEIGHTS),
    )(w_in, b_in.reshape(1, 512), w_mid, b_mid.reshape(1, 512), w_out.T, b_out.reshape(1, 15))
    zlow, zhigh = pl.pallas_call(
        pack_z_kernel,
        out_shape=(shape(32, 128, d=bf16), shape(32, 128, d=bf16)),
        in_specs=[hbm] * 2,
        out_specs=(vmem,) * 2,
        scratch_shapes=[
            pltpu.VMEM((19, 2, 32, 128), f32),
            pltpu.VMEM((6, 2, 32, 128), f32),
            pltpu.SemaphoreType.DMA((5,)),
        ],
        compiler_params=pltpu.CompilerParams(vmem_limit_bytes=LIMIT_PACK),
        cost_estimate=COST_PACK,
    )(populations, orientation)
    own, low_raw, high_raw = pl.pallas_call(
        own_kernel,
        out_shape=(shape(28, 2, 32, 128), shape(112, 128), shape(112, 128)),
        in_specs=[vmem] * 3,
        out_specs=(vmem,) * 3,
        compiler_params=params,
    )(populations, orientation, zlow)
    from_minus = lax.ppermute(zhigh, "gz", ring("gz", 1, False))
    from_plus = lax.ppermute(zlow, "gz", ring("gz", -1, False))
    sides, low_rows, high_rows = pl.pallas_call(
        pack_y_kernel,
        out_shape=(shape(2, 32, 128), shape(112, 128, d=bf16), shape(112, 128, d=bf16)),
        in_specs=[vmem] * 4,
        out_specs=(vmem,) * 3,
        scratch_shapes=[pltpu.VMEM((112, 128), f32), pltpu.VMEM((112, 128), f32)],
        compiler_params=params,
    )(from_minus, from_plus, low_raw, high_raw)
    fields_shape = shape(28, 2, 2, 64, 128)
    fields, state_mid, middle = pl.pallas_call(
        middle_kernel,
        out_shape=(fields_shape, shape(2, STATE, 2, 16, 128), shape(2, MID_ROWS, 128, d=bf16)),
        in_specs=[vmem] * 2,
        out_specs=(vmem,) * 3,
        scratch_shapes=[pltpu.VMEM((2, MID_ROWS, 128), f32)],
        compiler_params=params,
    )(own, sides)
    from_yminus = lax.ppermute(high_rows, "gy", ring("gy", 1, True))
    from_yplus = lax.ppermute(low_rows, "gy", ring("gy", -1, True))
    fields, state_rim, msg_low, msg_high = pl.pallas_call(
        step_one_kernel,
        out_shape=(
            fields_shape,
            shape(2, STATE, 2, 24, 128),
            shape(MSG_ROWS, 128, d=bf16),
            shape(MSG_ROWS, 128, d=bf16),
        ),
        in_specs=[vmem] * 4,
        out_specs=(vmem,) * 4,
        scratch_shapes=[
            pltpu.VMEM((52, 8, 128), f32),
            pltpu.VMEM((2, MSG_ROWS, 128), f32),
            pltpu.VMEM((2, 112, 128), f32),
        ],
        input_output_aliases={0: 0},
        compiler_params=params,
    )(fields, middle, from_yminus, from_yplus)
    from_low = lax.ppermute(msg_high, "gx", ring("gx", 1, True))
    from_high = lax.ppermute(msg_low, "gx", ring("gx", -1, True))
    return pl.pallas_call(
        step_two_kernel,
        out_shape=(shape(4, 2, 32, 128, d=bf16), shape(15, 2, 32, 128, d=bf16)),
        in_specs=[hbm] + [vmem] * 9,
        out_specs=(vmem,) * 2,
        scratch_shapes=[
            pltpu.VMEM((2, MSG_ROWS, 128), f32),
            pltpu.VMEM((33, 2, 2, 64, 128), f32),
            pltpu.VMEM((2, 10, 2, 64, 128), f32),
            pltpu.VMEM((2, 9, 32, 128), f32),
            pltpu.VMEM((65 * 8, 128), f32),
            pltpu.VMEM((65 * 16, 128), f32),
            pltpu.SMEM((17,), jnp.int32),
            pltpu.SMEM((2, 1, 32), jnp.int32),
            pltpu.SemaphoreType.DMA,
        ],
        compiler_params=params,
    )(slots, state_mid, state_rim, from_low, from_high, w_one, w_two, bias_mid, w_three, bias_out)


def solution(mesh):
    grid = P(None, "gx", "gy", "gz")
    in_specs = (grid, grid, P("gx", "gy", "gz"), P(), P(), P(), P(), P(), P())
    return jax.shard_map(local, mesh=mesh, in_specs=in_specs, out_specs=(grid, grid), check_vma=False)
```

```python
import functools

import jax
import jax.numpy as jnp
from jax import lax
from jax.experimental import pallas as pl
from jax.experimental.pallas import tpu as pltpu
from jax.sharding import PartitionSpec as P


VELOCITIES = [
    (0, 0, 0),
    (1, 0, 0),
    (-1, 0, 0),
    (0, 1, 0),
    (0, -1, 0),
    (0, 0, 1),
    (0, 0, -1),
    (1, 1, 0),
    (-1, -1, 0),
    (1, -1, 0),
    (-1, 1, 0),
    (1, 0, 1),
    (-1, 0, -1),
    (1, 0, -1),
    (-1, 0, 1),
    (0, 1, 1),
    (0, -1, -1),
    (0, 1, -1),
    (0, -1, 1),
]
WEIGHTS = [1.0 / 3.0] + [1.0 / 18.0] * 6 + [1.0 / 36.0] * 12
OMEGA = 1.0 / 0.8
SHAPE_FACTOR = 0.95
ORIENT_STEP = 4.0
PAIRS = [(0, 0), (1, 1), (2, 2), (0, 1), (0, 2), (1, 2)]
ENTRY = [[0, 3, 4], [3, 1, 5], [4, 5, 2]]
TOWARD = {
    0: [i for i in range(19) if VELOCITIES[i][0] == -1],
    1: [i for i in range(19) if VELOCITIES[i][0] == 1],
}
KNOWN = {0: [i for i in range(19) if VELOCITIES[i][0] != 1], 1: [i for i in range(19) if VELOCITIES[i][0] != -1]}
MSG_WIDE = 23
MSG_ROWS = 1072
MID_ROWS = 480
SIDE_MID = 464
RIM_AT = 480
HALO_AT = 944
SIDE_RIM = 1040
CORNER_AT = 1056
MIB = 1024 * 1024
LIMIT_PACK = 5375 * MIB // 100
COST_PACK = pl.CostEstimate(flops=10**10, bytes_accessed=10**7, transcendentals=0)
LIMIT_WEIGHTS = 4900 * MIB // 100
STATE = 38


def opposite(i):
    return 0 if i == 0 else (i + 1 if i % 2 == 1 else i - 1)


def lanes_of():
    return lax.broadcasted_iota(jnp.int32, (8, 128), 1)


def rows_of():
    return lax.broadcasted_iota(jnp.int32, (8, 128), 0)


def roll(v, shift, axis):
    shift = shift % v.shape[axis]
    return v if shift == 0 else pltpu.roll(v, shift, axis)


def add_all(terms):
    while len(terms) > 1:
        terms = [
            terms[k] + terms[k + 1] if k + 1 < len(terms) else terms[k] for k in range(0, len(terms), 2)
        ]
    return terms[0]


def moments(f, numbers):
    rho = add_all([f[i] for i in numbers])
    mom = []
    for ax in range(3):
        pos = [f[i] for i in numbers if VELOCITIES[i][ax] > 0]
        neg = [f[i] for i in numbers if VELOCITIES[i][ax] < 0]
        total = add_all(pos) if pos else None
        if neg:
            total = add_all(neg) * -1.0 if total is None else total - add_all(neg)
        mom.append(total)
    return rho, mom


def relax(f, rho, u, numbers):
    usq = 1.0 - 1.5 * (u[0] * u[0] + u[1] * u[1] + u[2] * u[2])
    scaled = {w: (w * OMEGA) * rho for w in sorted(set(WEIGHTS[i] for i in numbers))}
    out = {}
    for i in numbers:
        proj = None
        for ax in range(3):
            c = VELOCITIES[i][ax]
            if c != 0:
                if proj is None:
                    proj = u[ax] if c > 0 else -u[ax]
                else:
                    proj = proj + u[ax] if c > 0 else proj - u[ax]
        poly = usq if proj is None else usq + proj * (3.0 + 4.5 * proj)
        out[i] = f[i] * (1.0 - OMEGA) + scaled[WEIGHTS[i]] * poly
    return out


def plus(a, b):
    if a is None:
        return b
    if b is None:
        return a
    return a + b


def minus(a, b):
    if b is None:
        return a
    if a is None:
        return -b
    return a - b


def times(a, b):
    return None if a is None or b is None else a * b


def jeffery(a, g):
    half = [[None if g[j][k] is None else 0.5 * g[j][k] for k in range(3)] for j in range(3)]
    d = [[plus(half[j][k], half[k][j]) if j <= k else None for k in range(3)] for j in range(3)]
    w = [[minus(half[j][k], half[k][j]) if j < k else None for k in range(3)] for j in range(3)]
    full = lambda j, k: a[ENTRY[j][k]]
    strain = lambda j, k: d[min(j, k)][max(j, k)]

    def spin(j, k):
        if j == k:
            return None
        if j < k:
            return w[j][k]
        return None if w[k][j] is None else -w[k][j]

    contraction = None
    for j in range(3):
        contraction = plus(contraction, times(full(j, j), strain(j, j)))
    for j, k in ((0, 1), (0, 2), (1, 2)):
        cross = times(full(j, k), strain(j, k))
        contraction = plus(contraction, None if cross is None else 2.0 * cross)
    twice = 2.0 * contraction
    mix = [[plus(spin(j, k), times(strain(j, k), SHAPE_FACTOR)) for k in range(3)] for j in range(3)]
    z = [[None] * 3 for _ in range(3)]
    for j in range(3):
        for k in range(3):
            for m in range(3):
                z[j][k] = plus(z[j][k], times(full(j, m), mix[m][k]))
    scaled = SHAPE_FACTOR * twice
    return [plus(z[j][k], z[k][j]) - scaled * full(j, k) for j, k in PAIRS]


def field_row(k, r):
    return 16 * k + 8 * (r - 1) if r in (1, 2) else RIM_AT + 16 * k + 8 * (r // 3)


def side_row(r):
    return SIDE_MID + 8 * (r - 1) if r in (1, 2) else (CORNER_AT if r == 4 else SIDE_RIM + 8 * (r // 3))


def state_row(r):
    return {1: 0, 2: 8, 0: 0, 3: 8, 4: 16}[r]


def put(ref, at, r, v):
    if r < 4:
        ref[at + (pl.ds(16 + 8 * r, 8), slice(None))] = v
    else:
        ref[at + (pl.ds(8, 8), slice(None))] = v
        ref[at + (pl.ds(48, 8), slice(None))] = v


def get(ref, at, r, dy=0):
    if r < 4:
        return ref[at + (pl.ds(16 + 8 * r + dy, 8), slice(None))]
    if dy == 0:
        return ref[at + (pl.ds(48, 8), slice(None))]
    return jnp.where(
        rows_of() < 4,
        ref[at + (pl.ds(48 + dy, 8), slice(None))],
        ref[at + (pl.ds(8 + dy, 8), slice(None))],
    )


def pull_z(own, side, dz, want_side=True):
    if dz == 0:
        return own, side
    lane = lanes_of()
    own_r, side_r = roll(own, dz, 1), roll(side, dz, 1)
    edge = lane == (0 if dz > 0 else 127)
    return jnp.where(edge, side_r, own_r), jnp.where(edge, own_r, side_r) if want_side else None


def walls():
    layer = lax.axis_index("gz")
    last = lax.axis_size("gz") - 1
    lane = lanes_of()
    low = lane == jnp.where(layer == 0, 0, -1)
    high = lane == jnp.where(layer == last, 127, -1)
    return low, high


def wall_of(i, low, high):
    dz = VELOCITIES[i][2]
    return None if dz == 0 else (low if dz > 0 else high)


def stream(ref, at_of, i, r, low, high, reflected, want_side=True):
    _, cy, cz = VELOCITIES[i]
    own = get(ref, at_of(0), r, -cy)
    side = get(ref, at_of(1), r, -cy) if (want_side or cz != 0) else None
    if cz == 0:
        return own, side
    own, side = pull_z(own, side, cz, want_side)
    return jnp.where(wall_of(i, low, high), reflected(), own), side


def central(ref, at_of, r, axis, low, high, outside, want_side=True):
    if axis == 1:
        out = []
        for t in (0, 1) if want_side else (0,):
            out.append(0.5 * (get(ref, at_of(t), r, 1) - get(ref, at_of(t), r, -1)))
        return out
    own, side = get(ref, at_of(0), r), get(ref, at_of(1), r)
    behind, behind_side = pull_z(own, side, 1, want_side)
    ahead, ahead_side = pull_z(own, side, -1, want_side)
    past = own if outside else jnp.zeros_like(own)
    diff = 0.5 * (jnp.where(high, past, ahead) - jnp.where(low, past, behind))
    return [diff, 0.5 * (ahead_side - behind_side)] if want_side else [diff]


def fetch(pairs, sems):
    copies = [pltpu.make_async_copy(src, dst, sems.at[k]) for k, (src, dst) in enumerate(pairs)]
    for copy in copies:
        copy.start()
    return copies


PIECES = [(0, 5), (5, 10), (10, 15), (15, 19)]


def pack_z_kernel(pop_hbm, ori_hbm, zlow, zhigh, pop, ori, sems):
    pairs = [(pop_hbm.at[pl.ds(a, b - a)], pop.at[pl.ds(a, b - a)]) for a, b in PIECES]
    copies = fetch(pairs + [(ori_hbm, ori)], sems)
    starts = [a for a, _ in PIECES] + [19]
    lane = lax.broadcasted_iota(jnp.int32, (32, 128), 1)
    low = jnp.zeros((32, 128), jnp.float32)
    high = jnp.zeros((32, 128), jnp.float32)
    for f in range(25):
        if f in starts:
            copies[starts.index(f)].wait()
        src = pop if f < 19 else ori
        k = f if f < 19 else f - 19
        for x in range(2):
            s = 2 * f + x
            at = 2 * s
            v = roll(src[k, x], at + 2, 1)
            high = jnp.where((lane >= at) & (lane < at + 2), v, high)
            low = jnp.where((lane >= at + 2) & (lane < at + 4), v, low)
    zlow[...] = low.astype(jnp.bfloat16)
    zhigh[...] = high.astype(jnp.bfloat16)


def unpack_z(from_minus, from_plus, s):
    shift = -(2 * s + 2)
    return jnp.where(lanes_of() < 64, roll(from_plus, shift, 1), roll(from_minus, shift, 1))


def pack_y_kernel(from_minus, from_plus, low_in, high_in, sides, low_rows, high_rows, low, high):
    low[...] = low_in[...]
    high[...] = high_in[...]
    for t, part in enumerate((from_minus, from_plus)):
        sides[t] = part[...].astype(jnp.float32)
        low[pl.ds(100 + 2 * t, 2), :] = sides[t, 0:2, :]
        high[pl.ds(100 + 2 * t, 2), :] = sides[t, 30:32, :]
    low_rows[...] = low[...].astype(jnp.bfloat16)
    high_rows[...] = high[...].astype(jnp.bfloat16)


def own_kernel(pop, ori, after, own, low_rows, high_rows):
    del after
    for f in range(25):
        src = pop if f < 19 else ori
        k = f if f < 19 else f - 19
        for x in range(2):
            rows = pl.ds(2 * (2 * f + x), 2)
            low_rows[rows, :] = src[k, x, 0:2, :]
            high_rows[rows, :] = src[k, x, 30:32, :]
    low_rows[100:112, :] = jnp.zeros((12, 128), jnp.float32)
    high_rows[100:112, :] = jnp.zeros((12, 128), jnp.float32)
    numbers = list(range(19))
    for x in range(2):
        for r in range(4):
            rows = pl.ds(8 * r, 8)
            f = [pop[i, x, rows, :] for i in numbers]
            rho, mom = moments(f, numbers)
            inv = 1.0 / rho
            u = [m * inv for m in mom]
            relaxed = relax(f, rho, u, numbers)
            for i in numbers:
                own[i, x, rows, :] = relaxed[i]
            for j in range(3):
                own[19 + j, x, rows, :] = u[j]
            for k in range(6):
                own[22 + k, x, rows, :] = ori[k, x, rows, :]


def collide_group(raw, fields, x, t, r):
    numbers = list(range(19))
    f = [raw(i) for i in numbers]
    rho, mom = moments(f, numbers)
    inv = 1.0 / rho
    u = [m * inv for m in mom]
    relaxed = relax(f, rho, u, numbers)
    for i in numbers:
        put(fields, (i, x, t), r, relaxed[i])
    for j in range(3):
        put(fields, (19 + j, x, t), r, u[j])
    for k in range(6):
        put(fields, (22 + k, x, t), r, raw(19 + k))


def advance_group(fields, state, out, x, r, low, high):
    lane, row = lanes_of(), rows_of()
    place = lambda f, xs=x: (lambda t: (f, xs, t))
    known = [{}, {}]
    for i in KNOWN[x]:
        xs = x - VELOCITIES[i][0]
        pair = stream(fields, place(i, xs), i, r, low, high, lambda i=i: get(fields, (opposite(i), x, 0), r))
        known[0][i], known[1][i] = pair
    grad = [[[None] * 3 for _ in range(3)] for _ in range(2)]
    sign = 0.5 if x == 0 else -0.5
    for j in range(3):
        by_y = central(fields, place(19 + j), r, 1, low, high, False)
        by_z = central(fields, place(19 + j), r, 2, low, high, False)
        for t in range(2):
            grad[t][j][0] = sign * get(fields, (19 + j, 1 - x, t), r)
            grad[t][j][1] = by_y[t]
            grad[t][j][2] = by_z[t]
    u = [[get(fields, (19 + j, x, t), r) for j in range(3)] for t in range(2)]
    a = [[get(fields, (22 + k, x, t), r) for k in range(6)] for t in range(2)]
    advect = [[], []]
    for k in range(6):
        by_y = central(fields, place(22 + k), r, 1, low, high, True)
        by_z = central(fields, place(22 + k), r, 2, low, high, True)
        for t in range(2):
            by_x = sign * get(fields, (22 + k, 1 - x, t), r)
            advect[t].append(u[t][0] * by_x + u[t][1] * by_y[t] + u[t][2] * by_z[t])
    side_pack = jnp.zeros((8, 128), jnp.float32)
    for t in range(2):
        rate = jeffery(a[t], grad[t])
        part = [a[t][k] + ORIENT_STEP * (rate[k] - advect[t][k]) for k in range(6)]
        rho, mom = moments(known[t], KNOWN[x])
        outward = [get(fields, (i, x, t), r) for i in TOWARD[x]]
        keep = [known[t][i] for i in KNOWN[x]] + [rho] + mom + part + u[t] + a[t] + outward
        for k in range(STATE):
            state[x, k, t, pl.ds(state_row(r), 8), :] = keep[k]
        wide = outward + u[t] + a[t] + [rho] + mom + [known[t][i] for i in TOWARD[x]]
        if t == 1:
            for k in range(MSG_WIDE):
                at = 4 * k
                side_pack = jnp.where((lane >= at) & (lane < at + 4), roll(wide[k], at + 2, 1), side_pack)
        elif r < 4:
            for k, v in enumerate(wide + part):
                out[x, pl.ds(field_row(k, r), 8), :] = v
        else:
            inner = (row >= 2) & (row < 6)
            for k in range(0, MSG_WIDE, 2):
                v = wide[k]
                if k + 1 < MSG_WIDE:
                    v = jnp.where(inner, roll(wide[k + 1], 4, 0), v)
                out[x, pl.ds(HALO_AT + 4 * k, 8), :] = v
    out[x, pl.ds(side_row(r), 8), :] = side_pack


def middle_kernel(own, sides, fields, state, message, out):
    low, high = walls()
    for x in range(2):
        for r in range(4):
            rows = pl.ds(8 * r, 8)
            for k in range(28):
                put(fields, (k, x, 0), r, own[k, x, rows, :])

            def raw(f):
                return unpack_z(sides[0, rows, :], sides[1, rows, :], 2 * f + x)

            collide_group(raw, fields, x, 1, r)
    for x in range(2):
        for r in (1, 2):
            advance_group(fields, state, out, x, r, low, high)
    message[...] = out[...].astype(jnp.bfloat16)


def step_one_kernel(before, middle, from_yminus, from_yplus, fields, state, msg_low, msg_high, halo, out, got):
    del before
    low, high = walls()
    got[0] = from_yminus[...].astype(jnp.float32)
    got[1] = from_yplus[...].astype(jnp.float32)
    for s in range(52):
        halo[s, 0:2, :] = got[1, pl.ds(2 * s, 2), :]
        halo[s, 6:8, :] = got[0, pl.ds(2 * s, 2), :]
    for x in range(2):
        for t in range(2):

            def raw(f):
                s = 2 * f + x
                return halo[s] if t == 0 else unpack_z(halo[50], halo[51], s)

            collide_group(raw, fields, x, t, 4)
    for x in range(2):
        for r in (0, 3, 4):
            advance_group(fields, state, out, x, r, low, high)
        out[x, pl.ds(CORNER_AT + 8, 8), :] = jnp.zeros((8, 128), jnp.float32)
    for x, msg in enumerate((msg_low, msg_high)):
        msg[0:MID_ROWS, :] = middle[x]
        msg[MID_ROWS:MSG_ROWS, :] = out[x, MID_ROWS:MSG_ROWS, :].astype(jnp.bfloat16)


def weights_kernel(
    w_in_hbm, b_in_hbm, w_mid_hbm, b_mid_hbm, w_out_hbm, b_out_hbm, w_one, w_two, bias_mid, w_three, bias_out,
    w_in, b_in, w_mid, b_mid, b_out, wide, sems,
):
    pairs = [
        (w_mid_hbm, w_mid),
        (w_in_hbm, w_in),
        (b_in_hbm, b_in),
        (b_mid_hbm, b_mid),
        (b_out_hbm, b_out),
        (w_out_hbm, w_three),
    ]
    for copy in fetch(pairs, sems):
        copy.wait()
    f32, bf16 = jnp.float32, jnp.bfloat16
    row = lax.broadcasted_iota(jnp.int32, (8, 512), 0)
    bias = jnp.broadcast_to(0.5 * b_in[...], (8, 512))
    first = bias.astype(bf16).astype(f32)
    rest = bias - first
    padded = jnp.concatenate([0.5 * w_in[...].astype(f32), jnp.zeros((2, 512), f32)], axis=0)
    stacked = jnp.where(row == 6, first, jnp.where(row == 7, rest, padded))
    w_one[...] = stacked.T.astype(bf16)
    w_two[...] = (0.5 * w_mid[...].astype(f32)).T.astype(bf16)
    bias_mid[...] = jnp.broadcast_to(jnp.broadcast_to(0.5 * b_mid[...], (8, 512)).T[:, 0:1], (512, 128))
    wide[...] = jnp.zeros(wide.shape, f32)
    wide[:, 0:15] = jnp.broadcast_to(b_out[...], (8, 15))
    bias_out[...] = jnp.broadcast_to(wide[...].T[0:16, 0:1], (16, 128))


def step_two_kernel(
    slots_hbm, state_mid, state_rim, from_high, from_low, w_one, w_mid, b_mid, w_out, b_out, flow, closure,
    got, fields, near, level, feats, spread, place, slots, sem,
):
    low, high = walls()
    got[0] = from_low[...].astype(jnp.float32)
    got[1] = from_high[...].astype(jnp.float32)
    slots_copy = pltpu.make_async_copy(slots_hbm, slots, sem)
    slots_copy.start()

    def arrived(x, k, t, r):
        if t == 0 and r < 4:
            return got[x, pl.ds(field_row(k, r), 8), :]
        if t == 0:
            v = got[x, pl.ds(HALO_AT + 8 * (k // 2), 8), :]
            return roll(v, 4, 0) if k % 2 else v
        v = got[x, pl.ds(side_row(r), 8), :]
        return roll(v, -(4 * k + 2), 1)

    def kept(x, k, t, r):
        part = state_mid if r in (1, 2) else state_rim
        return part[x, k, t, pl.ds(state_row(r), 8), :]

    for x in range(2):
        for t in range(2):
            for r in range(5):
                for k in range(5):
                    put(near, (x, k, t), r, arrived(x, k, t, r))
                    put(near, (x, 5 + k, t), r, kept(x, 33 + k, t, r))
    numbers = list(range(19))
    for x in range(2):
        come = TOWARD[1 - x]
        go = TOWARD[x]
        sign = -0.5 if x == 0 else 0.5
        for r in range(5):
            come_f, go_f = [{}, {}], [{}, {}]
            for k, i in enumerate(come):
                back = go.index(opposite(i))
                pair = stream(
                    near, lambda t, k=k: (x, k, t), i, r, low, high,
                    lambda back=back: get(near, (x, 5 + back, 0), r),
                )
                come_f[0][i], come_f[1][i] = pair
            for k, i in enumerate(go):
                back = come.index(opposite(i))
                pair = stream(
                    near, lambda t, k=k: (x, 5 + k, t), i, r, low, high,
                    lambda back=back: get(near, (x, back, 0), r),
                )
                go_f[0][i], go_f[1][i] = pair
            for t in range(2):
                f = {i: kept(x, k, t, r) for k, i in enumerate(KNOWN[x])}
                f.update(come_f[t])
                rho_new, mom_new = moments(come_f[t], come)
                rho = kept(x, 14, t, r) + rho_new
                mom = [kept(x, 15 + j, t, r) + mom_new[j] for j in range(3)]
                inv = 1.0 / rho
                u = [m * inv for m in mom]
                relaxed = relax(f, rho, u, numbers)
                for i in numbers:
                    put(fields, (i, x, t), r, relaxed[i])
                for j in range(3):
                    put(fields, (19 + j, x, t), r, u[j])
                u0 = [kept(x, 24 + j, t, r) for j in range(3)]
                a0 = [kept(x, 27 + k, t, r) for k in range(6)]
                u0n = [arrived(x, 5 + j, t, r) for j in range(3)]
                a0n = [arrived(x, 8 + k, t, r) for k in range(6)]
                rate = jeffery(a0, [[sign * u0n[j], None, None] for j in range(3)])
                drift = (sign * u0[0])
                for k in range(6):
                    a1 = kept(x, 18 + k, t, r) + ORIENT_STEP * (rate[k] - drift * a0n[k])
                    put(fields, (22 + k, x, t), r, a1)
                rho_new, mom_new = moments(go_f[t], go)
                rho = arrived(x, 14, t, r) + rho_new
                inv = 1.0 / rho
                u = [(arrived(x, 15 + j, t, r) + mom_new[j]) * inv for j in range(3)]
                f = {i: arrived(x, 18 + k, t, r) for k, i in enumerate(come)}
                relaxed = relax(f, rho, u, come)
                for k, i in enumerate(come):
                    put(fields, (28 + k, x, t), r, relaxed[i])
                if t == 0 and r < 4:
                    rate = jeffery(a0n, [[-sign * u0[j], None, None] for j in range(3)])
                    drift = -sign * u0n[0]
                    for j in range(3):
                        level[x, j, pl.ds(8 * r, 8), :] = u[j]
                    for k in range(6):
                        a1 = arrived(x, 23 + k, t, r) + ORIENT_STEP * (rate[k] - drift * a0[k])
                        level[x, 3 + k, pl.ds(8 * r, 8), :] = a1

    slots_copy.wait()
    for s in range(17):
        place[s] = 64
    for b in range(64):
        s = slots[b // 32, 0, b % 32]
        place[jnp.where(s >= 0, s, 16)] = b
    feats[...] = jnp.ones(feats.shape, jnp.float32)
    for x in range(2):
        for r in range(4):
            f = {}
            for i in numbers:
                xs = x - VELOCITIES[i][0]
                if 0 <= xs <= 1:
                    at_of = lambda t, i=i, xs=xs: (i, xs, t)
                else:
                    k = TOWARD[1 - x].index(i)
                    at_of = lambda t, k=k: (28 + k, x, t)
                f[i], _ = stream(
                    fields, at_of, i, r, low, high, lambda i=i: get(fields, (opposite(i), x, 0), r), False
                )
            rho, mom = moments(f, numbers)
            inv = 1.0 / rho
            final = [rho] + [m * inv for m in mom]
            for k in range(4):
                spread[pl.ds(k * 64 + x * 32 + 8 * r, 8), :] = final[k]
            sign = -0.5 if x == 0 else 0.5
            by_x = lambda k, n: sign * (level[x, n, pl.ds(8 * r, 8), :] - get(fields, (k, 1 - x, 0), r))
            grad = [[None] * 3 for _ in range(3)]
            for j in range(3):
                place_u = lambda t, j=j: (19 + j, x, t)
                grad[j][0] = by_x(19 + j, j)
                grad[j][1] = central(fields, place_u, r, 1, low, high, False, False)[0]
                grad[j][2] = central(fields, place_u, r, 2, low, high, False, False)[0]
            u = [get(fields, (19 + j, x, 0), r) for j in range(3)]
            a = [get(fields, (22 + k, x, 0), r) for k in range(6)]
            rate = jeffery(a, grad)
            for k in range(6):
                place_a = lambda t, k=k: (22 + k, x, t)
                advect = (
                    u[0] * by_x(22 + k, 3 + k)
                    + u[1] * central(fields, place_a, r, 1, low, high, True, False)[0]
                    + u[2] * central(fields, place_a, r, 2, low, high, True, False)[0]
                )
                new = a[k] + ORIENT_STEP * (rate[k] - advect)
                feats[pl.ds((x * 32 + 8 * r) * 8 + k, 8, 8), :] = new
    for k in range(4):
        for x in range(2):
            flow[k, x] = spread[pl.ds(k * 64 + x * 32, 32), :].astype(jnp.bfloat16)

    spread[...] = jnp.zeros(spread.shape, jnp.float32)
    group = 8
    bias_mid = jnp.concatenate([b_mid[...]] * group, axis=1)
    for g in range(16 // group):
        at = [place[g * group + k] for k in range(group)]
        cells = [feats[pl.ds(pl.multiple_of(b * 8, 8), 8), :] for b in at]
        cells = jnp.concatenate(cells, axis=1).astype(jnp.bfloat16)
        v = jnp.dot(w_one[...], cells, preferred_element_type=jnp.float32)
        h = (v + v * jnp.tanh(v)).astype(jnp.bfloat16)
        v = jnp.dot(w_mid[...], h, preferred_element_type=jnp.float32) + bias_mid
        h = (v + v * jnp.tanh(v)).astype(jnp.bfloat16)
        v = jnp.dot(w_out[...], h, preferred_element_type=jnp.float32)
        for k in range(group):
            spread[pl.ds(pl.multiple_of(at[k] * 16, 16), 15), :] = v[:, 128 * k : 128 * k + 128] + b_out[0:15, :]
    for c in range(15):
        for x in range(2):
            closure[c, x] = spread[pl.ds(x * 512 + c, 32, 16), :].astype(jnp.bfloat16)


def local(populations, orientation, slot_table, w_in, b_in, w_mid, b_mid, w_out, b_out):
    f32, bf16 = jnp.float32, jnp.bfloat16
    shape = lambda *s, d=f32: jax.ShapeDtypeStruct(s, d)
    vmem = pl.BlockSpec(memory_space=pltpu.VMEM)
    params = pltpu.CompilerParams(vmem_limit_bytes=24 * MIB)

    def ring(axis, step, wrap):
        n = lax.axis_size(axis)
        return [(i, (i + step) % n) for i in range(n) if wrap or 0 <= i + step < n]

    hbm = pl.BlockSpec(memory_space=pltpu.HBM)
    slots = jnp.transpose(slot_table, (0, 2, 1))
    w_one, w_two, bias_mid, w_three, bias_out = pl.pallas_call(
        weights_kernel,
        out_shape=(
            shape(512, 8, d=bf16),
            shape(512, 512, d=bf16),
            shape(512, 128),
            shape(15, 512, d=bf16),
            shape(16, 128),
        ),
        in_specs=[hbm] * 6,
        out_specs=(vmem,) * 5,
        scratch_shapes=[
            pltpu.VMEM((6, 512), bf16),
            pltpu.VMEM((1, 512), f32),
            pltpu.VMEM((512, 512), bf16),
            pltpu.VMEM((1, 512), f32),
            pltpu.VMEM((1, 15), f32),
            pltpu.VMEM((8, 128), f32),
            pltpu.SemaphoreType.DMA((6,)),
        ],
        compiler_params=pltpu.CompilerParams(vmem_limit_bytes=LIMIT_WEIGHTS),
    )(w_in, b_in.reshape(1, 512), w_mid, b_mid.reshape(1, 512), w_out.T, b_out.reshape(1, 15))
    zlow, zhigh = pl.pallas_call(
        pack_z_kernel,
        out_shape=(shape(32, 128, d=bf16), shape(32, 128, d=bf16)),
        in_specs=[hbm] * 2,
        out_specs=(vmem,) * 2,
        scratch_shapes=[
            pltpu.VMEM((19, 2, 32, 128), f32),
            pltpu.VMEM((6, 2, 32, 128), f32),
            pltpu.SemaphoreType.DMA((5,)),
        ],
        compiler_params=pltpu.CompilerParams(vmem_limit_bytes=LIMIT_PACK),
        cost_estimate=COST_PACK,
    )(populations, orientation)
    own, low_raw, high_raw = pl.pallas_call(
        own_kernel,
        out_shape=(shape(28, 2, 32, 128), shape(112, 128), shape(112, 128)),
        in_specs=[vmem] * 3,
        out_specs=(vmem,) * 3,
        compiler_params=params,
    )(populations, orientation, zlow)
    from_minus = lax.ppermute(zhigh, "gz", ring("gz", 1, False))
    from_plus = lax.ppermute(zlow, "gz", ring("gz", -1, False))
    sides, low_rows, high_rows = pl.pallas_call(
        pack_y_kernel,
        out_shape=(shape(2, 32, 128), shape(112, 128, d=bf16), shape(112, 128, d=bf16)),
        in_specs=[vmem] * 4,
        out_specs=(vmem,) * 3,
        scratch_shapes=[pltpu.VMEM((112, 128), f32), pltpu.VMEM((112, 128), f32)],
        compiler_params=params,
    )(from_minus, from_plus, low_raw, high_raw)
    fields_shape = shape(28, 2, 2, 64, 128)
    fields, state_mid, middle = pl.pallas_call(
        middle_kernel,
        out_shape=(fields_shape, shape(2, STATE, 2, 16, 128), shape(2, MID_ROWS, 128, d=bf16)),
        in_specs=[vmem] * 2,
        out_specs=(vmem,) * 3,
        scratch_shapes=[pltpu.VMEM((2, MID_ROWS, 128), f32)],
        compiler_params=params,
    )(own, sides)
    from_yminus = lax.ppermute(high_rows, "gy", ring("gy", 1, True))
    from_yplus = lax.ppermute(low_rows, "gy", ring("gy", -1, True))
    fields, state_rim, msg_low, msg_high = pl.pallas_call(
        step_one_kernel,
        out_shape=(
            fields_shape,
            shape(2, STATE, 2, 24, 128),
            shape(MSG_ROWS, 128, d=bf16),
            shape(MSG_ROWS, 128, d=bf16),
        ),
        in_specs=[vmem] * 4,
        out_specs=(vmem,) * 4,
        scratch_shapes=[
            pltpu.VMEM((52, 8, 128), f32),
            pltpu.VMEM((2, MSG_ROWS, 128), f32),
            pltpu.VMEM((2, 112, 128), f32),
        ],
        input_output_aliases={0: 0},
        compiler_params=params,
    )(fields, middle, from_yminus, from_yplus)
    from_low = lax.ppermute(msg_high, "gx", ring("gx", 1, True))
    from_high = lax.ppermute(msg_low, "gx", ring("gx", -1, True))
    return pl.pallas_call(
        step_two_kernel,
        out_shape=(shape(4, 2, 32, 128, d=bf16), shape(15, 2, 32, 128, d=bf16)),
        in_specs=[hbm] + [vmem] * 9,
        out_specs=(vmem,) * 2,
        scratch_shapes=[
            pltpu.VMEM((2, MSG_ROWS, 128), f32),
            pltpu.VMEM((33, 2, 2, 64, 128), f32),
            pltpu.VMEM((2, 10, 2, 64, 128), f32),
            pltpu.VMEM((2, 9, 32, 128), f32),
            pltpu.VMEM((65 * 8, 128), f32),
            pltpu.VMEM((65 * 16, 128), f32),
            pltpu.SMEM((17,), jnp.int32),
            pltpu.SMEM((2, 1, 32), jnp.int32),
            pltpu.SemaphoreType.DMA,
        ],
        compiler_params=params,
    )(slots, state_mid, state_rim, from_high, from_low, w_one, w_two, bias_mid, w_three, bias_out)


def solution(mesh):
    grid = P(None, "gx", "gy", "gz")
    in_specs = (grid, grid, P("gx", "gy", "gz"), P(), P(), P(), P(), P(), P())
    return jax.shard_map(local, mesh=mesh, in_specs=in_specs, out_specs=(grid, grid), check_vma=False)
```
